32 devices in a mesh: dp: 4 (over y, core), wide: 4 (over z), narrow: 2 (over x).
Axes of the slice: x: 2, y: 2, z: 4, core: 2. Of those that a mesh axis runs over, the one named last changes fastest.
Arguments:
- streams: bfloat16 [4, 1024, 2048], P(None, 'dp', ('wide', 'narrow')), may hold values from -6 to 6
- prior: bfloat16 [12, 1024, 2048], P(None, 'dp', ('wide', 'narrow')), may hold values from -6 to 6
- streams_grad: bfloat16 [4, 1024, 2048], P(None, 'dp', ('wide', 'narrow')), may hold values from -6 to 6
- w_qkv: bfloat16 [3, 2048, 2048], P(None, 'wide', 'narrow')
- qkv_bias: bfloat16 [3, 2048], P(None, ('narrow', 'wide')), may hold values from -3 to 3
- w_out: bfloat16 [2048, 2048], P('narrow', 'wide'), may hold values from -1.5 to 1.5
- w_up: bfloat16 [2048, 8192], P('wide', 'narrow')
- up_bias: bfloat16 [8192], P(('narrow', 'wide')), may hold values from -3 to 3
- w_down: bfloat16 [8192, 2048], P('narrow', 'wide'), may hold values from -0.0625 to 0.0625
- branch_bias: bfloat16 [2048], P(('wide', 'narrow')), may hold values from -3 to 3
- norm_gain: bfloat16 [4, 2048], P(None, ('wide', 'narrow')), may hold values from 0.25 to 1.75
- norm_bias: bfloat16 [4, 2048], P(None, ('wide', 'narrow')), may hold values from -2 to 2
- mix_gain: bfloat16 [2048], P(('wide', 'narrow')), may hold values from 0.099609375 to 1.8984375
- mix_in: bfloat16 [2048, 52], P(('wide', 'narrow')), may hold values from -0.125 to 0.125
- mix_out: bfloat16 [52, 52], replicated, may hold values from -0.875 to 0.875
- mix_static: bfloat16 [52], replicated, may hold values from -3 to 3
Outputs:
- streams_out: bfloat16 [4, 1024, 2048], P(None, 'dp', ('wide', 'narrow'))
- streams_in_grad: bfloat16 [4, 1024, 2048], P(None, 'dp', ('wide', 'narrow'))
- prior_grad: bfloat16 [12, 1024, 2048], P(None, 'dp', ('wide', 'narrow'))
- w_qkv_grad: float32 [3, 2048, 2048], P(None, 'wide', 'narrow')
- qkv_bias_grad: float32 [3, 2048], P(None, ('narrow', 'wide'))
- w_out_grad: float32 [2048, 2048], P('narrow', 'wide')
- w_up_grad: float32 [2048, 8192], P('wide', 'narrow')
- up_bias_grad: float32 [8192], P(('narrow', 'wide'))
- w_down_grad: float32 [8192, 2048], P('narrow', 'wide')
- branch_bias_grad: float32 [2048], P(('wide', 'narrow'))
- norm_gain_grad: float32 [4, 2048], P(None, ('wide', 'narrow'))
- norm_bias_grad: float32 [4, 2048], P(None, ('wide', 'narrow'))
- mix_gain_grad: float32 [2048], P(('wide', 'narrow'))
- mix_in_grad: float32 [2048, 52], P(('wide', 'narrow'))
- mix_out_grad: float32 [52, 52], replicated
- mix_static_grad: float32 [52], replicated
The draws below stay inside these ranges and needn't reach their ends.
All inputs are finite; a program needn't handle non-finite values.
Results may differ from the reference program's by a relative error of at most 0.02.
Values may be sent and summed in bfloat16 or wider, within the bound.
No kernel may reach another device: no remote copies, remote signals or barrier semaphores. Data moves between devices by JAX's collectives and lax.ppermute only.
A program may use at most 192 MiB of HBM per device.

```python
import math
import jax
import jax.numpy as jnp
from jax import lax

D = 2048
H = 16
HD = 128
ROT = 32
FF = 8192
MIXH = 52
STACK = 13
TOK_DEV = 256
TOKENS = 1024
N_DP = 4


def column_weights(key, rows, shape, offset_shape):
    first_key = jax.random.fold_in(key, 11)
    second_key = jax.random.fold_in(key, 23)
    spread = rows ** (-0.5)
    base = jax.random.truncated_normal(first_key, -4.0, 4.0, shape, jnp.float32) * spread
    offset = jax.random.truncated_normal(second_key, -4.0, 4.0, offset_shape, jnp.float32) * spread
    return base + offset


def draw_w_qkv(key, part):
    return column_weights(key, D, (3, D, D), (3, 1, D)).astype(jnp.bfloat16)


def draw_w_up(key, part):
    return column_weights(key, D, (D, FF), (1, FF)).astype(jnp.bfloat16)


def steps_of(stream_key, extent, shards, smallest, high):
    loudness, own = 1.0, jax.random.fold_in(stream_key, 6)
    for axis_at, blocks in shards:
        steps = jnp.exp(jax.random.uniform(jax.random.fold_in(own, axis_at), (blocks,), jnp.float32, smallest / len(shards), high / len(shards)))
        loudness = loudness * jnp.repeat(steps, extent[axis_at] // blocks).reshape([-1 if axis == axis_at else 1 for axis in range(len(extent))])
    return loudness


def gaussian(stream_key, dims, deviation, bound, pieces=(), held_as=jnp.bfloat16):
    values = deviation * jax.random.normal(stream_key, dims, jnp.float32)
    if pieces:
        values = values * steps_of(stream_key, dims, pieces, -0.22, 0.18)
    return jnp.clip(values, -bound, bound).astype(held_as)


def setup_inputs(seed: int = 0) -> dict:
    arg_keys = jax.random.split(jax.random.key(seed), 17)
    streams = gaussian(arg_keys[0], (4, TOKENS, D), 1.0, 6.0, ((1, 4), (2, 8)))
    prior = gaussian(arg_keys[1], (STACK - 1, TOKENS, D), 1.0, 6.0, ((1, 4), (2, 8)))
    streams_grad = gaussian(arg_keys[2], (4, TOKENS, D), 1.0, 6.0, ((1, 4), (2, 8)))
    w_qkv = draw_w_qkv(jax.random.fold_in(arg_keys[16], 71), 0)
    qkv_bias = gaussian(arg_keys[4], (3, D), 0.5, 3.0, ((1, 8),))
    w_out = gaussian(arg_keys[5], (D, D), (max(D // 128, 4)) ** -0.5, 1.5, ((0, 2), (1, 4)))
    w_up = draw_w_up(jax.random.fold_in(arg_keys[16], 71), 0)
    up_bias = gaussian(arg_keys[7], (FF,), 0.5, 3.0, ((0, 8),))
    w_down = gaussian(arg_keys[8], (FF, D), FF ** -0.5, 0.0625, ((0, 2), (1, 4)))
    branch_bias = gaussian(arg_keys[9], (D,), 0.5, 3.0, ((0, 8),))
    norm_gain = jnp.clip(1.0 + 0.15 * jax.random.normal(arg_keys[10], (4, D), jnp.float32), 0.25, 1.75).astype(jnp.bfloat16)
    norm_bias = gaussian(arg_keys[11], (4, D), 0.3, 2.0, ((1, 8),))
    mix_gain = jnp.clip(1.0 + 0.18 * jax.random.normal(arg_keys[12], (D,), jnp.float32), 0.099609375, 1.8984375).astype(jnp.bfloat16)
    mix_in = gaussian(arg_keys[13], (D, MIXH), D ** -0.5, 0.125, ((0, 8),))
    mix_out = gaussian(arg_keys[14], (MIXH, MIXH), MIXH ** -0.5, 0.875)
    mix_static = gaussian(arg_keys[15], (MIXH,), 0.5, 3.0)
    return {"streams": streams, "prior": prior, "streams_grad": streams_grad, "w_qkv": w_qkv, "qkv_bias": qkv_bias, "w_out": w_out, "w_up": w_up, "up_bias": up_bias, "w_down": w_down, "branch_bias": branch_bias, "norm_gain": norm_gain, "norm_bias": norm_bias, "mix_gain": mix_gain, "mix_in": mix_in, "mix_out": mix_out, "mix_static": mix_static}


@jax.custom_vjp
def low(v):
    return lax.optimization_barrier(v.astype(jnp.bfloat16)).astype(jnp.float32)

@jax.custom_vjp
def low_back(v):
    return v

def low_keep(v):
    return (low(v), None)

def low_pass(kept, grad):
    return (grad,)

def back_keep(v):
    return (v, None)

def back_low(kept, grad):
    return (low(grad),)
low.defvjp(low_keep, low_pass)
low_back.defvjp(back_keep, back_low)

def gelu_exact(inputs):
    return 0.5 * inputs * (1.0 + lax.erf(inputs * (1.0 / math.sqrt(2.0))))

def layer_norm(inputs, norm_scale, norm_shift):
    row_mean = lax.optimization_barrier(jnp.mean(inputs, axis=-1, keepdims=True))
    row_var = lax.optimization_barrier(jnp.mean(inputs * inputs, axis=-1, keepdims=True)) - row_mean * row_mean
    return (inputs - row_mean) * lax.rsqrt(row_var + 1e-05) * norm_scale + norm_shift

def rotate(heads_in, cosine, sine_table):
    half = ROT // 2
    first = heads_in[..., :half]
    second = heads_in[..., half:ROT]
    rest_part = heads_in[..., ROT:]
    cos_b = cosine[:, None, :]
    sin_b = sine_table[:, None, :]
    return jnp.concatenate([first * cos_b - second * sin_b, second * cos_b + first * sin_b, rest_part], axis=-1)

def attention(queries, key_heads, value_heads):
    length = queries.shape[0]
    row_block = min(512, length)
    scale = 1.0 / math.sqrt(HD)

    def one_block(block_index):
        row_start = block_index * row_block
        query_rows = lax.dynamic_slice_in_dim(queries, row_start, row_block, 0)
        scores = jnp.einsum('qhd,khd->hqk', query_rows, key_heads, precision=lax.Precision.HIGHEST) * scale
        scores = low_back(scores)
        row_ids = row_start + lax.broadcasted_iota(jnp.int32, (row_block, length), 0)
        col_ids = lax.broadcasted_iota(jnp.int32, (row_block, length), 1)
        scores = jnp.where((col_ids <= row_ids)[None], scores, -1e+30)
        attn_probs = low(jax.nn.softmax(scores, axis=-1))
        return jnp.einsum('hqk,khd->qhd', attn_probs, value_heads, precision=lax.Precision.HIGHEST)
    outputs = lax.map(jax.checkpoint(one_block), jnp.arange(length // row_block, dtype=jnp.int32))
    return outputs.reshape(length, H * HD)

def one_sequence(params, streams, prior):
    w_qkv, qkv_bias, w_out, w_up, up_bias, w_down, branch_bias, norm_gain, norm_bias, mix_gain, mix_in, mix_out, mix_static = params
    length = streams.shape[1]
    high = lax.Precision.HIGHEST
    normed = low(layer_norm(streams, norm_gain[:, None, :], norm_bias[:, None, :]))
    projected = jnp.einsum('std,sdf->stf', normed[:3], w_qkv, precision=high) + qkv_bias[:, None, :]
    projected = low_back(projected)
    up_pre = low_back(jnp.dot(normed[3], w_up, precision=high) + up_bias)
    positions = jnp.arange(length).astype(jnp.float32)
    freqs = jnp.exp(jnp.arange(ROT // 2).astype(jnp.float32) * (-2.0 * math.log(10000.0) / ROT))
    angles = positions[:, None] * freqs[None, :]
    cosine = jnp.cos(angles)
    sine_table = jnp.sin(angles)
    head_view = projected.reshape(3, length, H, HD)
    queries = low(rotate(head_view[0], cosine, sine_table))
    key_heads = low(rotate(head_view[1], cosine, sine_table))
    value_heads = low(head_view[2])
    attn = low(low_back(attention(queries, key_heads, value_heads)))
    hidden = low(gelu_exact(up_pre))
    branch = low_back(jnp.dot(attn, w_out, precision=high) + jnp.dot(hidden, w_down, precision=high) + branch_bias)
    layer_out = streams[3] + branch
    rms = lax.rsqrt(lax.optimization_barrier(jnp.mean(layer_out * layer_out, axis=-1, keepdims=True)) + 1e-06)
    logits = jnp.dot(layer_out * rms * mix_gain, mix_in, precision=high)
    weights = jnp.dot(gelu_exact(logits), mix_out, precision=high) + mix_static
    coef = weights.reshape(length, 4, STACK)
    mixed = jnp.einsum('tsj,jtl->stl', coef[:, :, :STACK - 1], prior, precision=high)
    return mixed + jnp.transpose(coef[:, :, STACK - 1])[:, :, None] * layer_out[None]

def reference(streams, prior, streams_grad, w_qkv, qkv_bias, w_out, w_up, up_bias, w_down, branch_bias, norm_gain, norm_bias, mix_gain, mix_in, mix_out, mix_static):
    params = tuple((item.astype(jnp.float32) for item in (w_qkv, qkv_bias, w_out, w_up, up_bias, w_down, branch_bias, norm_gain, norm_bias, mix_gain, mix_in, mix_out, mix_static)))

    def to_seqs(array, count):
        return jnp.transpose(array.astype(jnp.float32).reshape(count, N_DP, TOK_DEV, D), (1, 0, 2, 3))

    def from_seqs(array, count):
        return jnp.transpose(array, (1, 0, 2, 3)).reshape(count, TOKENS, D)
    stream_seqs = to_seqs(streams, 4)
    prior_seqs = to_seqs(prior, STACK - 1)

    def forward(params_in, stream_in, prior_in):

        def per_sequence(pair):
            return jax.checkpoint(one_sequence)(params_in, pair[0], pair[1])
        return lax.map(per_sequence, (stream_in, prior_in))
    outputs, pullback = jax.vjp(forward, params, stream_seqs, prior_seqs)
    param_grads, stream_grads, prior_grads = pullback(to_seqs(streams_grad, 4))
    streams_out = from_seqs(outputs, 4).astype(jnp.bfloat16)
    streams_in_grad = from_seqs(stream_grads, 4).astype(jnp.bfloat16)
    prior_grad = from_seqs(prior_grads, STACK - 1).astype(jnp.bfloat16)
    return (streams_out, streams_in_grad, prior_grad, param_grads[0], param_grads[1], param_grads[2], param_grads[3], param_grads[4], param_grads[5], param_grads[6], param_grads[7], param_grads[8], param_grads[9], param_grads[10], param_grads[11], param_grads[12])
```

```python
import math

import jax
import jax.numpy as jnp
from jax import lax
from jax.sharding import PartitionSpec as P

D = 2048
HD = 128
ROT = 32
MIXH = 52
STACK = 13
CORES = 2

norm_eps = 1e-05
rms_eps = 1e-06

f32 = jnp.float32
bf16 = jnp.bfloat16


def gelu_exact(inputs):
    return 0.5 * inputs * (1.0 + lax.erf(inputs * (1.0 / math.sqrt(2.0))))


def gelu_slope(inputs):
    normal_cdf = 0.5 * (1.0 + lax.erf(inputs * (1.0 / math.sqrt(2.0))))
    return normal_cdf + inputs * jnp.exp(-0.5 * inputs * inputs) * (1.0 / math.sqrt(2.0 * math.pi))


def rotate(heads_in, cosine, sine_table, direction):
    half = ROT // 2
    first = heads_in[..., :half]
    second = heads_in[..., half:ROT]
    rest_part = heads_in[..., ROT:]
    cos_b = cosine[:, None, :]
    sin_b = direction * sine_table[:, None, :]
    return jnp.concatenate(
        [first * cos_b - second * sin_b, second * cos_b + first * sin_b, rest_part], axis=-1
    )


def masked_scores(queries, key_heads, scale):
    scores = jnp.einsum("qhd,khd->hqk", queries, key_heads, preferred_element_type=f32) * scale
    length = queries.shape[0]
    row_ids = lax.broadcasted_iota(jnp.int32, (length, length), 0)
    col_ids = lax.broadcasted_iota(jnp.int32, (length, length), 1)
    return jnp.where((col_ids <= row_ids)[None], scores, -1e30)


def attend(queries, key_heads, value_heads, scale):
    scores = masked_scores(queries, key_heads, scale)
    row_top = jnp.max(scores, axis=2, keepdims=True)
    log_total = row_top + jnp.log(jnp.sum(jnp.exp(scores - row_top), axis=2, keepdims=True))
    attn_probs = jnp.exp(scores - log_total).astype(bf16)
    output = jnp.einsum("hqk,khd->qhd", attn_probs, value_heads, preferred_element_type=f32)
    return output, log_total


def attend_back(queries, key_heads, value_heads, out_grad, log_total, scale):
    scores = masked_scores(queries, key_heads, scale)
    attn_probs = jnp.exp(scores - log_total)
    probs_low = attn_probs.astype(bf16)
    value_grad = jnp.einsum("hqk,qhd->khd", probs_low, out_grad, preferred_element_type=f32)
    prob_grad = jnp.einsum("qhd,khd->hqk", out_grad, value_heads, preferred_element_type=f32)
    row_dot = jnp.sum(attn_probs * prob_grad, axis=2, keepdims=True)
    score_grad = (attn_probs * (prob_grad - row_dot)).astype(bf16)
    query_grad = jnp.einsum("hqk,khd->qhd", score_grad, key_heads, preferred_element_type=f32)
    key_grad = jnp.einsum("hqk,qhd->khd", score_grad, queries, preferred_element_type=f32)
    return query_grad * scale, key_grad * scale, value_grad


def contract_rows(left, right):
    return lax.dot_general(left, right, (((0,), (0,)), ((), ())), preferred_element_type=f32)


def contract_cols(left, right):
    return lax.dot_general(left, right, (((1,), (1,)), ((), ())), preferred_element_type=f32)


def build(n_dp, n_wide, n_narrow):
    high = lax.Precision.HIGHEST

    def shift(value, axis, size, step):
        return lax.ppermute(value, axis, [(i, (i + step) % size) for i in range(size)])

    def swap(value, axis, size, bit):
        return lax.ppermute(value, axis, [(i, i ^ bit) for i in range(size)])

    def butterfly(value, axis, size, start=1):
        bit = start
        while bit < size:
            value = value + swap(value, axis, size, bit)
            bit *= 2
        return value

    def model_sum(value):
        return butterfly(butterfly(value, "narrow", n_narrow), "wide", n_wide)

    def dp_sum(value):
        return butterfly(value, "dp", n_dp)

    def dp_gather(value):
        held = [value]
        far = value
        for _ in range(n_dp // CORES - 1):
            far = shift(far, "dp", n_dp, CORES)
            held.append(far)
        return held + [swap(item, "dp", n_dp, 1) for item in held]

    def reduce_ring(partial):
        me = lax.axis_index("wide")
        block = lambda back: lax.rem(me + (n_wide - back), n_wide)
        total = partial(block(1))
        for step in range(n_wide - 1):
            arrived = shift(total.astype(bf16), "wide", n_wide, 1)
            total = arrived.astype(f32) + partial(block(step + 2) if step + 2 < n_wide else me)
        return total

    def gather_ring(value):
        me = lax.axis_index("wide")
        held = [(me, value)]
        for step in range(1, n_wide):
            value = shift(value, "wide", n_wide, 1)
            held.append((lax.rem(me + (n_wide - step), n_wide), value))
        return held

    def narrow_pair(value, axis):
        if n_narrow == 1:
            return value
        if n_narrow != 2:
            return lax.all_gather(value, "narrow", axis=axis, tiled=True)
        other = swap(value, "narrow", n_narrow, 1)
        first = lax.axis_index("narrow") == 0
        return jnp.concatenate(
            [jnp.where(first, value, other), jnp.where(first, other, value)], axis=axis
        )

    def narrow_scatter(value, axis):
        if n_narrow == 1:
            return value
        if n_narrow != 2:
            return lax.psum_scatter(value, "narrow", scatter_dimension=axis, tiled=True)
        width = value.shape[axis] // 2
        halves = [lax.slice_in_dim(value, k * width, (k + 1) * width, axis=axis) for k in (0, 1)]
        first = lax.axis_index("narrow") == 0
        mine = jnp.where(first, halves[0], halves[1])
        theirs = jnp.where(first, halves[1], halves[0]).astype(bf16)
        return mine + swap(theirs, "narrow", n_narrow, 1).astype(f32)

    def per_device(
        streams, prior, streams_grad, w_qkv, qkv_bias, w_out, w_up, up_bias, w_down, branch_bias,
        norm_gain, norm_bias, mix_gain, mix_in, mix_out, mix_static,
    ):
        length = streams.shape[1]
        cols = streams.shape[2]
        heads = cols // HD
        scale = 1.0 / math.sqrt(HD)
        wide_rows = cols * n_narrow
        up_cols = w_up.shape[1] // n_wide
        raw = streams.astype(f32)
        sums = model_sum(jnp.stack([jnp.sum(raw, axis=2), jnp.sum(raw * raw, axis=2)]))
        row_mean = sums[0] / D
        inv_std = lax.rsqrt(sums[1] / D - row_mean * row_mean + norm_eps)
        pair = narrow_pair(streams, 2).astype(f32)
        centred_pair = (pair - row_mean[:, :, None]) * inv_std[:, :, None]
        gain_pair = narrow_pair(norm_gain, 1).astype(f32)
        shift_pair = narrow_pair(norm_bias, 1).astype(f32)
        near = (centred_pair * gain_pair[:, None, :] + shift_pair[:, None, :]).astype(bf16)
        near_all = dp_gather(near)
        centred = (raw - row_mean[:, :, None]) * inv_std[:, :, None]
        norm_scale = norm_gain.astype(f32)[:, None, :]
        grad_out = streams_grad.astype(f32)
        prior_vals = prior.astype(f32)
        prior_part = jnp.einsum("stl,jtl->tsj", grad_out, prior_vals, precision=high)
        prior_coef_grad = model_sum(prior_part.reshape(length, 4 * (STACK - 1)))

        def qkv_partial(block):
            weight = lax.dynamic_slice_in_dim(w_qkv, block * cols, cols, axis=2)
            return jnp.einsum("std,sdf->stf", near[:3], weight, preferred_element_type=f32)

        def up_partial(block):
            weight = lax.dynamic_slice_in_dim(w_up, block * up_cols, up_cols, axis=1)
            return jnp.dot(near[3], weight, preferred_element_type=f32)

        qkv_pre = reduce_ring(qkv_partial) + qkv_bias.astype(f32)[:, None, :]
        up_pre = reduce_ring(up_partial) + up_bias.astype(f32)[None, :]
        positions = lax.iota(f32, length)
        freqs = jnp.exp(lax.iota(f32, ROT // 2) * (-2.0 * math.log(10000.0) / ROT))
        angles = positions[:, None] * freqs[None, :]
        cosine = jnp.cos(angles)
        sine_table = jnp.sin(angles)
        head_view = qkv_pre.reshape(3, length, heads, HD)
        queries = rotate(head_view[0], cosine, sine_table, 1.0).astype(bf16)
        key_heads = rotate(head_view[1], cosine, sine_table, 1.0).astype(bf16)
        value_heads = head_view[2].astype(bf16)
        attn_heads, log_total = attend(queries, key_heads, value_heads, scale)
        attn_low = attn_heads.reshape(length, cols).astype(bf16)
        hidden = gelu_exact(up_pre).astype(bf16)
        attn_ring = gather_ring(attn_low)
        hidden_ring = gather_ring(hidden)
        branch_part = 0.0
        for block, item in attn_ring:
            weight = lax.dynamic_slice_in_dim(w_out, block * cols, cols, axis=0)
            branch_part = branch_part + jnp.dot(item, weight, preferred_element_type=f32)
        for block, item in hidden_ring:
            weight = lax.dynamic_slice_in_dim(w_down, block * up_cols, up_cols, axis=0)
            branch_part = branch_part + jnp.dot(item, weight, preferred_element_type=f32)
        branch = narrow_scatter(branch_part, 1) + branch_bias.astype(f32)[None, :]
        layer_out = raw[3] + branch
        mix_scale = mix_gain.astype(f32)
        scaled = layer_out * mix_scale[None, :]
        mix_weight = mix_in.astype(f32)
        mix_back = mix_out.astype(f32)
        layer_part = jnp.einsum("stl,tl->ts", grad_out, layer_out, precision=high)
        packed = model_sum(
            jnp.concatenate(
                [
                    jnp.dot(scaled, mix_weight, precision=high),
                    jnp.sum(layer_out * layer_out, axis=1)[:, None],
                    layer_part,
                ],
                axis=1,
            )
        )
        logit_sum = packed[:, :MIXH]
        energy = packed[:, MIXH]
        layer_coef_grad = packed[:, MIXH + 1 : MIXH + 5]
        rms = lax.rsqrt(energy / D + rms_eps)
        logits = logit_sum * rms[:, None]
        mix_hidden = gelu_exact(logits)
        weights = (
            jnp.dot(mix_hidden, mix_back, precision=high) + mix_static.astype(f32)[None, :]
        )
        coef = weights.reshape(length, 4, STACK)
        mixed = jnp.einsum("tsj,jtl->stl", coef[:, :, : STACK - 1], prior_vals, precision=high)
        streams_out = (
            mixed + jnp.transpose(coef[:, :, STACK - 1])[:, :, None] * layer_out[None]
        ).astype(bf16)
        coef_grad = jnp.concatenate(
            [prior_coef_grad.reshape(length, 4, STACK - 1), layer_coef_grad[:, :, None]], axis=2
        ).reshape(length, MIXH)
        prior_grad = jnp.einsum(
            "tsj,stl->jtl", coef[:, :, : STACK - 1], grad_out, precision=high
        ).astype(bf16)
        layer_grad = jnp.einsum("ts,stl->tl", coef[:, :, STACK - 1], grad_out, precision=high)
        logit_grad = jnp.dot(coef_grad, mix_back.T, precision=high) * gelu_slope(logits)
        sum_grad = logit_grad * rms[:, None]
        rms_grad = jnp.sum(logit_grad * logit_sum, axis=1)
        energy_grad = -0.5 * rms_grad * rms * rms * rms / D
        mix_in_grad = jnp.dot(scaled.T, sum_grad, precision=high)
        scaled_grad = jnp.dot(sum_grad, mix_weight.T, precision=high)
        mix_gain_grad = jnp.sum(scaled_grad * layer_out, axis=0)
        layer_grad = (
            layer_grad + scaled_grad * mix_scale[None, :] + 2.0 * energy_grad[:, None] * layer_out
        )
        branch_grad = layer_grad.astype(bf16)
        branch_bias_grad = jnp.sum(branch_grad.astype(f32), axis=0)
        share = length // (n_wide * n_narrow)
        place = (lax.axis_index("wide") * n_narrow + lax.axis_index("narrow")) * share
        coef_share = lax.dynamic_slice_in_dim(coef_grad, place, share, axis=0)
        hidden_share = lax.dynamic_slice_in_dim(mix_hidden, place, share, axis=0)
        mix_out_part = lax.dot_general(
            hidden_share, coef_share, (((0,), (0,)), ((), ())), precision=high
        )
        replicated = dp_sum(
            model_sum(
                jnp.concatenate([mix_out_part, jnp.sum(coef_share, axis=0, keepdims=True)], axis=0)
            )
        )
        mix_out_grad = replicated[:MIXH]
        static_grad = replicated[MIXH]
        branch_near = narrow_pair(branch_grad, 1)

        def hidden_back(block):
            weight = lax.dynamic_slice_in_dim(w_down, block * up_cols, up_cols, axis=0)
            return contract_cols(branch_near, weight)

        def attn_back(block):
            weight = lax.dynamic_slice_in_dim(w_out, block * cols, cols, axis=0)
            return contract_cols(branch_near, weight)

        attn_grad = reduce_ring(attn_back)
        hidden_grad = reduce_ring(hidden_back)
        up_grad = (hidden_grad * gelu_slope(up_pre)).astype(bf16)
        up_bias_grad = jnp.sum(up_grad.astype(f32), axis=0)
        attn_low_grad = attn_grad.astype(bf16).reshape(length, heads, HD)
        query_grad, key_grad, value_grad = attend_back(
            queries, key_heads, value_heads, attn_low_grad, log_total, scale
        )
        query_pre = rotate(query_grad, cosine, sine_table, -1.0).reshape(length, cols)
        key_pre = rotate(key_grad, cosine, sine_table, -1.0).reshape(length, cols)
        projected_grad = jnp.stack([query_pre, key_pre, value_grad.reshape(length, cols)])
        projected_grad = projected_grad.astype(bf16)
        qkv_bias_grad = jnp.sum(projected_grad.astype(f32), axis=1)
        up_far = gather_ring(up_grad)
        qkv_far = gather_ring(projected_grad)
        up_near_grad = 0.0
        for block, item in up_far:
            weight = lax.dynamic_slice_in_dim(w_up, block * up_cols, up_cols, axis=1)
            up_near_grad = up_near_grad + contract_cols(item, weight)
        qkv_near_grad = 0.0
        for block, item in qkv_far:
            weight = lax.dynamic_slice_in_dim(w_qkv, block * cols, cols, axis=2)
            qkv_near_grad = qkv_near_grad + jnp.einsum(
                "stf,sdf->std", item, weight, preferred_element_type=f32
            )
        near_grad = jnp.concatenate([qkv_near_grad, up_near_grad[None]], axis=0)
        scaled_near = near_grad * gain_pair[:, None, :]
        stats = model_sum(
            jnp.stack([jnp.sum(scaled_near, axis=2), jnp.sum(scaled_near * centred_pair, axis=2)])
        )
        normed_grad = narrow_scatter(near_grad, 2)
        gain_grad = jnp.sum(normed_grad * centred, axis=1)
        shift_grad = jnp.sum(normed_grad, axis=1)
        centred_grad = normed_grad * norm_scale
        input_grad = inv_std[:, :, None] * (
            centred_grad - (stats[0] / D)[:, :, None] - centred * (stats[1] / D)[:, :, None]
        )
        input_grad = input_grad.at[3].add(layer_grad)
        streams_in_grad = input_grad.astype(bf16)

        near_tokens = jnp.concatenate(near_all, axis=1)
        branch_tokens = jnp.concatenate(dp_gather(branch_near), axis=0)

        def along(ring, axis):
            held = [dp_gather(item) for _, item in ring]
            return [(block, jnp.concatenate(parts, axis=axis)) for (block, _), parts in zip(ring, held)]

        out_weight_grad = jnp.zeros(w_out.shape, f32)
        for block, item in along(attn_ring, 0):
            out_weight_grad = lax.dynamic_update_slice_in_dim(
                out_weight_grad, contract_rows(item, branch_tokens), block * cols, axis=0
            )
        down_weight_grad = jnp.zeros(w_down.shape, f32)
        for block, item in along(hidden_ring, 0):
            down_weight_grad = lax.dynamic_update_slice_in_dim(
                down_weight_grad, contract_rows(item, branch_tokens), block * up_cols, axis=0
            )
        up_weight_grad = jnp.zeros(w_up.shape, f32)
        for block, item in along(up_far, 0):
            up_weight_grad = lax.dynamic_update_slice_in_dim(
                up_weight_grad, contract_rows(near_tokens[3], item), block * up_cols, axis=1
            )
        qkv_weight_grad = jnp.zeros(w_qkv.shape, f32)
        for block, item in along(qkv_far, 1):
            qkv_weight_grad = lax.dynamic_update_slice_in_dim(
                qkv_weight_grad,
                jnp.einsum("std,stf->sdf", near_tokens[:3], item, preferred_element_type=f32),
                block * cols,
                axis=2,
            )
        small = [qkv_bias_grad, up_bias_grad, branch_bias_grad, gain_grad, shift_grad,
                 mix_gain_grad, mix_in_grad]
        flat = dp_sum(jnp.concatenate([item.reshape(-1) for item in small]))
        summed = []
        at = 0
        for item in small:
            summed.append(flat[at : at + item.size].reshape(item.shape))
            at += item.size
        return (
            streams_out, streams_in_grad, prior_grad, qkv_weight_grad, summed[0], out_weight_grad,
            up_weight_grad, summed[1], down_weight_grad, summed[2], summed[3], summed[4],
            summed[5], summed[6], mix_out_grad, static_grad,
        )

    return per_device


def solution(mesh):
    tokens = P(None, "dp", ("wide", "narrow"))
    outer = P(("wide", "narrow"))
    inner = P(None, ("wide", "narrow"))
    column = P(("narrow", "wide"))
    return jax.shard_map(
        build(mesh.shape["dp"], mesh.shape["wide"], mesh.shape["narrow"]),
        mesh=mesh,
        in_specs=(
            tokens, tokens, tokens, P(None, "wide", "narrow"), P(None, ("narrow", "wide")),
            P("narrow", "wide"), P("wide", "narrow"), column, P("narrow", "wide"), outer, inner,
            inner, outer, P(("wide", "narrow"), None), P(), P(),
        ),
        out_specs=(
            tokens, tokens, tokens, P(None, "wide", "narrow"), P(None, ("narrow", "wide")),
            P("narrow", "wide"), P("wide", "narrow"), column, P("narrow", "wide"), outer, inner,
            inner, outer, P(("wide", "narrow"), None), P(), P(),
        ),
        check_vma=False,
    )
```

```python
import functools
import math

import jax
import jax.numpy as jnp
from jax import lax
from jax.experimental import pallas as pl
from jax.experimental.pallas import tpu as pltpu
from jax.sharding import PartitionSpec as P

D = 2048
HD = 128
ROT = 32
MIXH = 52
STACK = 13
CORES = 2
LANES = 128
ROWS = 16

norm_eps = 1e-05
rms_eps = 1e-06

f32 = jnp.float32
bf16 = jnp.bfloat16
high = lax.Precision.HIGHEST
VMEM_BYTES = 48 * 1024 * 1024


def gelu_exact(inputs):
    return 0.5 * inputs * (1.0 + lax.erf(inputs * (1.0 / math.sqrt(2.0))))


def gelu_slope(inputs):
    normal_cdf = 0.5 * (1.0 + lax.erf(inputs * (1.0 / math.sqrt(2.0))))
    return normal_cdf + inputs * jnp.exp(-0.5 * inputs * inputs) * (1.0 / math.sqrt(2.0 * math.pi))


def dot(left, right, dims, precision=None):
    return lax.dot_general(
        left, right, (dims, ((), ())), precision=precision, preferred_element_type=f32
    )


def contract_rows(left, right, precision=None):
    return dot(left, right, ((0,), (0,)), precision)


def contract_cols(left, right, precision=None):
    return dot(left, right, ((1,), (1,)), precision)


def plain_dot(left, right, precision=None):
    return dot(left, right, ((1,), (0,)), precision)


def to_columns(rows_in):
    pad = jnp.zeros((LANES - rows_in.shape[0], rows_in.shape[1]), f32)
    return jnp.concatenate([rows_in, pad], axis=0).T


def lane_ids(shape):
    return lax.broadcasted_iota(jnp.int32, shape, 1)


def call(body, outs, args, scalars=(), flops=0, after=(), scratch=()):
    n_in = len(args)

    def kernel(*refs):
        body(*refs[:n_in], *refs[n_in + len(after) :])

    moved = sum(a.size * a.dtype.itemsize for a in args) + sum(
        math.prod(o.shape) * o.dtype.itemsize for o in outs
    )
    vmem = pl.BlockSpec(memory_space=pltpu.VMEM)
    smem = pl.BlockSpec(memory_space=pltpu.SMEM)
    in_specs = [smem if k in scalars else vmem for k in range(n_in)]
    in_specs += [pl.BlockSpec(memory_space=pl.ANY)] * len(after)
    return pl.pallas_call(
        kernel,
        out_shape=outs,
        in_specs=in_specs,
        out_specs=[vmem] * len(outs),
        scratch_shapes=list(scratch),
        compiler_params=pltpu.CompilerParams(vmem_limit_bytes=VMEM_BYTES),
        cost_estimate=pl.CostEstimate(flops=flops, bytes_accessed=moved, transcendentals=0),
    )(*args, *after)


def out(shape, dtype):
    return jax.ShapeDtypeStruct(shape, dtype)


def near_body(parts, *refs):
    sums = refs[0][...]
    for k in range(1, parts):
        sums = sums + refs[k][...]
    idx, own, other, gain_own, gain_other, bias_own, bias_other, near, stat = refs[parts:]
    cols = own.shape[2]
    mean = sums[0:4] * (1.0 / D)
    inv_std = lax.rsqrt(sums[4:8] * (1.0 / D) - mean * mean + norm_eps)
    table = to_columns(jnp.concatenate([mean, inv_std], axis=0))
    stat[...] = table
    at = idx[0]
    for which, (src, gain, bias) in enumerate(
        ((own, gain_own, bias_own), (other, gain_other, bias_other))
    ):
        place = pl.multiple_of((at if which == 0 else 1 - at) * cols, LANES)
        for s in range(4):
            centred = (src[s].astype(f32) - table[:, s : s + 1]) * table[:, 4 + s : 5 + s]
            value = centred * gain[s : s + 1].astype(f32) + bias[s : s + 1].astype(f32)
            near[s, :, pl.ds(place, cols)] = value.astype(bf16)


def near_stats_body(base, count, idx, grad, own, other, stat, gain_own, gain_other, theirs, stats):
    cols = own.shape[2]
    at = idx[0]
    table = stat[...]
    lanes = lane_ids(table.shape)
    packed = jnp.zeros(table.shape, f32)
    for k in range(count):
        s = base + k
        total = jnp.zeros((own.shape[1], 1), f32)
        cross = jnp.zeros((own.shape[1], 1), f32)
        for which, (src, gain) in enumerate(((own, gain_own), (other, gain_other))):
            place = pl.multiple_of((at if which == 0 else 1 - at) * cols, LANES)
            part = grad[k, :, pl.ds(place, cols)]
            if which == 1:
                theirs[k] = part.astype(bf16)
            centred = (src[s].astype(f32) - table[:, s : s + 1]) * table[:, 4 + s : 5 + s]
            scaled = part * gain[s : s + 1].astype(f32)
            total = total + jnp.sum(scaled, axis=1, keepdims=True)
            cross = cross + jnp.sum(scaled * centred, axis=1, keepdims=True)
        packed = jnp.where(lanes == k, total, packed)
        packed = jnp.where(lanes == 4 + k, cross, packed)
    stats[...] = packed.T[:8]


def norm_back_body(parts, idx, grad, arrived, own, stat, gain, *refs):
    sums = refs[0][...]
    for k in range(1, parts):
        sums = sums + refs[k][...]
    layer_grad, result, reduced = refs[parts:]
    cols = own.shape[2]
    place = pl.multiple_of(idx[0] * cols, LANES)
    table = stat[...]
    totals = to_columns(sums * (1.0 / D))
    for k in range(4):
        s = k
        value = grad[k, :, pl.ds(place, cols)] + arrived[k].astype(f32)
        inv_std = table[:, 4 + s : 5 + s]
        centred = (own[s].astype(f32) - table[:, s : s + 1]) * inv_std
        reduced[k : k + 1] = jnp.sum(value * centred, axis=0, keepdims=True)
        reduced[4 + k : 5 + k] = jnp.sum(value, axis=0, keepdims=True)
        back = inv_std * (
            value * gain[s : s + 1].astype(f32)
            - totals[:, k : k + 1]
            - centred * totals[:, 4 + k : 5 + k]
        )
        if s == 3:
            back = back + layer_grad[...]
        result[k] = back.astype(bf16)


def turn(x, tables, direction):
    cosine, low_sine, high_sine = tables
    half = ROT // 2
    return (
        x * cosine
        + direction * (jnp.roll(x, -half, axis=1) * low_sine + jnp.roll(x, half, axis=1) * high_sine)
    )


def rotary_tables(length):
    positions = lax.iota(f32, length)
    freqs = jnp.exp(lax.iota(f32, ROT // 2) * (-2.0 * math.log(10000.0) / ROT))
    angles = positions[:, None] * freqs[None, :]
    cosine = jnp.cos(angles)
    sine = jnp.sin(angles)
    zero = jnp.zeros((length, ROT // 2), f32)
    rest = jnp.zeros((length, HD - ROT), f32)
    return (
        jnp.concatenate([cosine, cosine, rest + 1.0], axis=1),
        jnp.concatenate([-sine, zero, rest], axis=1),
        jnp.concatenate([zero, sine, rest], axis=1),
    )


def probabilities(query, key, scale):
    scores = contract_cols(query, key) * scale
    rows = lax.broadcasted_iota(jnp.int32, scores.shape, 0)
    scores = jnp.where(lane_ids(scores.shape) <= rows, scores, -1e30)
    top = jnp.max(scores, axis=1, keepdims=True)
    log_total = top + jnp.log(jnp.sum(jnp.exp(scores - top), axis=1, keepdims=True))
    return jnp.exp(scores - log_total)


def forward_body(scale, arrived, own, qkv_bias, up_bias, cosine, low_sine, high_sine, qkv, pre, features):
    tables = (cosine[...], low_sine[...], high_sine[...])
    cols, width = qkv.shape[2], pre.shape[1]
    for h in range(cols // HD):
        parts = []
        for i in range(3):
            at = slice(i * cols + h * HD, i * cols + (h + 1) * HD)
            bias = qkv_bias[i : i + 1, h * HD : (h + 1) * HD].astype(f32)
            value = arrived[:, at].astype(f32) + own[:, at] + bias
            if i < 2:
                value = turn(value, tables, 1.0)
            value = value.astype(bf16)
            qkv[i, :, h * HD : (h + 1) * HD] = value
            parts.append(value)
        probs = probabilities(parts[0], parts[1], scale).astype(bf16)
        features[:, width + h * HD : width + (h + 1) * HD] = plain_dot(probs, parts[2]).astype(bf16)
    value = arrived[:, 3 * cols :].astype(f32) + own[:, 3 * cols :] + up_bias[...].astype(f32)
    pre[...] = value
    features[:, :width] = gelu_exact(value).astype(bf16)


def backward_body(scale, arrived, own, qkv, pre, cosine, low_sine, high_sine, grads, qkv_rows, up_rows):
    tables = (cosine[...], low_sine[...], high_sine[...])
    cols, width = qkv.shape[2], pre.shape[1]
    for h in range(cols // HD):
        at = slice(h * HD, (h + 1) * HD)
        query, key, value = qkv[0, :, at], qkv[1, :, at], qkv[2, :, at]
        place = slice(width + h * HD, width + (h + 1) * HD)
        out_grad = (own[:, place] + arrived[:, place].astype(f32)).astype(bf16)
        probs = probabilities(query, key, scale)
        value_grad = contract_rows(probs.astype(bf16), out_grad)
        prob_grad = contract_cols(out_grad, value)
        row_dot = jnp.sum(probs * prob_grad, axis=1, keepdims=True)
        score_grad = (probs * (prob_grad - row_dot)).astype(bf16)
        query_grad = turn(plain_dot(score_grad, key) * scale, tables, -1.0)
        key_grad = turn(contract_rows(score_grad, query) * scale, tables, -1.0)
        for i, grad in enumerate((query_grad, key_grad, value_grad)):
            low = grad.astype(bf16)
            grads[:, i * cols + h * HD : i * cols + (h + 1) * HD] = low
            qkv_rows[i : i + 1, at] = jnp.sum(low.astype(f32), axis=0, keepdims=True)
    qkv_rows[3:8] = jnp.zeros((5, cols), f32)
    total = arrived[:, :width].astype(f32) + own[:, :width]
    low = (total * gelu_slope(pre[...])).astype(bf16)
    grads[:, 3 * cols :] = low
    for t in range(8):
        if t < width // cols:
            part = low[:, t * cols : (t + 1) * cols].astype(f32)
            up_rows[t : t + 1] = jnp.sum(part, axis=0, keepdims=True)
        else:
            up_rows[t : t + 1] = jnp.zeros((1, cols), f32)


def fold(value):
    total = value[:, :LANES]
    for k in range(1, value.shape[1] // LANES):
        total = total + value[:, k * LANES : (k + 1) * LANES]
    return total


def prior_body(grad_out, prior, result, held):
    def group(r, carry):
        rows = pl.ds(pl.multiple_of(r * ROWS, ROWS), ROWS)
        grads = [grad_out[s, rows, :].astype(f32) for s in range(4)]
        lanes = lane_ids((ROWS, LANES))
        packed = jnp.zeros((ROWS, LANES), f32)
        for j in range(STACK - 1):
            value = prior[j, rows, :].astype(f32)
            for s in range(4):
                column = jnp.sum(fold(grads[s] * value), axis=1, keepdims=True)
                packed = jnp.where(lanes == s * STACK + j, column, packed)
        held[rows, :] = packed
        return carry

    lax.fori_loop(0, held.shape[0] // ROWS, group, 0)
    result[...] = held[...].T[:64]


def prior_products(streams_grad, prior, after=()):
    length, cols = prior.shape[1:]
    block = min(length, LANES)

    def kernel(grad_ref, prior_ref, *refs):
        prior_body(grad_ref, prior_ref, *refs[len(after) :])

    return pl.pallas_call(
        kernel,
        grid=(length // block,),
        out_shape=out((64, length), f32),
        in_specs=[
            pl.BlockSpec((4, block, cols), lambda t: (0, t, 0)),
            pl.BlockSpec((STACK - 1, block, cols), lambda t: (0, t, 0)),
        ]
        + [pl.BlockSpec(memory_space=pl.ANY)] * len(after),
        out_specs=pl.BlockSpec((64, block), lambda t: (0, t)),
        scratch_shapes=[pltpu.VMEM((block, LANES), f32)],
        compiler_params=pltpu.CompilerParams(vmem_limit_bytes=VMEM_BYTES),
        cost_estimate=pl.CostEstimate(
            flops=20_000_000, bytes_accessed=2 * length * cols * 16, transcendentals=0
        ),
    )(streams_grad, prior, *after)


def mix_first_body(
    parts, streams, own, *refs
):
    arrived = refs[:parts]
    branch_bias, gain, mix_in, grad_out, layer_out, packed_out = refs[parts:]
    value = own[...]
    for item in arrived:
        value = value + item[...].astype(f32)
    value = streams[3].astype(f32) + (value + branch_bias[...].astype(f32))
    layer_out[...] = value
    packed = plain_dot(value * gain[...].astype(f32), mix_in[...], high)
    lanes = lane_ids(packed.shape)
    energy = jnp.sum(fold(value * value), axis=1, keepdims=True)
    packed = jnp.where(lanes == MIXH, energy, packed)
    for s in range(4):
        column = jnp.sum(fold(grad_out[s].astype(f32) * value), axis=1, keepdims=True)
        packed = jnp.where(lanes == MIXH + 1 + s, column, packed)
    packed_out[...] = packed.T[:64]


def mix_second_body(parts, me, *refs):
    held = refs[-1]
    for k in range(parts):
        held[lax.rem(me[0] + (parts - k), parts)] = refs[k][...]
    sums = held[0]
    for k in range(1, parts):
        sums = sums + held[k]
    for k in range(parts):
        held[lax.rem(me[0] + (parts - k), parts)] = refs[parts + k][...]
    prior_coef = held[0]
    for k in range(1, parts):
        prior_coef = prior_coef + held[k]
    (layer_out, grad_out, gain, mix_in, mix_out, mix_static,
     branch_grad, layer_grad, tables, reduced) = refs[2 * parts : -1]
    packed = to_columns(sums)
    lanes = lane_ids(packed.shape)
    energy = packed[:, MIXH : MIXH + 1]
    rms = lax.rsqrt(energy * (1.0 / D) + rms_eps)
    logit_sum = jnp.where(lanes < MIXH, packed, 0.0)
    logits = logit_sum * rms
    mix_hidden = gelu_exact(logits)
    coef = plain_dot(mix_hidden, mix_out[...], high) + mix_static[...]
    coef_grad = to_columns(prior_coef)
    for s in range(4):
        column = packed[:, MIXH + 1 + s : MIXH + 2 + s]
        coef_grad = jnp.where(lanes == s * STACK + STACK - 1, column, coef_grad)
    logit_grad = contract_cols(coef_grad, mix_out[...], high) * gelu_slope(logits)
    sum_grad = logit_grad * rms
    rms_grad = jnp.sum(logit_grad * logit_sum, axis=1, keepdims=True)
    energy_grad = rms_grad * rms * rms * rms * (-1.0 / D)
    value = layer_out[...]
    scaled_grad = contract_cols(sum_grad, mix_in[...], high)
    total = scaled_grad * gain[...].astype(f32) + energy_grad * value
    for s in range(4):
        at = s * STACK + STACK - 1
        total = total + coef[:, at : at + 1] * grad_out[s].astype(f32)
    low = total.astype(bf16)
    branch_grad[...] = low
    layer_grad[...] = total
    tables[0] = coef
    tables[1] = coef_grad
    tables[2] = mix_hidden
    tables[3] = sum_grad
    cols = value.shape[1]
    reduced[0:1] = jnp.sum(scaled_grad * value, axis=0, keepdims=True)
    reduced[1:2] = jnp.sum(low.astype(f32), axis=0, keepdims=True)
    reduced[2:8] = jnp.zeros((6, cols), f32)


def mix_third_body(tables, layer_out, prior, grad_out, gain,
                   streams_out, prior_grad, weight_grads):
    block, cols = layer_out.shape

    def group(r, carry):
        rows = pl.ds(pl.multiple_of(r * ROWS, ROWS), ROWS)
        coef = tables[0, rows, :]
        grads = [grad_out[s, rows, :].astype(f32) for s in range(4)]
        value = layer_out[rows, :]
        totals = []
        for s in range(4):
            at = s * STACK + STACK - 1
            totals.append(coef[:, at : at + 1] * value)
        for j in range(STACK - 1):
            value = prior[j, rows, :].astype(f32)
            back = None
            for s in range(4):
                at = s * STACK + j
                column = jnp.broadcast_to(coef[:, at : at + 1], (ROWS, cols))
                totals[s] = totals[s] + column * value
                term = column * grads[s]
                back = term if back is None else back + term
            prior_grad[j, rows, :] = back.astype(bf16)
        for s in range(4):
            streams_out[s, rows, :] = totals[s].astype(bf16)
        return carry

    lax.fori_loop(0, block // ROWS, group, 0)
    step = pl.program_id(0)

    @pl.when(step == 0)
    def _():
        weight_grads[...] = jnp.zeros(weight_grads.shape, f32)

    scaled = layer_out[...] * gain[...].astype(f32)
    weight_grads[:cols] += contract_rows(scaled, tables[3], high)
    chosen = jnp.where(lane_ids((block, LANES)) == MIXH, 1.0, tables[2])
    weight_grads[cols:] += contract_rows(chosen, tables[1], high)[: weight_grads.shape[0] - cols]


def mix_third(tables, layer_out, prior, streams_grad, gain, after=()):
    length, cols = layer_out.shape
    block = min(length, 64)
    tokens = lambda count: pl.BlockSpec((count, block, cols), lambda t: (0, t, 0))

    def kernel(*refs):
        mix_third_body(*refs[:5], *refs[5 + len(after) :])

    return pl.pallas_call(
        kernel,
        grid=(length // block,),
        out_shape=[
            out((4, length, cols), bf16),
            out((STACK - 1, length, cols), bf16),
            out((cols + 56, LANES), f32),
        ],
        in_specs=[
            pl.BlockSpec((4, block, LANES), lambda t: (0, t, 0)),
            pl.BlockSpec((block, cols), lambda t: (t, 0)),
            tokens(STACK - 1),
            tokens(4),
            pl.BlockSpec((1, cols), lambda t: (0, 0)),
        ]
        + [pl.BlockSpec(memory_space=pl.ANY)] * len(after),
        out_specs=[
            tokens(4),
            tokens(STACK - 1),
            pl.BlockSpec((cols + 56, LANES), lambda t: (0, 0)),
        ],
        compiler_params=pltpu.CompilerParams(vmem_limit_bytes=VMEM_BYTES),
        cost_estimate=pl.CostEstimate(
            flops=30_000_000, bytes_accessed=2 * length * cols * 34, transcendentals=0
        ),
    )(tables, layer_out, prior, streams_grad, gain, *after)


def cost(flops, moved):
    return pl.CostEstimate(flops=flops, bytes_accessed=moved, transcendentals=0)


ANY = pl.BlockSpec(memory_space=pl.ANY)
PARAMS = pltpu.CompilerParams(vmem_limit_bytes=VMEM_BYTES)


def prefetched(kernel, scalars, grid, in_specs, out_specs, out_shape, args, estimate, aliases=None):
    return pl.pallas_call(
        kernel,
        grid_spec=pltpu.PrefetchScalarGridSpec(
            num_scalar_prefetch=len(scalars), grid=grid, in_specs=in_specs, out_specs=out_specs
        ),
        out_shape=out_shape,
        input_output_aliases=aliases or {},
        compiler_params=PARAMS,
        cost_estimate=estimate,
    )(*scalars, *args)


def spread(block, near, w_qkv, w_up, up_cols, dtype, after):
    _, length, depth = near.shape
    cols = depth // 2
    width = 3 * cols + up_cols

    def kernel(b, near_ref, qkv_ref, up_ref, *refs):
        step = pl.program_id(0)

        @pl.when(step < 3)
        def _():
            place = pl.multiple_of(step * cols, LANES)
            refs[-1][:, pl.ds(place, cols)] = plain_dot(near_ref[0], qkv_ref[0]).astype(dtype)

        @pl.when(step == 3)
        def _():
            refs[-1][:, 3 * cols :] = plain_dot(near_ref[0], up_ref[...]).astype(dtype)

    return prefetched(
        kernel,
        [block],
        (4,),
        [
            pl.BlockSpec((1, length, depth), lambda i, b: (i, 0, 0)),
            pl.BlockSpec((1, depth, cols), lambda i, b: (jnp.minimum(i, 2), 0, b[0])),
            pl.BlockSpec((depth, up_cols), lambda i, b: (0, b[0])),
        ]
        + [ANY] * len(after),
        pl.BlockSpec((length, width), lambda i, b: (0, 0)),
        out((length, width), dtype),
        [near, w_qkv, w_up, *after],
        cost(2 * length * depth * width, 2 * depth * width + 4 * length * width),
    )


def spread_back(idx, block, own, other, w_down, w_out, up_cols, dtype, after):
    length, cols = own.shape

    def kernel(b, idx_ref, own_ref, other_ref, down_ref, out_ref, *refs):
        result, pair = refs[-2:]
        pair[:, pl.ds(pl.multiple_of(idx_ref[0] * cols, LANES), cols)] = own_ref[...]
        pair[:, pl.ds(pl.multiple_of((1 - idx_ref[0]) * cols, LANES), cols)] = other_ref[...]
        result[:, :up_cols] = contract_cols(pair[...], down_ref[...]).astype(dtype)
        result[:, up_cols:] = contract_cols(pair[...], out_ref[...]).astype(dtype)

    depth = up_cols + cols
    whole = pl.BlockSpec((length, cols), lambda i, b, x: (0, 0))
    return pl.pallas_call(
        kernel,
        grid_spec=pltpu.PrefetchScalarGridSpec(
            num_scalar_prefetch=2,
            grid=(1,),
            in_specs=[
                whole,
                whole,
                pl.BlockSpec((up_cols, 2 * cols), lambda i, b, x: (b[0], 0)),
                pl.BlockSpec((cols, 2 * cols), lambda i, b, x: (b[0], 0)),
            ]
            + [ANY] * len(after),
            out_specs=pl.BlockSpec((length, depth), lambda i, b, x: (0, 0)),
            scratch_shapes=[pltpu.VMEM((length, 2 * cols), bf16)],
        ),
        out_shape=out((length, depth), dtype),
        compiler_params=PARAMS,
        cost_estimate=cost(4 * length * depth * cols, 4 * depth * cols + 4 * length * depth),
    )(block, idx, own, other, w_down, w_out, *after)


def add_body(arrived, term, result):
    result[...] = (arrived[...].astype(f32) + term[...]).astype(bf16)


def branch_step(block, item, so_far, w_down, w_out, up_cols, after):
    length, depth = item.shape
    cols = depth - up_cols
    wide_cols = w_down.shape[1]
    earlier = [] if so_far is None else [so_far]
    whole = pl.BlockSpec((length, wide_cols), lambda i, b: (0, 0))

    def kernel(b, item_ref, down_ref, out_ref, *refs):
        value = plain_dot(item_ref[:, :up_cols], down_ref[...]) + plain_dot(
            item_ref[:, up_cols:], out_ref[...]
        )
        refs[-1][...] = refs[0][...] + value if earlier else value

    return prefetched(
        kernel,
        [block],
        (1,),
        [
            pl.BlockSpec((length, depth), lambda i, b: (0, 0)),
            pl.BlockSpec((up_cols, wide_cols), lambda i, b: (b[0], 0)),
            pl.BlockSpec((cols, wide_cols), lambda i, b: (b[0], 0)),
        ]
        + [whole] * len(earlier)
        + [ANY] * len(after),
        whole,
        out((length, wide_cols), f32),
        [item, w_down, w_out, *earlier, *after],
        cost(2 * length * depth * wide_cols, 2 * depth * wide_cols),
    )


def halves_body(idx, value, theirs, mine):
    cols = mine.shape[1]
    mine[...] = value[:, pl.ds(pl.multiple_of(idx[0] * cols, LANES), cols)]
    theirs[...] = value[:, pl.ds(pl.multiple_of((1 - idx[0]) * cols, LANES), cols)].astype(bf16)


def near_step(block, item, so_far, w_qkv, w_up, cols, after):
    length = item.shape[0]
    depth = w_up.shape[0]
    up_cols = item.shape[1] - 3 * cols
    earlier = [] if so_far is None else [so_far]
    one = pl.BlockSpec((1, length, depth), lambda s, b: (s, 0, 0))

    def kernel(b, item_ref, qkv_ref, up_ref, *refs):
        step = pl.program_id(0)
        base = refs[0][0] if earlier else 0.0

        @pl.when(step < 3)
        def _():
            part = item_ref[:, pl.ds(pl.multiple_of(step * cols, LANES), cols)]
            refs[-1][0] = contract_cols(part, qkv_ref[0]) + base

        @pl.when(step == 3)
        def _():
            refs[-1][0] = contract_cols(item_ref[:, 3 * cols :], up_ref[...]) + base

    return prefetched(
        kernel,
        [block],
        (4,),
        [
            pl.BlockSpec(item.shape, lambda s, b: (0, 0)),
            pl.BlockSpec((1, depth, cols), lambda s, b: (jnp.minimum(s, 2), 0, b[0])),
            pl.BlockSpec((depth, up_cols), lambda s, b: (0, b[0])),
        ]
        + [one] * len(earlier)
        + [ANY] * len(after),
        one,
        out((4, length, depth), f32),
        [item, w_qkv, w_up, *earlier, *after],
        cost(2 * item.size * depth, 2 * item.size * depth // length + 32 * length * depth),
    )


def near_weights(order, block, near, parts, shapes, before):
    n_dp, _, length, depth = near.shape
    cols = depth // 2
    tiles = parts[0].shape[1] // cols - 3

    def kernel(order_ref, b, near_ref, *refs):
        left, right = refs[-2:]
        qkv_grad, up_grad, done = refs[-5:-2]
        done[...] = jnp.zeros(done.shape, f32)
        step = pl.program_id(0)

        @pl.when(step <= 3)
        def _():
            for p in range(n_dp):
                left[:, p * length : (p + 1) * length] = near_ref[order_ref[p], 0].T

        place = pl.multiple_of(step * cols, LANES)
        for p in range(n_dp):
            right[p * length : (p + 1) * length] = refs[p][:, pl.ds(place, cols)]
        value = plain_dot(left[...], right[...])

        @pl.when(step < 3)
        def _():
            qkv_grad[0] = value

        @pl.when(step >= 3)
        def _():
            up_grad[...] = value

    total = sum(item.size for item in parts)
    return pl.pallas_call(
        kernel,
        grid_spec=pltpu.PrefetchScalarGridSpec(
            num_scalar_prefetch=2,
            grid=(3 + tiles,),
            in_specs=[
                pl.BlockSpec((n_dp, 1, length, depth), lambda i, o, b: (0, jnp.minimum(i, 3), 0, 0))
            ]
            + [pl.BlockSpec(parts[0].shape, lambda i, o, b: (0, 0))] * n_dp
            + [ANY] * len(before),
            out_specs=[
                pl.BlockSpec((1, depth, cols), lambda i, o, b: (jnp.minimum(i, 2), 0, b[0])),
                pl.BlockSpec(
                    (depth, cols), lambda i, o, b: (0, b[0] * tiles + jnp.maximum(i - 3, 0))
                ),
                pl.BlockSpec((8, LANES), lambda i, o, b: (0, 0)),
            ],
            scratch_shapes=[
                pltpu.VMEM((depth, n_dp * length), bf16),
                pltpu.VMEM((n_dp * length, cols), bf16),
            ],
        ),
        out_shape=[out(shape, f32) for shape in (*shapes, (8, LANES))],
        input_output_aliases={3 + n_dp + k: k for k in range(len(before))},
        compiler_params=PARAMS,
        cost_estimate=cost(2 * depth * total, 2 * total + 4 * depth * total // length),
    )(order, block, near, *parts, *before)


def branch_weights(order, block, features, parts, up_cols, shapes, before):
    n_dp, length, depth = features.shape
    cols = depth - up_cols
    width = parts[0].shape[1]

    def kernel(order_ref, b, features_ref, *refs):
        left = jnp.concatenate([features_ref[order_ref[p]] for p in range(n_dp)], axis=0)
        right = jnp.concatenate([item[...] for item in refs[:n_dp]], axis=0)
        refs[-3][...] = contract_rows(left[:, :up_cols], right)
        refs[-2][...] = contract_rows(left[:, up_cols:], right)
        refs[-1][...] = jnp.zeros(refs[-1].shape, f32)

    return prefetched(
        kernel,
        [order, block],
        (1,),
        [pl.BlockSpec(features.shape, lambda i, o, b: (0, 0, 0))]
        + [pl.BlockSpec((length, width), lambda i, o, b: (0, 0))] * n_dp
        + [ANY] * len(before),
        [
            pl.BlockSpec((up_cols, width), lambda i, o, b: (b[0], 0)),
            pl.BlockSpec((cols, width), lambda i, o, b: (b[0], 0)),
            pl.BlockSpec((8, LANES), lambda i, o, b: (0, 0)),
        ],
        [out(shape, f32) for shape in (*shapes, (8, LANES))],
        [features, *parts, *before],
        cost(2 * features.size * width, 2 * features.size + 4 * depth * width),
        {3 + n_dp + k: k for k in range(len(before))},
    )


def gate(value, after):
    def kernel(*refs):
        pass

    spec = pl.BlockSpec(memory_space=pl.ANY)
    return pl.pallas_call(
        kernel,
        out_shape=out(value.shape, value.dtype),
        in_specs=[spec] * (1 + len(after)),
        out_specs=spec,
        input_output_aliases={0: 0},
        compiler_params=pltpu.CompilerParams(has_side_effects=True),
    )(value, *after)


def stats_body(streams, sums):
    length = streams.shape[1]
    lanes = lane_ids((length, LANES))
    packed = jnp.zeros((length, LANES), f32)
    for s in range(4):
        value = streams[s].astype(f32)
        packed = jnp.where(lanes == s, jnp.sum(fold(value), axis=1, keepdims=True), packed)
        packed = jnp.where(
            lanes == 4 + s, jnp.sum(fold(value * value), axis=1, keepdims=True), packed
        )
    sums[...] = packed.T[:8]


def build(n_dp, n_wide, n_narrow):
    def shift(value, axis, size, step):
        return lax.ppermute(value, axis, [(i, (i + step) % size) for i in range(size)])

    def swap(value, axis, size, bit):
        return lax.ppermute(value, axis, [(i, i ^ bit) for i in range(size)])

    def butterfly(value, axis, size):
        bit = 1
        while bit < size:
            value = value + swap(value, axis, size, bit)
            bit *= 2
        return value

    def narrow_swap(value):
        return swap(value, "narrow", n_narrow, 1)

    def model_parts(value):
        value = value + narrow_swap(value)
        return [value] + [shift(value, "wide", n_wide, k) for k in range(1, n_wide)]

    def model_butterfly(value):
        return butterfly(butterfly(value, "narrow", n_narrow), "wide", n_wide)

    def dp_sum(value):
        return butterfly(value, "dp", n_dp)

    def dp_gather(value):
        held = [value]
        far = value
        for _ in range(n_dp // CORES - 1):
            far = shift(far, "dp", n_dp, CORES)
            held.append(far)
        return held + [swap(item, "dp", n_dp, 1) for item in held]

    def across(value):
        held = [value]
        for _ in range(n_dp // CORES - 1):
            held.append(shift(held[-1], "dp", n_dp, CORES))
        return held

    def dp_order():
        me = lax.axis_index("dp")
        steps = [lax.rem(me + n_dp - CORES * k, n_dp) for k in range(n_dp // CORES)]
        return steps + [item ^ 1 for item in steps]

    def reduce_ring(product, hold):
        me = lax.axis_index("wide").astype(jnp.int32)
        block = lambda back: lax.rem(me + (n_wide - back), n_wide)[None]
        total = product(block(1), bf16, [])
        sent = [total]
        for at in range(n_wide - 1):
            arrived = shift(total, "wide", n_wide, 1)
            term = product(block(at + 2) if at + 2 < n_wide else me[None], f32, [total])
            if at < n_wide - 2:
                (total,) = call(
                    add_body, [out(total.shape, bf16)], [arrived, term], after=hold(at, total)
                )
                sent.append(total)
        return arrived, term, sent

    def per_device(
        streams, prior, streams_grad, w_qkv, qkv_bias, w_out, w_up, up_bias, w_down, branch_bias,
        norm_gain, norm_bias, mix_gain, mix_in, mix_out, mix_static,
    ):
        length = streams.shape[1]
        cols = streams.shape[2]
        scale = 1.0 / math.sqrt(HD)
        up_cols = w_up.shape[1] // n_wide
        tiles = up_cols // cols
        depth = up_cols + cols
        idx = lax.axis_index("narrow").astype(jnp.int32)[None]
        me = lax.axis_index("wide").astype(jnp.int32)
        order = jnp.stack(dp_order()).astype(jnp.int32)
        other = narrow_swap(streams)
        (sums,) = call(stats_body, [out((8, length), f32)], [streams])
        wide_sum = sums
        for k in range(1, n_wide):
            wide_sum = wide_sum + shift(sums, "wide", n_wide, k)
        stat_parts = [wide_sum, narrow_swap(wide_sum)]
        params = jnp.concatenate([norm_gain, norm_bias], axis=0)
        other_params = narrow_swap(params)
        gain_other, bias_other = other_params[:4], other_params[4:]
        near, stat = call(
            functools.partial(near_body, len(stat_parts)),
            [out((4, length, 2 * cols), bf16), out((length, LANES), f32)],
            [*stat_parts, idx, streams, other, norm_gain, gain_other, norm_bias, bias_other],
            scalars={2},
        )
        tables = rotary_tables(length)

        near_all = lax.all_gather(near, "dp", axis=0, tiled=False)
        tables = rotary_tables(length)
        arrived, own, sent = reduce_ring(
            lambda block, dtype, after: spread(block, near, w_qkv, w_up, up_cols, dtype, after),
            lambda at, total: [],
        )
        prior_rows = prior_products(streams_grad, prior, after=[sent[0]])
        prior_side = prior_rows + narrow_swap(prior_rows)
        prior_parts = [prior_side] + [shift(prior_side, "wide", n_wide, k) for k in range(1, n_wide)]
        qkv, up_pre, features = call(
            functools.partial(forward_body, scale),
            [
                out((3, length, cols), bf16),
                out((length, up_cols), f32),
                out((length, up_cols + cols), bf16),
            ],
            [arrived, own, qkv_bias, up_bias[None], *tables],
            flops=8 * length * length * cols,
            after=[prior_side],
        )
        blocks = [lax.rem(me + (n_wide - k), n_wide)[None] for k in range(n_wide)]
        item, branch_part, features_all = features, None, []
        for k in range(n_wide):
            branch_part = branch_step(blocks[k], item, branch_part, w_down, w_out, up_cols, [])
            features_all.append(lax.all_gather(item, "dp", axis=0, tiled=False))
            if k < n_wide - 1:
                side = prior_parts if k == 0 else []
                item = gate(shift(item, "wide", n_wide, 1), [branch_part, *side])
        theirs, branch_own = call(
            halves_body,
            [out((length, cols), bf16), out((length, cols), f32)],
            [idx, branch_part],
            scalars={0},
        )
        branch_arrived = narrow_swap(theirs)
        mix_in_pad = jnp.pad(mix_in.astype(f32), ((0, 0), (0, LANES - MIXH)))
        mix_out_pad = jnp.pad(mix_out.astype(f32), ((0, LANES - MIXH), (0, LANES - MIXH)))
        static_pad = jnp.pad(mix_static.astype(f32)[None], ((0, 0), (0, LANES - MIXH)))
        gain_row = mix_gain[None]
        layer_out, packed = call(
            functools.partial(mix_first_body, 1),
            [out((length, cols), f32), out((64, length), f32)],
            [streams, branch_own, branch_arrived, branch_bias[None], gain_row, mix_in_pad, streams_grad],
            after=[near_all],
        )
        packed_parts = model_parts(packed)
        branch_grad, layer_grad, mixed, mix_rows = call(
            functools.partial(mix_second_body, n_wide),
            [
                out((length, cols), bf16),
                out((length, cols), f32),
                out((4, length, LANES), f32),
                out((8, cols), f32),
            ],
            [me[None], *packed_parts, *prior_parts, layer_out, streams_grad, gain_row, mix_in_pad,
             mix_out_pad, static_pad],
            scalars={0},
            scratch=[pltpu.VMEM((n_wide, 64, length), f32)],
        )
        branch_other = narrow_swap(branch_grad)
        mixer_outs, branch_grads, tokens = [], [], []

        def branch_side(at, total):
            if at == 0:
                mixer_outs.extend(
                    mix_third(mixed, layer_out, prior, streams_grad, gain_row, after=[total])
                )
                first = lax.axis_index("narrow") == 0
                pair = [gate(branch_grad, [total]), branch_other]
                near = jnp.concatenate(
                    [jnp.where(first, pair[0], pair[1]), jnp.where(first, pair[1], pair[0])], axis=1
                )
                branch_all = dp_gather(near)
                for k, block in enumerate(blocks):
                    *grads, token = branch_weights(
                        order, block, features_all[k], branch_all, up_cols,
                        (w_down.shape, w_out.shape), branch_grads[-1] if branch_grads else [],
                    )
                    branch_grads.append(grads)
                    tokens.append(token)
                return [mixer_outs[2]]
            return tokens[:1]

        arrived, own, sent = reduce_ring(
            lambda block, dtype, after: spread_back(
                idx, block, branch_grad, branch_other, w_down, w_out, up_cols, dtype, after
            ),
            lambda at, total: branch_side(at, total),
        )
        grads, qkv_rows, up_rows = call(
            functools.partial(backward_body, scale),
            [
                out((length, up_cols + 3 * cols), bf16),
                out((8, cols), f32),
                out((8, cols), f32),
            ],
            [arrived, own, qkv, up_pre, *tables],
            flops=14 * length * length * cols,
            after=tokens[:2],
        )
        item, near_grad, near_grads, held = grads, None, [], []
        for k in range(n_wide):
            near_grad = near_step(blocks[k], item, near_grad, w_qkv, w_up, cols, [])
            held.append(across(item))
            after = [near_grad, held[k][-1], *tokens[2:]]
            if k:
                crossed = held[k - 1] + [swap(part, "dp", n_dp, 1) for part in held[k - 1]]
                *near_grads, token = near_weights(
                    order, blocks[k - 1], near_all, crossed, (w_qkv.shape, w_up.shape), near_grads
                )
                after.append(token)
            if k < n_wide - 1:
                item = gate(shift(item, "wide", n_wide, 1), after)
        crossed = held[-1] + [swap(part, "dp", n_dp, 1) for part in held[-1]]
        *near_grads, _ = near_weights(
            order, blocks[-1], near_all, crossed, (w_qkv.shape, w_up.shape), near_grads
        )
        down_weight_grad, out_weight_grad = branch_grads[-1]
        streams_out, prior_grad, mix_weight_grads = mixer_outs
        qkv_weight_grad, up_weight_grad = near_grads
        theirs, stats = call(
            functools.partial(near_stats_body, 0, 4),
            [out((4, length, cols), bf16), out((8, length), f32)],
            [idx, near_grad, streams, other, stat, norm_gain, gain_other],
            scalars={0},
        )
        wide_sum = stats
        for k in range(1, n_wide):
            wide_sum = wide_sum + shift(stats, "wide", n_wide, k)
        stat_parts = [wide_sum, narrow_swap(wide_sum)]
        streams_in_grad, near_rows = call(
            functools.partial(norm_back_body, len(stat_parts)),
            [out((4, length, cols), bf16), out((8, cols), f32)],
            [idx, near_grad, narrow_swap(theirs), streams, stat, norm_gain, *stat_parts, layer_grad],
            scalars={0},
        )
        mix_sums = dp_sum(mix_weight_grads)
        rows = dp_sum(jnp.concatenate([qkv_rows, mix_rows, up_rows, near_rows], axis=0))
        gain_grad, shift_grad = rows[24:28], rows[28:32]
        return (
            streams_out, streams_in_grad, prior_grad, qkv_weight_grad, rows[0:3], out_weight_grad,
            up_weight_grad, rows[16 : 16 + tiles].reshape(-1), down_weight_grad, rows[9], gain_grad,
            shift_grad, rows[8], mix_sums[:cols, :MIXH], mix_sums[cols : cols + MIXH, :MIXH],
            mix_sums[cols + MIXH, :MIXH],
        )

    return per_device


def solution(mesh):
    tokens = P(None, "dp", ("wide", "narrow"))
    outer = P(("wide", "narrow"))
    inner = P(None, ("wide", "narrow"))
    column = P(("narrow", "wide"))
    return jax.shard_map(
        build(mesh.shape["dp"], mesh.shape["wide"], mesh.shape["narrow"]),
        mesh=mesh,
        in_specs=(
            tokens, tokens, tokens, P(None, "wide", "narrow"), P(None, ("narrow", "wide")),
            P("narrow", "wide"), P("wide", "narrow"), column, P("narrow", "wide"), outer, inner,
            inner, outer, P(("wide", "narrow"), None), P(), P(),
        ),
        out_specs=(
            tokens, tokens, tokens, P(None, "wide", "narrow"), P(None, ("narrow", "wide")),
            P("narrow", "wide"), P("wide", "narrow"), column, P("narrow", "wide"), outer, inner,
            inner, outer, P(("wide", "narrow"), None), P(), P(),
        ),
        check_vma=False,
    )
```

```python
import functools
import math

import jax
import jax.numpy as jnp
from jax import lax
from jax.experimental import pallas as pl
from jax.experimental.pallas import tpu as pltpu
from jax.sharding import PartitionSpec as P

D = 2048
HD = 128
ROT = 32
MIXH = 52
STACK = 13
CORES = 2
LANES = 128
ROWS = 16

norm_eps = 1e-05
rms_eps = 1e-06

f32 = jnp.float32
bf16 = jnp.bfloat16
high = lax.Precision.HIGHEST
VMEM_BYTES = 48 * 1024 * 1024


def gelu_exact(inputs):
    return 0.5 * inputs * (1.0 + lax.erf(inputs * (1.0 / math.sqrt(2.0))))


def gelu_slope(inputs):
    normal_cdf = 0.5 * (1.0 + lax.erf(inputs * (1.0 / math.sqrt(2.0))))
    return normal_cdf + inputs * jnp.exp(-0.5 * inputs * inputs) * (1.0 / math.sqrt(2.0 * math.pi))


def dot(left, right, dims, precision=None):
    return lax.dot_general(
        left, right, (dims, ((), ())), precision=precision, preferred_element_type=f32
    )


def contract_rows(left, right, precision=None):
    return dot(left, right, ((0,), (0,)), precision)


def contract_cols(left, right, precision=None):
    return dot(left, right, ((1,), (1,)), precision)


def plain_dot(left, right, precision=None):
    return dot(left, right, ((1,), (0,)), precision)


def to_columns(rows_in):
    pad = jnp.zeros((LANES - rows_in.shape[0], rows_in.shape[1]), f32)
    return jnp.concatenate([rows_in, pad], axis=0).T


def lane_ids(shape):
    return lax.broadcasted_iota(jnp.int32, shape, 1)


def waits(after):
    return [
        pl.BlockSpec(memory_space=pltpu.VMEM if item.size <= 4096 else pl.ANY) for item in after
    ]


def call(body, outs, args, scalars=(), flops=0, after=(), scratch=()):
    n_in = len(args)

    def kernel(*refs):
        body(*refs[:n_in], *refs[n_in + len(after) :])

    moved = sum(a.size * a.dtype.itemsize for a in args) + sum(
        math.prod(o.shape) * o.dtype.itemsize for o in outs
    )
    vmem = pl.BlockSpec(memory_space=pltpu.VMEM)
    smem = pl.BlockSpec(memory_space=pltpu.SMEM)
    in_specs = [smem if k in scalars else vmem for k in range(n_in)]
    in_specs += waits(after)
    return pl.pallas_call(
        kernel,
        out_shape=outs,
        in_specs=in_specs,
        out_specs=[vmem] * len(outs),
        scratch_shapes=list(scratch),
        compiler_params=pltpu.CompilerParams(vmem_limit_bytes=VMEM_BYTES),
        cost_estimate=pl.CostEstimate(flops=flops, bytes_accessed=moved, transcendentals=0),
    )(*args, *after)


def out(shape, dtype):
    return jax.ShapeDtypeStruct(shape, dtype)


def near_body(parts, *refs):
    sums = refs[0][...]
    for k in range(1, parts):
        sums = sums + refs[k][...]
    idx, own, other, own_params, other_params, near, stat = refs[parts:]
    cols = own.shape[2]
    mean = sums[0:4] * (1.0 / D)
    inv_std = lax.rsqrt(sums[4:8] * (1.0 / D) - mean * mean + norm_eps)
    table = to_columns(jnp.concatenate([mean, inv_std], axis=0))
    stat[...] = table
    at = idx[0]
    for which, (src, affine) in enumerate(
        ((own, own_params), (other, other_params))
    ):
        place = pl.multiple_of((at if which == 0 else 1 - at) * cols, LANES)
        for s in range(4):
            centred = (src[s].astype(f32) - table[:, s : s + 1]) * table[:, 4 + s : 5 + s]
            value = centred * affine[s : s + 1].astype(f32) + affine[4 + s : 5 + s].astype(f32)
            near[s, :, pl.ds(place, cols)] = value.astype(bf16)


def norm_back_body(parts, grad, arrived, own, stat, gain, *refs):
    sums = refs[0][...]
    for k in range(1, parts):
        sums = sums + refs[k][...]
    layer_grad, result, reduced = refs[parts:]
    table = stat[...]
    totals = to_columns(sums * (1.0 / D))
    for k in range(4):
        s = k
        value = grad[k] + arrived[k].astype(f32)
        inv_std = table[:, 4 + s : 5 + s]
        centred = (own[s].astype(f32) - table[:, s : s + 1]) * inv_std
        reduced[k : k + 1] = jnp.sum(value * centred, axis=0, keepdims=True)
        reduced[4 + k : 5 + k] = jnp.sum(value, axis=0, keepdims=True)
        back = inv_std * (
            value * gain[s : s + 1].astype(f32)
            - totals[:, k : k + 1]
            - centred * totals[:, 4 + k : 5 + k]
        )
        if s == 3:
            back = back + layer_grad[...]
        result[k] = back.astype(bf16)


def turn(x, tables, direction):
    cosine, low_sine, high_sine = tables
    half = ROT // 2
    return (
        x * cosine
        + direction * (jnp.roll(x, -half, axis=1) * low_sine + jnp.roll(x, half, axis=1) * high_sine)
    )


def rotary_tables(length):
    positions = lax.iota(f32, length)
    freqs = jnp.exp(lax.iota(f32, ROT // 2) * (-2.0 * math.log(10000.0) / ROT))
    angles = positions[:, None] * freqs[None, :]
    cosine = jnp.cos(angles)
    sine = jnp.sin(angles)
    zero = jnp.zeros((length, ROT // 2), f32)
    rest = jnp.zeros((length, HD - ROT), f32)
    return (
        jnp.concatenate([cosine, cosine, rest + 1.0], axis=1),
        jnp.concatenate([-sine, zero, rest], axis=1),
        jnp.concatenate([zero, sine, rest], axis=1),
    )


def probabilities(query, key, scale):
    scores = contract_cols(query, key) * scale
    rows = lax.broadcasted_iota(jnp.int32, scores.shape, 0)
    scores = jnp.where(lane_ids(scores.shape) <= rows, scores, -1e30)
    top = jnp.max(scores, axis=1, keepdims=True)
    log_total = top + jnp.log(jnp.sum(jnp.exp(scores - top), axis=1, keepdims=True))
    return jnp.exp(scores - log_total)


def forward_body(scale, arrived, own, qkv_bias, up_bias, cosine, low_sine, high_sine, qkv, pre, features):
    tables = (cosine[...], low_sine[...], high_sine[...])
    cols, width = qkv.shape[2], pre.shape[1]
    for h in range(cols // HD):
        parts = []
        for i in range(3):
            at = slice(i * cols + h * HD, i * cols + (h + 1) * HD)
            bias = qkv_bias[i : i + 1, h * HD : (h + 1) * HD].astype(f32)
            value = arrived[:, at].astype(f32) + own[:, at] + bias
            if i < 2:
                value = turn(value, tables, 1.0)
            value = value.astype(bf16)
            qkv[i, :, h * HD : (h + 1) * HD] = value
            parts.append(value)
        probs = probabilities(parts[0], parts[1], scale).astype(bf16)
        features[:, width + h * HD : width + (h + 1) * HD] = plain_dot(probs, parts[2]).astype(bf16)
    value = arrived[:, 3 * cols :].astype(f32) + own[:, 3 * cols :] + up_bias[...].astype(f32)
    pre[...] = value
    features[:, :width] = gelu_exact(value).astype(bf16)


def backward_body(scale, arrived, own, qkv, pre, cosine, low_sine, high_sine, grads, qkv_rows, up_rows):
    tables = (cosine[...], low_sine[...], high_sine[...])
    cols, width = qkv.shape[2], pre.shape[1]
    for h in range(cols // HD):
        at = slice(h * HD, (h + 1) * HD)
        query, key, value = qkv[0, :, at], qkv[1, :, at], qkv[2, :, at]
        place = slice(width + h * HD, width + (h + 1) * HD)
        out_grad = (own[:, place] + arrived[:, place].astype(f32)).astype(bf16)
        probs = probabilities(query, key, scale)
        value_grad = contract_rows(probs.astype(bf16), out_grad)
        prob_grad = contract_cols(out_grad, value)
        row_dot = jnp.sum(probs * prob_grad, axis=1, keepdims=True)
        score_grad = (probs * (prob_grad - row_dot)).astype(bf16)
        query_grad = turn(plain_dot(score_grad, key) * scale, tables, -1.0)
        key_grad = turn(contract_rows(score_grad, query) * scale, tables, -1.0)
        for i, grad in enumerate((query_grad, key_grad, value_grad)):
            low = grad.astype(bf16)
            grads[:, i * cols + h * HD : i * cols + (h + 1) * HD] = low
            qkv_rows[i : i + 1, at] = jnp.sum(low.astype(f32), axis=0, keepdims=True)
    qkv_rows[3:8] = jnp.zeros((5, cols), f32)
    total = arrived[:, :width].astype(f32) + own[:, :width]
    low = (total * gelu_slope(pre[...])).astype(bf16)
    grads[:, 3 * cols :] = low
    for t in range(8):
        if t < width // cols:
            part = low[:, t * cols : (t + 1) * cols].astype(f32)
            up_rows[t : t + 1] = jnp.sum(part, axis=0, keepdims=True)
        else:
            up_rows[t : t + 1] = jnp.zeros((1, cols), f32)


def fold(value):
    total = value[:, :LANES]
    for k in range(1, value.shape[1] // LANES):
        total = total + value[:, k * LANES : (k + 1) * LANES]
    return total


def prior_body(grad_out, prior, result, held):
    def group(r, carry):
        rows = pl.ds(pl.multiple_of(r * ROWS, ROWS), ROWS)
        grads = [grad_out[s, rows, :].astype(f32) for s in range(4)]
        lanes = lane_ids((ROWS, LANES))
        packed = jnp.zeros((ROWS, LANES), f32)
        for j in range(STACK - 1):
            value = prior[j, rows, :].astype(f32)
            for s in range(4):
                column = jnp.sum(fold(grads[s] * value), axis=1, keepdims=True)
                packed = jnp.where(lanes == s * STACK + j, column, packed)
        held[rows, :] = packed
        return carry

    lax.fori_loop(0, held.shape[0] // ROWS, group, 0)
    result[...] = held[...].T[:64]


def prior_products(streams_grad, prior, after=()):
    length, cols = prior.shape[1:]
    block = min(length, LANES)

    def kernel(grad_ref, prior_ref, *refs):
        prior_body(grad_ref, prior_ref, *refs[len(after) :])

    return pl.pallas_call(
        kernel,
        grid=(length // block,),
        out_shape=out((64, length), f32),
        in_specs=[
            pl.BlockSpec((4, block, cols), lambda t: (0, t, 0)),
            pl.BlockSpec((STACK - 1, block, cols), lambda t: (0, t, 0)),
        ]
        + waits(after),
        out_specs=pl.BlockSpec((64, block), lambda t: (0, t)),
        scratch_shapes=[pltpu.VMEM((block, LANES), f32)],
        compiler_params=pltpu.CompilerParams(vmem_limit_bytes=VMEM_BYTES),
        cost_estimate=pl.CostEstimate(
            flops=20_000_000, bytes_accessed=2 * length * cols * 16, transcendentals=0
        ),
    )(streams_grad, prior, *after)


def mix_first_body(
    parts, streams, own, *refs
):
    arrived = refs[:parts]
    branch_bias, gain, mix_in, grad_out, layer_out, packed_out = refs[parts:]
    value = own[...]
    for item in arrived:
        value = value + item[...].astype(f32)
    value = streams[3].astype(f32) + (value + branch_bias[...].astype(f32))
    layer_out[...] = value
    packed = plain_dot(value * gain[...].astype(f32), mix_in[...], high)
    lanes = lane_ids(packed.shape)
    energy = jnp.sum(fold(value * value), axis=1, keepdims=True)
    packed = jnp.where(lanes == MIXH, energy, packed)
    for s in range(4):
        column = jnp.sum(fold(grad_out[s].astype(f32) * value), axis=1, keepdims=True)
        packed = jnp.where(lanes == MIXH + 1 + s, column, packed)
    packed_out[...] = packed.T[:64]


def mix_tables(packed, prior_coef, mix_in, mix_out, mix_static, gain, value, grad_out):
    lanes = lane_ids(packed.shape)
    energy = packed[:, MIXH : MIXH + 1]
    rms = lax.rsqrt(energy * (1.0 / D) + rms_eps)
    logit_sum = jnp.where(lanes < MIXH, packed, 0.0)
    logits = logit_sum * rms
    mix_hidden = gelu_exact(logits)
    coef = plain_dot(mix_hidden, mix_out, high) + mix_static
    coef_grad = prior_coef
    for s in range(4):
        column = packed[:, MIXH + 1 + s : MIXH + 2 + s]
        coef_grad = jnp.where(lanes == s * STACK + STACK - 1, column, coef_grad)
    logit_grad = contract_cols(coef_grad, mix_out, high) * gelu_slope(logits)
    sum_grad = logit_grad * rms
    rms_grad = jnp.sum(logit_grad * logit_sum, axis=1, keepdims=True)
    energy_grad = rms_grad * rms * rms * rms * (-1.0 / D)
    scaled_grad = contract_cols(sum_grad, mix_in, high)
    total = scaled_grad * gain + energy_grad * value
    for s in range(4):
        at = s * STACK + STACK - 1
        total = total + coef[:, at : at + 1] * grad_out[s].astype(f32)
    return coef, coef_grad, mix_hidden, sum_grad, scaled_grad, total


def mix_second_body(parts, me, *refs):
    held = refs[-1]
    for k in range(parts):
        held[lax.rem(me[0] + (parts - k), parts)] = refs[k][...]
    sums = held[0]
    for k in range(1, parts):
        sums = sums + held[k]
    (prior_coef, layer_out, grad_out, gain, mix_in, mix_out, mix_static,
     branch_grad, packed) = refs[parts:-1]
    packed[...] = sums
    total = mix_tables(
        to_columns(sums), to_columns(prior_coef[...]), mix_in[...], mix_out[...], mix_static[...],
        gain[...].astype(f32), layer_out[...], grad_out,
    )[-1]
    branch_grad[...] = total.astype(bf16)


def mix_third_body(packed, prior_coef, mix_in, mix_out, mix_static, layer_out, prior, grad_out, gain,
                   streams_out, prior_grad, weight_grads, token, layer_grad, reduced, held):
    block, cols = layer_out.shape
    step = pl.program_id(0)
    coef, coef_grad, mix_hidden, sum_grad, scaled_grad, total = mix_tables(
        to_columns(packed[...]), to_columns(prior_coef[...]), mix_in[...], mix_out[...],
        mix_static[...], gain[...].astype(f32), layer_out[...], grad_out,
    )
    held[...] = coef
    layer_grad[...] = total

    @pl.when(step == 0)
    def _():
        weight_grads[...] = jnp.zeros(weight_grads.shape, f32)
        reduced[...] = jnp.zeros(reduced.shape, f32)
        mark(token)

    reduced[0:1] += jnp.sum(scaled_grad * layer_out[...], axis=0, keepdims=True)
    reduced[1:2] += jnp.sum(total.astype(bf16).astype(f32), axis=0, keepdims=True)
    scaled = layer_out[...] * gain[...].astype(f32)
    weight_grads[:cols] += contract_rows(scaled, sum_grad, high)
    chosen = jnp.where(lane_ids((block, LANES)) == MIXH, 1.0, mix_hidden)
    weight_grads[cols:] += contract_rows(chosen, coef_grad, high)[: weight_grads.shape[0] - cols]

    def group(r, carry):
        rows = pl.ds(pl.multiple_of(r * ROWS, ROWS), ROWS)
        coef = held[rows, :]
        grads = [grad_out[s, rows, :].astype(f32) for s in range(4)]
        value = layer_out[rows, :]
        totals = []
        for s in range(4):
            at = s * STACK + STACK - 1
            totals.append(coef[:, at : at + 1] * value)
        for j in range(STACK - 1):
            value = prior[j, rows, :].astype(f32)
            back = None
            for s in range(4):
                at = s * STACK + j
                column = jnp.broadcast_to(coef[:, at : at + 1], (ROWS, cols))
                totals[s] = totals[s] + column * value
                term = column * grads[s]
                back = term if back is None else back + term
            prior_grad[j, rows, :] = back.astype(bf16)
        for s in range(4):
            streams_out[s, rows, :] = totals[s].astype(bf16)
        return carry

    lax.fori_loop(0, block // ROWS, group, 0)


def mix_third(packed, prior_coef, mix_in, mix_out, mix_static, layer_out, prior, streams_grad, gain, after):
    length, cols = layer_out.shape
    block = min(length, LANES)
    tokens = lambda count: pl.BlockSpec((count, block, cols), lambda t: (0, t, 0))
    whole = lambda *shape: pl.BlockSpec(shape, lambda t: (0,) * len(shape))

    def kernel(*refs):
        mix_third_body(*refs[:9], *refs[9 + len(after) :])

    return pl.pallas_call(
        kernel,
        grid=(length // block,),
        out_shape=[
            out((4, length, cols), bf16),
            out((STACK - 1, length, cols), bf16),
            out((cols + 56, LANES), f32),
            TOKEN,
            out((length, cols), f32),
            out((8, cols), f32),
        ],
        in_specs=[
            pl.BlockSpec((64, block), lambda t: (0, t)),
            pl.BlockSpec((64, block), lambda t: (0, t)),
            whole(cols, LANES),
            whole(LANES, LANES),
            whole(1, LANES),
            pl.BlockSpec((block, cols), lambda t: (t, 0)),
            tokens(STACK - 1),
            tokens(4),
            whole(1, cols),
        ]
        + waits(after),
        out_specs=[
            tokens(4),
            tokens(STACK - 1),
            whole(cols + 56, LANES),
            whole(8, LANES),
            pl.BlockSpec((block, cols), lambda t: (t, 0)),
            whole(8, cols),
        ],
        scratch_shapes=[pltpu.VMEM((block, LANES), f32)],
        compiler_params=PARAMS,
        cost_estimate=pl.CostEstimate(
            flops=30_000_000, bytes_accessed=2 * length * cols * 34, transcendentals=0
        ),
    )(packed, prior_coef, mix_in, mix_out, mix_static, layer_out, prior, streams_grad, gain, *after)


def cost(flops, moved):
    return pl.CostEstimate(flops=flops, bytes_accessed=moved, transcendentals=0)


ANY = pl.BlockSpec(memory_space=pl.ANY)
PARAMS = pltpu.CompilerParams(vmem_limit_bytes=VMEM_BYTES)
WIDE_PARAMS = pltpu.CompilerParams(vmem_limit_bytes=60 * 1024 * 1024)


def prefetched(kernel, scalars, grid, in_specs, out_specs, out_shape, args, estimate, aliases=None):
    return pl.pallas_call(
        kernel,
        grid_spec=pltpu.PrefetchScalarGridSpec(
            num_scalar_prefetch=len(scalars), grid=grid, in_specs=in_specs, out_specs=out_specs
        ),
        out_shape=out_shape,
        input_output_aliases=aliases or {},
        compiler_params=PARAMS,
        cost_estimate=estimate,
    )(*scalars, *args)


def fetch(pairs, sems):
    copies = [pltpu.make_async_copy(src, dst, sems.at[k]) for k, (src, dst) in enumerate(pairs)]
    for item in copies:
        item.start()
    return copies


def spread(block, near, w_qkv, w_up, up_cols, dtype, after):
    _, length, depth = near.shape
    cols = depth // 2
    width = 3 * cols + up_cols

    def kernel(b, near_ref, qkv_ref, up_ref, *refs):
        result, left, qkv, up, sems = refs[len(after) :]
        pairs = []
        for s in range(4):
            pairs.append((near_ref.at[s], left.at[s]))
            if s < 3:
                place = pl.multiple_of(b[0] * cols, LANES)
                pairs.append((qkv_ref.at[s, :, pl.ds(place, cols)], qkv.at[s]))
            else:
                place = pl.multiple_of(b[0] * up_cols, LANES)
                pairs.append((up_ref.at[:, pl.ds(place, up_cols)], up))
        copies = fetch(pairs, sems)
        for s in range(4):
            copies[2 * s].wait()
            copies[2 * s + 1].wait()
            if s < 3:
                result[:, s * cols : (s + 1) * cols] = plain_dot(left[s], qkv[s]).astype(dtype)
            else:
                result[:, 3 * cols :] = plain_dot(left[s], up[...]).astype(dtype)

    vmem = pl.BlockSpec(memory_space=pltpu.VMEM)
    return pl.pallas_call(
        kernel,
        out_shape=out((length, width), dtype),
        in_specs=[pl.BlockSpec(memory_space=pltpu.SMEM)] + [ANY] * 3 + waits(after),
        out_specs=vmem,
        scratch_shapes=[
            pltpu.VMEM((4, length, depth), bf16),
            pltpu.VMEM((3, depth, cols), bf16),
            pltpu.VMEM((depth, up_cols), bf16),
            pltpu.SemaphoreType.DMA((8,)),
        ],
        compiler_params=PARAMS if after else WIDE_PARAMS,
        cost_estimate=cost(2 * length * depth * width, 2 * depth * width + 4 * length * width),
    )(block, near, w_qkv, w_up, *after)


def spread_back(idx, block, own, other, w_down, w_out, up_cols, dtype, after):
    length, cols = own.shape

    def kernel(b, idx_ref, own_ref, other_ref, down_ref, out_ref, *refs):
        result, pair, down, outer, sems = refs[len(after) :]
        copies = fetch(
            [
                (down_ref.at[pl.ds(pl.multiple_of(b[0] * up_cols, up_cols), up_cols)], down),
                (out_ref.at[pl.ds(pl.multiple_of(b[0] * cols, cols), cols)], outer),
            ],
            sems,
        )
        pair[:, pl.ds(pl.multiple_of(idx_ref[0] * cols, LANES), cols)] = own_ref[...]
        pair[:, pl.ds(pl.multiple_of((1 - idx_ref[0]) * cols, LANES), cols)] = other_ref[...]
        copies[0].wait()
        result[:, :up_cols] = contract_cols(pair[...], down[...]).astype(dtype)
        copies[1].wait()
        result[:, up_cols:] = contract_cols(pair[...], outer[...]).astype(dtype)

    depth = up_cols + cols
    smem = pl.BlockSpec(memory_space=pltpu.SMEM)
    vmem = pl.BlockSpec(memory_space=pltpu.VMEM)
    return pl.pallas_call(
        kernel,
        out_shape=out((length, depth), dtype),
        in_specs=[smem, smem, vmem, vmem, ANY, ANY] + waits(after),
        out_specs=vmem,
        scratch_shapes=[
            pltpu.VMEM((length, 2 * cols), bf16),
            pltpu.VMEM((up_cols, 2 * cols), bf16),
            pltpu.VMEM((cols, 2 * cols), bf16),
            pltpu.SemaphoreType.DMA((2,)),
        ],
        compiler_params=PARAMS,
        cost_estimate=cost(4 * length * depth * cols, 4 * depth * cols + 4 * length * depth),
    )(block, idx, own, other, w_down, w_out, *after)


def add_body(arrived, term, result):
    result[...] = (arrived[...].astype(f32) + term[...]).astype(bf16)


def branch_step(block, item, so_far, w_down, w_out, up_cols, after):
    length, depth = item.shape
    cols = depth - up_cols
    wide_cols = w_down.shape[1]
    earlier = [] if so_far is None else [so_far]
    whole = pl.BlockSpec((length, wide_cols), lambda i, b: (0, 0))

    def kernel(b, item_ref, down_ref, out_ref, *refs):
        value = plain_dot(item_ref[:, :up_cols], down_ref[...]) + plain_dot(
            item_ref[:, up_cols:], out_ref[...]
        )
        refs[-2][...] = refs[0][...] + value if earlier else value
        mark(refs[-1])

    return prefetched(
        kernel,
        [block],
        (1,),
        [
            pl.BlockSpec((length, depth), lambda i, b: (0, 0)),
            pl.BlockSpec((up_cols, wide_cols), lambda i, b: (b[0], 0)),
            pl.BlockSpec((cols, wide_cols), lambda i, b: (b[0], 0)),
        ]
        + [whole] * len(earlier)
        + waits(after),
        [whole, pl.BlockSpec((8, LANES), lambda i, b: (0, 0))],
        [out((length, wide_cols), f32), TOKEN],
        [item, w_down, w_out, *earlier, *after],
        cost(2 * length * depth * wide_cols, 2 * depth * wide_cols),
    )


def halves_body(idx, value, theirs, mine):
    cols = mine.shape[1]
    mine[...] = value[:, pl.ds(pl.multiple_of(idx[0] * cols, LANES), cols)]
    theirs[...] = value[:, pl.ds(pl.multiple_of((1 - idx[0]) * cols, LANES), cols)].astype(bf16)


def near_step(block, item, so_far, w_qkv, w_up, cols, after):
    length = item.shape[0]
    depth = w_up.shape[0]
    up_cols = item.shape[1] - 3 * cols
    earlier = [] if so_far is None else [so_far]
    one = pl.BlockSpec((1, length, depth), lambda s, b: (s, 0, 0))

    def kernel(b, item_ref, qkv_ref, up_ref, *refs):
        step = pl.program_id(0)
        base = refs[0][0] if earlier else 0.0

        @pl.when(step < 3)
        def _():
            part = item_ref[:, pl.ds(pl.multiple_of(step * cols, LANES), cols)]
            refs[-2][0] = contract_cols(part, qkv_ref[0]) + base

        @pl.when(step == 3)
        def _():
            refs[-2][0] = contract_cols(item_ref[:, 3 * cols :], up_ref[...]) + base
            mark(refs[-1])

    return prefetched(
        kernel,
        [block],
        (4,),
        [
            pl.BlockSpec(item.shape, lambda s, b: (0, 0)),
            pl.BlockSpec((1, depth, cols), lambda s, b: (jnp.minimum(s, 2), 0, b[0])),
            pl.BlockSpec((depth, up_cols), lambda s, b: (0, b[0])),
        ]
        + [one] * len(earlier)
        + waits(after),
        [one, pl.BlockSpec((8, LANES), lambda s, b: (0, 0))],
        [out((4, length, depth), f32), TOKEN],
        [item, w_qkv, w_up, *earlier, *after],
        cost(2 * item.size * depth, 2 * item.size * depth // length + 32 * length * depth),
    )


def near_last(idx, block, item, so_far, w_qkv, w_up, own, other, stat, gain_own, gain_other):
    length = item.shape[0]
    depth = w_up.shape[0]
    cols = depth // 2
    up_cols = item.shape[1] - 3 * cols

    def kernel(b, x, item_ref, qkv_ref, up_ref, base, own_ref, other_ref, stat_ref, gain_o, gain_f,
               theirs, mine, stats, value, packed):
        step = pl.program_id(0)

        @pl.when(step < 3)
        def _():
            part = item_ref[:, pl.ds(pl.multiple_of(step * cols, LANES), cols)]
            value[...] = contract_cols(part, qkv_ref[0]) + base[0]

        @pl.when(step == 3)
        def _():
            value[...] = contract_cols(item_ref[:, 3 * cols :], up_ref[...]) + base[0]

        table = stat_ref[...]
        lanes = lane_ids(table.shape)
        mean = jnp.sum(jnp.where(lanes == step, table, 0.0), axis=1, keepdims=True)
        inv_std = jnp.sum(jnp.where(lanes == step + 4, table, 0.0), axis=1, keepdims=True)
        total = jnp.zeros((length, LANES), f32)
        cross = jnp.zeros((length, LANES), f32)
        for which, (src, gain) in enumerate(((own_ref, gain_o), (other_ref, gain_f))):
            place = pl.multiple_of((x[0] if which == 0 else 1 - x[0]) * cols, LANES)
            part = value[:, pl.ds(place, cols)]
            if which == 0:
                mine[0] = part
            else:
                theirs[0] = part.astype(bf16)
            scaled = part * gain[0].astype(f32)
            total = total + fold(scaled)
            cross = cross + fold(scaled * ((src[0].astype(f32) - mean) * inv_std))
        kept = jnp.where(step == 0, 0.0, packed[...])
        kept = jnp.where(lanes == step, jnp.sum(total, axis=1, keepdims=True), kept)
        kept = jnp.where(lanes == step + 4, jnp.sum(cross, axis=1, keepdims=True), kept)
        packed[...] = kept

        @pl.when(step == 3)
        def _():
            stats[...] = packed[...].T[:8]

    half = pl.BlockSpec((1, length, cols), lambda s, b, x: (s, 0, 0))
    row = pl.BlockSpec((1, 1, cols), lambda s, b, x: (s, 0, 0))
    return pl.pallas_call(
        kernel,
        grid_spec=pltpu.PrefetchScalarGridSpec(
            num_scalar_prefetch=2,
            grid=(4,),
            in_specs=[
                pl.BlockSpec(item.shape, lambda s, b, x: (0, 0)),
                pl.BlockSpec((1, depth, cols), lambda s, b, x: (jnp.minimum(s, 2), 0, b[0])),
                pl.BlockSpec((depth, up_cols), lambda s, b, x: (0, b[0])),
                pl.BlockSpec((1, length, depth), lambda s, b, x: (s, 0, 0)),
                half,
                half,
                pl.BlockSpec((length, LANES), lambda s, b, x: (0, 0)),
                row,
                row,
            ],
            out_specs=[half, half, pl.BlockSpec((8, length), lambda s, b, x: (0, 0))],
            scratch_shapes=[pltpu.VMEM((length, depth), f32), pltpu.VMEM((length, LANES), f32)],
        ),
        out_shape=[
            out((4, length, cols), bf16), out((4, length, cols), f32), out((8, length), f32),
        ],
        compiler_params=PARAMS,
        cost_estimate=cost(2 * item.size * depth, 2 * item.size * depth // length + 24 * length * depth),
    )(block, idx, item, w_qkv, w_up, so_far, own, other, stat, gain_own[:, None], gain_other[:, None])


def near_weights(order, block, near, parts, shapes, before, after=()):
    n_dp, _, length, depth = near.shape
    cols = depth // 2
    up_cols = parts[0].shape[1] - 3 * cols

    def kernel(order_ref, b, near_ref, *refs):
        qkv_grad, up_grad, done = refs[-3:]
        step = pl.program_id(0)
        left = jnp.concatenate([near_ref[order_ref[p], 0] for p in range(n_dp)], axis=0)

        @pl.when(step < 3)
        def _():
            place = pl.multiple_of(step * cols, LANES)
            right = jnp.concatenate([item[:, pl.ds(place, cols)] for item in refs[:n_dp]], axis=0)
            qkv_grad[0] = contract_rows(left, right)

        @pl.when(step == 3)
        def _():
            right = jnp.concatenate([item[:, 3 * cols :] for item in refs[:n_dp]], axis=0)
            up_grad[...] = contract_rows(left, right)
            done[...] = jnp.zeros(done.shape, f32)

    return prefetched(
        kernel,
        [order, block],
        (4,),
        [pl.BlockSpec((n_dp, 1, length, depth), lambda i, o, b: (0, i, 0, 0))]
        + [pl.BlockSpec(parts[0].shape, lambda i, o, b: (0, 0))] * n_dp
        + [ANY] * len(before)
        + waits(after),
        [
            pl.BlockSpec((1, depth, cols), lambda i, o, b: (jnp.minimum(i, 2), 0, b[0])),
            pl.BlockSpec((depth, up_cols), lambda i, o, b: (0, b[0])),
            pl.BlockSpec((8, LANES), lambda i, o, b: (0, 0)),
        ],
        [out(shape, f32) for shape in (*shapes, (8, LANES))],
        [near, *parts, *before, *after],
        cost(1000, 1000),
        {3 + n_dp + k: k for k in range(len(before))},
    )


def branch_weights(order, block, features, parts, up_cols, shapes, before):
    n_dp, length, depth = features.shape
    cols = depth - up_cols
    width = parts[0].shape[1]

    def kernel(order_ref, b, features_ref, *refs):
        left = jnp.concatenate([features_ref[order_ref[p]] for p in range(n_dp)], axis=0)
        right = jnp.concatenate([item[...] for item in refs[:n_dp]], axis=0)
        refs[-3][...] = contract_rows(left[:, :up_cols], right)
        refs[-2][...] = contract_rows(left[:, up_cols:], right)
        refs[-1][...] = jnp.zeros(refs[-1].shape, f32)

    return prefetched(
        kernel,
        [order, block],
        (1,),
        [pl.BlockSpec(features.shape, lambda i, o, b: (0, 0, 0))]
        + [pl.BlockSpec((length, width), lambda i, o, b: (0, 0))] * n_dp
        + [ANY] * len(before),
        [
            pl.BlockSpec((up_cols, width), lambda i, o, b: (b[0], 0)),
            pl.BlockSpec((cols, width), lambda i, o, b: (b[0], 0)),
            pl.BlockSpec((8, LANES), lambda i, o, b: (0, 0)),
        ],
        [out(shape, f32) for shape in (*shapes, (8, LANES))],
        [features, *parts, *before],
        cost(2 * features.size * width, 2 * features.size + 4 * depth * width),
        {3 + n_dp + k: k for k in range(len(before))},
    )


def gate(value, after):
    def kernel(*refs):
        pass

    return pl.pallas_call(
        kernel,
        out_shape=out(value.shape, value.dtype),
        in_specs=[ANY] + waits(after),
        out_specs=ANY,
        input_output_aliases={0: 0},
        compiler_params=pltpu.CompilerParams(
            has_side_effects=True, vmem_limit_bytes=VMEM_BYTES
        ),
    )(value, *after)


TOKEN = out((8, LANES), f32)


def mark(ref):
    ref[...] = jnp.zeros(ref.shape, f32)


def finish_body(rows, far, qkv_bias, up_bias, branch_bias, mix_gain, gain, shift_grad):
    total = rows[...] + far[...]
    qkv_bias[...] = total[0:3]
    mix_gain[...] = total[8:9]
    branch_bias[...] = total[9:10]
    up_bias[...] = total[16 : 16 + up_bias.shape[0]]
    gain[...] = total[24:28]
    shift_grad[...] = total[28:32]


def add_rows_body(*refs):
    total = refs[0][...]
    for item in refs[1:-1]:
        total = total + item[...]
    refs[-1][...] = total


def stats_body(streams, sums):
    length = streams.shape[1]
    lanes = lane_ids((length, LANES))
    packed = jnp.zeros((length, LANES), f32)
    for s in range(4):
        value = streams[s].astype(f32)
        packed = jnp.where(lanes == s, jnp.sum(fold(value), axis=1, keepdims=True), packed)
        packed = jnp.where(
            lanes == 4 + s, jnp.sum(fold(value * value), axis=1, keepdims=True), packed
        )
    sums[...] = packed.T[:8]


def build(n_dp, n_wide, n_narrow):
    def shift(value, axis, size, step):
        return lax.ppermute(value, axis, [(i, (i + step) % size) for i in range(size)])

    def swap(value, axis, size, bit):
        return lax.ppermute(value, axis, [(i, i ^ bit) for i in range(size)])

    def butterfly(value, axis, size):
        bit = 1
        while bit < size:
            value = value + swap(value, axis, size, bit)
            bit *= 2
        return value

    def narrow_swap(value):
        return swap(value, "narrow", n_narrow, 1)

    def model_parts(value):
        value = value + narrow_swap(value)
        return [value] + [shift(value, "wide", n_wide, k) for k in range(1, n_wide)]

    def model_butterfly(value):
        return butterfly(butterfly(value, "narrow", n_narrow), "wide", n_wide)

    def dp_sum(value):
        return butterfly(value, "dp", n_dp)

    def dp_gather(value):
        held = [value]
        far = value
        for _ in range(n_dp // CORES - 1):
            far = shift(far, "dp", n_dp, CORES)
            held.append(far)
        return held + [swap(item, "dp", n_dp, 1) for item in held]

    def across(value):
        held = [value]
        for _ in range(n_dp // CORES - 1):
            held.append(shift(held[-1], "dp", n_dp, CORES))
        return held

    def dp_order():
        me = lax.axis_index("dp")
        steps = [lax.rem(me + n_dp - CORES * k, n_dp) for k in range(n_dp // CORES)]
        return steps + [item ^ 1 for item in steps]

    def reduce_ring(product, hold):
        me = lax.axis_index("wide").astype(jnp.int32)
        block = lambda back: lax.rem(me + (n_wide - back), n_wide)[None]
        total = product(block(1), bf16, [])
        sent = [total]
        for at in range(n_wide - 1):
            arrived = shift(total, "wide", n_wide, 1)
            term = product(block(at + 2) if at + 2 < n_wide else me[None], f32, [total])
            if at < n_wide - 2:
                (total,) = call(
                    add_body, [out(total.shape, bf16)], [arrived, term], after=hold(at, total)
                )
                sent.append(total)
        return arrived, term, sent

    def per_device(
        streams, prior, streams_grad, w_qkv, qkv_bias, w_out, w_up, up_bias, w_down, branch_bias,
        norm_gain, norm_bias, mix_gain, mix_in, mix_out, mix_static,
    ):
        length = streams.shape[1]
        cols = streams.shape[2]
        scale = 1.0 / math.sqrt(HD)
        up_cols = w_up.shape[1] // n_wide
        tiles = up_cols // cols
        depth = up_cols + cols
        idx = lax.axis_index("narrow").astype(jnp.int32)[None]
        me = lax.axis_index("wide").astype(jnp.int32)
        order = jnp.stack(dp_order()).astype(jnp.int32)
        params = jnp.concatenate([norm_gain, norm_bias], axis=0)
        other_params = narrow_swap(params)
        gain_other = other_params[:4]
        other = narrow_swap(streams)
        (sums,) = call(stats_body, [out((8, length), f32)], [streams])
        (wide_sums,) = call(
            add_rows_body,
            [out((8, length), f32)],
            [sums] + [shift(sums, "wide", n_wide, k) for k in range(1, n_wide)],
            after=[other],
        )
        stat_parts = [wide_sums, narrow_swap(wide_sums)]
        near, stat = call(
            functools.partial(near_body, len(stat_parts)),
            [out((4, length, 2 * cols), bf16), out((length, LANES), f32)],
            [*stat_parts, idx, streams, other, params, other_params],
            scalars={len(stat_parts)},
        )
        tables = rotary_tables(length)

        near_all = lax.all_gather(near, "dp", axis=0, tiled=False)
        near_token = near_all[0, 0, :8, :LANES]
        tables = rotary_tables(length)
        prior_rows = prior_products(streams_grad, prior)
        prior_sum = lax.psum(prior_rows, ("wide", "narrow"))
        arrived, own, sent = reduce_ring(
            lambda block, dtype, after: spread(
                block, near, w_qkv, w_up, up_cols, dtype, after
            ),
            lambda at, total: [],
        )
        qkv, up_pre, features = call(
            functools.partial(forward_body, scale),
            [
                out((3, length, cols), bf16),
                out((length, up_cols), f32),
                out((length, up_cols + cols), bf16),
            ],
            [arrived, own, qkv_bias, up_bias[None], *tables],
            flops=8 * length * length * cols,
        )
        blocks = [lax.rem(me + (n_wide - k), n_wide)[None] for k in range(n_wide)]
        item, branch_part, features_all = features, None, []
        for k in range(n_wide):
            branch_part, token = branch_step(
                blocks[k], item, branch_part, w_down, w_out, up_cols, []
            )
            features_all.append(lax.all_gather(item, "dp", axis=0, tiled=False))
            if k < n_wide - 1:
                item = gate(shift(item, "wide", n_wide, 1), [token])
        theirs, branch_own = call(
            halves_body,
            [out((length, cols), bf16), out((length, cols), f32)],
            [idx, branch_part],
            scalars={0},
        )
        branch_arrived = narrow_swap(theirs)
        mix_in_pad = jnp.pad(mix_in.astype(f32), ((0, 0), (0, LANES - MIXH)))
        mix_out_pad = jnp.pad(mix_out.astype(f32), ((0, LANES - MIXH), (0, LANES - MIXH)))
        static_pad = jnp.pad(mix_static.astype(f32)[None], ((0, 0), (0, LANES - MIXH)))
        gain_row = mix_gain[None]
        layer_out, packed = call(
            functools.partial(mix_first_body, 1),
            [out((length, cols), f32), out((64, length), f32)],
            [streams, branch_own, branch_arrived, branch_bias[None], gain_row, mix_in_pad, streams_grad],
            after=[near_token],
        )
        packed_parts = model_parts(packed)
        branch_grad, packed_sum = call(
            functools.partial(mix_second_body, n_wide),
            [
                out((length, cols), bf16),
                out((64, length), f32),
            ],
            [me[None], *packed_parts, prior_sum, layer_out, streams_grad, gain_row, mix_in_pad,
             mix_out_pad, static_pad],
            scalars={0},
            scratch=[pltpu.VMEM((n_wide, 64, length), f32)],
        )
        branch_other = narrow_swap(branch_grad)
        mixer_outs, mixer_sums, branch_grads, tokens = [], [], [], []

        def branch_side(at, total):
            if at == 0:
                mixer_outs.extend(
                    mix_third(
                        packed_sum, prior_sum, mix_in_pad, mix_out_pad, static_pad, layer_out, prior,
                        streams_grad, gain_row, [total],
                    )
                )
                first = lax.axis_index("narrow") == 0
                pair = [gate(branch_grad, [total]), branch_other]
                near = jnp.concatenate(
                    [jnp.where(first, pair[0], pair[1]), jnp.where(first, pair[1], pair[0])], axis=1
                )
                branch_all = dp_gather(near)
                for k, block in enumerate(blocks):
                    *grads, token = branch_weights(
                        order, block, features_all[k], branch_all, up_cols,
                        (w_down.shape, w_out.shape), branch_grads[-1] if branch_grads else [],
                    )
                    branch_grads.append(grads)
                    tokens.append(token)
                mixer_sums.append(dp_sum(mixer_outs[2]))
                return [mixer_outs[3]]
            return tokens[:1]

        arrived, own, sent = reduce_ring(
            lambda block, dtype, after: spread_back(
                idx, block, branch_grad, branch_other, w_down, w_out, up_cols, dtype, after
            ),
            lambda at, total: branch_side(at, total),
        )
        grads, qkv_rows, up_rows = call(
            functools.partial(backward_body, scale),
            [
                out((length, up_cols + 3 * cols), bf16),
                out((8, cols), f32),
                out((8, cols), f32),
            ],
            [arrived, own, qkv, up_pre, *tables],
            flops=14 * length * length * cols,
            after=tokens[:2] + [mixer_sums[0][:8]],
        )
        (mix_sums,) = mixer_sums
        item, near_grad, near_grads, held, mates = grads, None, [], [], []
        for k in range(n_wide):
            after = []
            if k < n_wide - 1:
                near_grad, token = near_step(blocks[k], item, near_grad, w_qkv, w_up, cols, [])
                after = [token, *(tokens[2:] if k == 0 else [])]
            else:
                theirs, mine, stats = near_last(
                    idx, blocks[k], item, near_grad, w_qkv, w_up, streams, other, stat, norm_gain,
                    gain_other,
                )
            held.append(across(item))
            if k:
                far = [gate(part, [item]) for part in held[k - 1][1:]]
                crossed = [held[k - 1][0], *far, mates[k - 1]]
                crossed = crossed + [swap(part, "dp", n_dp, 1) for part in far]
                *near_grads, token = near_weights(
                    order, blocks[k - 1], near_all, crossed, (w_qkv.shape, w_up.shape), near_grads
                )
                after.append(token)
            if k < n_wide - 1:
                mates.append(swap(item, "dp", n_dp, 1))
                after += [held[k][-1], mates[k]]
            else:
                (wide_sum,) = call(
                    add_rows_body,
                    [out((8, length), f32)],
                    [stats] + [shift(stats, "wide", n_wide, j) for j in range(1, n_wide)],
                    after=[token],
                )
                mates.append(swap(gate(item, [wide_sum]), "dp", n_dp, 1))
            if k < n_wide - 1:
                item = gate(shift(item, "wide", n_wide, 1), after)
        down_weight_grad, out_weight_grad = branch_grads[-1]
        streams_out, prior_grad, _, _, layer_grad, mix_rows = mixer_outs
        stat_parts = [wide_sum, narrow_swap(wide_sum)]
        streams_in_grad, near_rows = call(
            functools.partial(norm_back_body, len(stat_parts)),
            [out((4, length, cols), bf16), out((8, cols), f32)],
            [mine, narrow_swap(theirs), streams, stat, norm_gain, *stat_parts, layer_grad],
        )
        far = [gate(part, [near_rows]) for part in held[-1][1:]]
        crossed = [held[-1][0], *far, mates[-1]] + [swap(part, "dp", n_dp, 1) for part in far]
        *near_grads, last_token = near_weights(
            order, blocks[-1], near_all, crossed, (w_qkv.shape, w_up.shape), near_grads
        )
        qkv_weight_grad, up_weight_grad = near_grads
        rows = jnp.concatenate([qkv_rows, mix_rows, up_rows, near_rows], axis=0)
        bit = 1
        while 2 * bit < n_dp:
            rows = rows + swap(rows, "dp", n_dp, bit)
            bit *= 2
        qkv_bias_grad, up_bias_grad, branch_bias_grad, mix_gain_grad, gain_grad, shift_grad = call(
            finish_body,
            [out((3, cols), f32), out((tiles, cols), f32), out((1, cols), f32), out((1, cols), f32),
             out((4, cols), f32), out((4, cols), f32)],
            [rows, swap(rows, "dp", n_dp, bit)],
            after=[last_token],
        )
        return (
            streams_out, streams_in_grad, prior_grad, qkv_weight_grad, qkv_bias_grad, out_weight_grad,
            up_weight_grad, up_bias_grad.reshape(-1), down_weight_grad, branch_bias_grad[0], gain_grad,
            shift_grad, mix_gain_grad[0], mix_sums[:cols, :MIXH],
            mix_sums[cols : cols + MIXH, :MIXH], mix_sums[cols + MIXH, :MIXH],
        )

    return per_device


def solution(mesh):
    tokens = P(None, "dp", ("wide", "narrow"))
    outer = P(("wide", "narrow"))
    inner = P(None, ("wide", "narrow"))
    column = P(("narrow", "wide"))
    return jax.shard_map(
        build(mesh.shape["dp"], mesh.shape["wide"], mesh.shape["narrow"]),
        mesh=mesh,
        in_specs=(
            tokens, tokens, tokens, P(None, "wide", "narrow"), P(None, ("narrow", "wide")),
            P("narrow", "wide"), P("wide", "narrow"), column, P("narrow", "wide"), outer, inner,
            inner, outer, P(("wide", "narrow"), None), P(), P(),
        ),
        out_specs=(
            tokens, tokens, tokens, P(None, "wide", "narrow"), P(None, ("narrow", "wide")),
            P("narrow", "wide"), P("wide", "narrow"), column, P("narrow", "wide"), outer, inner,
            inner, outer, P(("wide", "narrow"), None), P(), P(),
        ),
        check_vma=False,
    )
```

```python
import functools
import math

import jax
import jax.numpy as jnp
from jax import lax
from jax.experimental import pallas as pl
from jax.experimental.pallas import tpu as pltpu
from jax.sharding import PartitionSpec as P

D = 2048
HD = 128
ROT = 32
MIXH = 52
STACK = 13
CORES = 2
LANES = 128
ROWS = 16

norm_eps = 1e-05
rms_eps = 1e-06

f32 = jnp.float32
bf16 = jnp.bfloat16
high = lax.Precision.HIGHEST
VMEM_BYTES = 48 * 1024 * 1024


def gelu_exact(inputs):
    return 0.5 * inputs * (1.0 + lax.erf(inputs * (1.0 / math.sqrt(2.0))))


def gelu_slope(inputs):
    normal_cdf = 0.5 * (1.0 + lax.erf(inputs * (1.0 / math.sqrt(2.0))))
    return normal_cdf + inputs * jnp.exp(-0.5 * inputs * inputs) * (1.0 / math.sqrt(2.0 * math.pi))


def dot(left, right, dims, precision=None):
    return lax.dot_general(
        left, right, (dims, ((), ())), precision=precision, preferred_element_type=f32
    )


def contract_rows(left, right, precision=None):
    return dot(left, right, ((0,), (0,)), precision)


def contract_cols(left, right, precision=None):
    return dot(left, right, ((1,), (1,)), precision)


def plain_dot(left, right, precision=None):
    return dot(left, right, ((1,), (0,)), precision)


def to_columns(rows_in):
    pad = jnp.zeros((LANES - rows_in.shape[0], rows_in.shape[1]), f32)
    return jnp.concatenate([rows_in, pad], axis=0).T


def lane_ids(shape):
    return lax.broadcasted_iota(jnp.int32, shape, 1)


def waits(after):
    return [
        pl.BlockSpec(memory_space=pltpu.VMEM if item.size <= 4096 else pl.ANY) for item in after
    ]


def call(body, outs, args, scalars=(), flops=0, after=(), scratch=()):
    n_in = len(args)

    def kernel(*refs):
        body(*refs[:n_in], *refs[n_in + len(after) :])

    moved = sum(a.size * a.dtype.itemsize for a in args) + sum(
        math.prod(o.shape) * o.dtype.itemsize for o in outs
    )
    vmem = pl.BlockSpec(memory_space=pltpu.VMEM)
    smem = pl.BlockSpec(memory_space=pltpu.SMEM)
    in_specs = [smem if k in scalars else vmem for k in range(n_in)]
    in_specs += waits(after)
    return pl.pallas_call(
        kernel,
        out_shape=outs,
        in_specs=in_specs,
        out_specs=[vmem] * len(outs),
        scratch_shapes=list(scratch),
        compiler_params=pltpu.CompilerParams(vmem_limit_bytes=VMEM_BYTES),
        cost_estimate=pl.CostEstimate(flops=flops, bytes_accessed=moved, transcendentals=0),
    )(*args, *after)


def out(shape, dtype):
    return jax.ShapeDtypeStruct(shape, dtype)


def norm_table(parts):
    sums = parts[0][...]
    for item in parts[1:]:
        sums = sums + item[...]
    mean = sums[0:4] * (1.0 / D)
    inv_std = lax.rsqrt(sums[4:8] * (1.0 / D) - mean * mean + norm_eps)
    return to_columns(jnp.concatenate([mean, inv_std], axis=0))


def table_body(*refs):
    refs[-1][...] = norm_table(refs[:-1])


def near_body(parts, *refs):
    idx, own, other, own_params, other_params, near = refs[parts:]
    cols = own.shape[2]
    table = norm_table(refs[:parts])
    at = idx[0]
    for which, (src, affine) in enumerate(
        ((own, own_params), (other, other_params))
    ):
        place = pl.multiple_of((at if which == 0 else 1 - at) * cols, LANES)
        for s in range(4):
            centred = (src[s].astype(f32) - table[:, s : s + 1]) * table[:, 4 + s : 5 + s]
            value = centred * affine[s : s + 1].astype(f32) + affine[4 + s : 5 + s].astype(f32)
            near[s, :, pl.ds(place, cols)] = value.astype(bf16)


def norm_back_body(parts, grad, arrived, own, stat, gain, *refs):
    sums = refs[0][...]
    for k in range(1, parts):
        sums = sums + refs[k][...]
    layer_grad, result, reduced = refs[parts:]
    table = stat[...]
    totals = to_columns(sums * (1.0 / D))
    for k in range(4):
        s = k
        value = grad[k] + arrived[k].astype(f32)
        inv_std = table[:, 4 + s : 5 + s]
        centred = (own[s].astype(f32) - table[:, s : s + 1]) * inv_std
        reduced[k : k + 1] = jnp.sum(value * centred, axis=0, keepdims=True)
        reduced[4 + k : 5 + k] = jnp.sum(value, axis=0, keepdims=True)
        back = inv_std * (
            value * gain[s : s + 1].astype(f32)
            - totals[:, k : k + 1]
            - centred * totals[:, 4 + k : 5 + k]
        )
        if s == 3:
            back = back + layer_grad[...]
        result[k] = back.astype(bf16)


def turn(x, tables, direction):
    cosine, low_sine, high_sine = tables
    half = ROT // 2
    return (
        x * cosine
        + direction * (jnp.roll(x, -half, axis=1) * low_sine + jnp.roll(x, half, axis=1) * high_sine)
    )


def rotary_tables(length):
    positions = lax.iota(f32, length)
    freqs = jnp.exp(lax.iota(f32, ROT // 2) * (-2.0 * math.log(10000.0) / ROT))
    angles = positions[:, None] * freqs[None, :]
    cosine = jnp.cos(angles)
    sine = jnp.sin(angles)
    zero = jnp.zeros((length, ROT // 2), f32)
    rest = jnp.zeros((length, HD - ROT), f32)
    return (
        jnp.concatenate([cosine, cosine, rest + 1.0], axis=1),
        jnp.concatenate([-sine, zero, rest], axis=1),
        jnp.concatenate([zero, sine, rest], axis=1),
    )


def probabilities(query, key, scale):
    scores = contract_cols(query, key) * scale
    rows = lax.broadcasted_iota(jnp.int32, scores.shape, 0)
    scores = jnp.where(lane_ids(scores.shape) <= rows, scores, -1e30)
    top = jnp.max(scores, axis=1, keepdims=True)
    log_total = top + jnp.log(jnp.sum(jnp.exp(scores - top), axis=1, keepdims=True))
    return jnp.exp(scores - log_total)


def forward_body(scale, arrived, own, qkv_bias, up_bias, cosine, low_sine, high_sine, qkv, pre, features):
    tables = (cosine[...], low_sine[...], high_sine[...])
    cols, width = qkv.shape[2], pre.shape[1]
    for h in range(cols // HD):
        parts = []
        for i in range(3):
            at = slice(i * cols + h * HD, i * cols + (h + 1) * HD)
            bias = qkv_bias[i : i + 1, h * HD : (h + 1) * HD].astype(f32)
            value = arrived[:, at].astype(f32) + own[:, at] + bias
            if i < 2:
                value = turn(value, tables, 1.0)
            value = value.astype(bf16)
            qkv[i, :, h * HD : (h + 1) * HD] = value
            parts.append(value)
        probs = probabilities(parts[0], parts[1], scale).astype(bf16)
        features[:, width + h * HD : width + (h + 1) * HD] = plain_dot(probs, parts[2]).astype(bf16)
    value = arrived[:, 3 * cols :].astype(f32) + own[:, 3 * cols :] + up_bias[...].astype(f32)
    pre[...] = value
    features[:, :width] = gelu_exact(value).astype(bf16)


def backward_body(scale, arrived, own, qkv, pre, cosine, low_sine, high_sine, grads):
    tables = (cosine[...], low_sine[...], high_sine[...])
    cols, width = qkv.shape[2], pre.shape[1]
    for h in range(cols // HD):
        at = slice(h * HD, (h + 1) * HD)
        query, key, value = qkv[0, :, at], qkv[1, :, at], qkv[2, :, at]
        place = slice(width + h * HD, width + (h + 1) * HD)
        out_grad = (own[:, place] + arrived[:, place].astype(f32)).astype(bf16)
        probs = probabilities(query, key, scale)
        value_grad = contract_rows(probs.astype(bf16), out_grad)
        prob_grad = contract_cols(out_grad, value)
        row_dot = jnp.sum(probs * prob_grad, axis=1, keepdims=True)
        score_grad = (probs * (prob_grad - row_dot)).astype(bf16)
        query_grad = turn(plain_dot(score_grad, key) * scale, tables, -1.0)
        key_grad = turn(contract_rows(score_grad, query) * scale, tables, -1.0)
        for i, grad in enumerate((query_grad, key_grad, value_grad)):
            low = grad.astype(bf16)
            grads[:, i * cols + h * HD : i * cols + (h + 1) * HD] = low
    total = arrived[:, :width].astype(f32) + own[:, :width]
    low = (total * gelu_slope(pre[...])).astype(bf16)
    grads[:, 3 * cols :] = low


def bias_rows_body(grads, rows):
    cols = rows.shape[1]
    total = jnp.sum(grads[...].astype(f32), axis=0, keepdims=True)
    rows[...] = jnp.zeros(rows.shape, f32)
    for t in range(total.shape[1] // cols):
        at = t if t < 3 else 8 + t - 3
        rows[at : at + 1] = total[:, t * cols : (t + 1) * cols]


def fold(value):
    total = value[:, :LANES]
    for k in range(1, value.shape[1] // LANES):
        total = total + value[:, k * LANES : (k + 1) * LANES]
    return total


def prior_body(grad_out, prior, result, held):
    def group(r, carry):
        rows = pl.ds(pl.multiple_of(r * ROWS, ROWS), ROWS)
        grads = [grad_out[s, rows, :].astype(f32) for s in range(4)]
        lanes = lane_ids((ROWS, LANES))
        packed = jnp.zeros((ROWS, LANES), f32)
        for j in range(STACK - 1):
            value = prior[j, rows, :].astype(f32)
            for s in range(4):
                column = jnp.sum(fold(grads[s] * value), axis=1, keepdims=True)
                packed = jnp.where(lanes == s * STACK + j, column, packed)
        held[rows, :] = packed
        return carry

    lax.fori_loop(0, held.shape[0] // ROWS, group, 0)
    result[...] = held[...].T[:64]


def prior_products(streams_grad, prior, after=()):
    length, cols = prior.shape[1:]
    block = min(length, LANES)

    def kernel(grad_ref, prior_ref, *refs):
        prior_body(grad_ref, prior_ref, *refs[len(after) :])

    return pl.pallas_call(
        kernel,
        grid=(length // block,),
        out_shape=out((64, length), f32),
        in_specs=[
            pl.BlockSpec((4, block, cols), lambda t: (0, t, 0)),
            pl.BlockSpec((STACK - 1, block, cols), lambda t: (0, t, 0)),
        ]
        + waits(after),
        out_specs=pl.BlockSpec((64, block), lambda t: (0, t)),
        scratch_shapes=[pltpu.VMEM((block, LANES), f32)],
        compiler_params=pltpu.CompilerParams(vmem_limit_bytes=VMEM_BYTES),
        cost_estimate=pl.CostEstimate(
            flops=20_000_000, bytes_accessed=2 * length * cols * 16, transcendentals=0
        ),
    )(streams_grad, prior, *after)


def mix_first_body(
    parts, streams, own, *refs
):
    arrived = refs[:parts]
    branch_bias, gain, mix_in, grad_out, layer_out, packed_out = refs[parts:]
    value = own[...]
    for item in arrived:
        value = value + item[...].astype(f32)
    value = streams[3].astype(f32) + (value + branch_bias[...].astype(f32))
    layer_out[...] = value
    packed = plain_dot(value * gain[...].astype(f32), mix_in[...], high)
    lanes = lane_ids(packed.shape)
    energy = jnp.sum(fold(value * value), axis=1, keepdims=True)
    packed = jnp.where(lanes == MIXH, energy, packed)
    for s in range(4):
        column = jnp.sum(fold(grad_out[s].astype(f32) * value), axis=1, keepdims=True)
        packed = jnp.where(lanes == MIXH + 1 + s, column, packed)
    packed_out[...] = packed.T[:64]


def mix_tables(packed, prior_coef, mix_in, mix_out, mix_static, gain, value, grad_out):
    lanes = lane_ids(packed.shape)
    energy = packed[:, MIXH : MIXH + 1]
    rms = lax.rsqrt(energy * (1.0 / D) + rms_eps)
    logit_sum = jnp.where(lanes < MIXH, packed, 0.0)
    logits = logit_sum * rms
    mix_hidden = gelu_exact(logits)
    coef = plain_dot(mix_hidden, mix_out, high) + mix_static
    coef_grad = prior_coef
    for s in range(4):
        column = packed[:, MIXH + 1 + s : MIXH + 2 + s]
        coef_grad = jnp.where(lanes == s * STACK + STACK - 1, column, coef_grad)
    logit_grad = contract_cols(coef_grad, mix_out, high) * gelu_slope(logits)
    sum_grad = logit_grad * rms
    rms_grad = jnp.sum(logit_grad * logit_sum, axis=1, keepdims=True)
    energy_grad = rms_grad * rms * rms * rms * (-1.0 / D)
    scaled_grad = contract_cols(sum_grad, mix_in, high)
    total = scaled_grad * gain + energy_grad * value
    for s in range(4):
        at = s * STACK + STACK - 1
        total = total + coef[:, at : at + 1] * grad_out[s].astype(f32)
    return coef, coef_grad, mix_hidden, sum_grad, scaled_grad, total


def mix_second_body(parts, me, *refs):
    held = refs[-1]
    for k in range(parts):
        held[lax.rem(me[0] + (parts - k), parts)] = refs[k][...]
    sums = held[0]
    for k in range(1, parts):
        sums = sums + held[k]
    (prior_coef, layer_out, grad_out, gain, mix_in, mix_out, mix_static,
     branch_grad, packed) = refs[parts:-1]
    packed[...] = sums
    total = mix_tables(
        to_columns(sums), to_columns(prior_coef[...]), mix_in[...], mix_out[...], mix_static[...],
        gain[...].astype(f32), layer_out[...], grad_out,
    )[-1]
    branch_grad[...] = total.astype(bf16)


def mix_third_body(packed, prior_coef, mix_in, mix_out, mix_static, layer_out, prior, grad_out, gain,
                   streams_out, prior_grad, weight_grads, token, layer_grad, reduced, held):
    block, cols = layer_out.shape
    step = pl.program_id(0)
    coef, coef_grad, mix_hidden, sum_grad, scaled_grad, total = mix_tables(
        to_columns(packed[...]), to_columns(prior_coef[...]), mix_in[...], mix_out[...],
        mix_static[...], gain[...].astype(f32), layer_out[...], grad_out,
    )
    held[...] = coef
    layer_grad[...] = total

    @pl.when(step == 0)
    def _():
        weight_grads[...] = jnp.zeros(weight_grads.shape, f32)
        reduced[...] = jnp.zeros(reduced.shape, f32)
        mark(token)

    reduced[0:1] += jnp.sum(scaled_grad * layer_out[...], axis=0, keepdims=True)
    reduced[1:2] += jnp.sum(total.astype(bf16).astype(f32), axis=0, keepdims=True)
    scaled = layer_out[...] * gain[...].astype(f32)
    weight_grads[:cols] += contract_rows(scaled, sum_grad, high)
    chosen = jnp.where(lane_ids((block, LANES)) == MIXH, 1.0, mix_hidden)
    weight_grads[cols:] += contract_rows(chosen, coef_grad, high)[: weight_grads.shape[0] - cols]

    def group(r, carry):
        rows = pl.ds(pl.multiple_of(r * ROWS, ROWS), ROWS)
        coef = held[rows, :]
        grads = [grad_out[s, rows, :].astype(f32) for s in range(4)]
        value = layer_out[rows, :]
        totals = []
        for s in range(4):
            at = s * STACK + STACK - 1
            totals.append(coef[:, at : at + 1] * value)
        for j in range(STACK - 1):
            value = prior[j, rows, :].astype(f32)
            back = None
            for s in range(4):
                at = s * STACK + j
                column = jnp.broadcast_to(coef[:, at : at + 1], (ROWS, cols))
                totals[s] = totals[s] + column * value
                term = column * grads[s]
                back = term if back is None else back + term
            prior_grad[j, rows, :] = back.astype(bf16)
        for s in range(4):
            streams_out[s, rows, :] = totals[s].astype(bf16)
        return carry

    lax.fori_loop(0, block // ROWS, group, 0)


def mix_third(packed, prior_coef, mix_in, mix_out, mix_static, layer_out, prior, streams_grad, gain, after):
    length, cols = layer_out.shape
    block = min(length, LANES)
    tokens = lambda count: pl.BlockSpec((count, block, cols), lambda t: (0, t, 0))
    whole = lambda *shape: pl.BlockSpec(shape, lambda t: (0,) * len(shape))

    def kernel(*refs):
        mix_third_body(*refs[:9], *refs[9 + len(after) :])

    return pl.pallas_call(
        kernel,
        grid=(length // block,),
        out_shape=[
            out((4, length, cols), bf16),
            out((STACK - 1, length, cols), bf16),
            out((cols + 56, LANES), f32),
            TOKEN,
            out((length, cols), f32),
            out((8, cols), f32),
        ],
        in_specs=[
            pl.BlockSpec((64, block), lambda t: (0, t)),
            pl.BlockSpec((64, block), lambda t: (0, t)),
            whole(cols, LANES),
            whole(LANES, LANES),
            whole(1, LANES),
            pl.BlockSpec((block, cols), lambda t: (t, 0)),
            tokens(STACK - 1),
            tokens(4),
            whole(1, cols),
        ]
        + waits(after),
        out_specs=[
            tokens(4),
            tokens(STACK - 1),
            whole(cols + 56, LANES),
            whole(8, LANES),
            pl.BlockSpec((block, cols), lambda t: (t, 0)),
            whole(8, cols),
        ],
        scratch_shapes=[pltpu.VMEM((block, LANES), f32)],
        compiler_params=PARAMS,
        cost_estimate=pl.CostEstimate(
            flops=30_000_000, bytes_accessed=2 * length * cols * 34, transcendentals=0
        ),
    )(packed, prior_coef, mix_in, mix_out, mix_static, layer_out, prior, streams_grad, gain, *after)


def cost(flops, moved):
    return pl.CostEstimate(flops=flops, bytes_accessed=moved, transcendentals=0)


ANY = pl.BlockSpec(memory_space=pl.ANY)
PARAMS = pltpu.CompilerParams(vmem_limit_bytes=VMEM_BYTES)
WIDE_PARAMS = pltpu.CompilerParams(vmem_limit_bytes=60 * 1024 * 1024)


def prefetched(kernel, scalars, grid, in_specs, out_specs, out_shape, args, estimate, aliases=None):
    return pl.pallas_call(
        kernel,
        grid_spec=pltpu.PrefetchScalarGridSpec(
            num_scalar_prefetch=len(scalars), grid=grid, in_specs=in_specs, out_specs=out_specs
        ),
        out_shape=out_shape,
        input_output_aliases=aliases or {},
        compiler_params=PARAMS,
        cost_estimate=estimate,
    )(*scalars, *args)


def fetch(pairs, sems):
    copies = [pltpu.make_async_copy(src, dst, sems.at[k]) for k, (src, dst) in enumerate(pairs)]
    for item in copies:
        item.start()
    return copies


def spread(block, near, w_qkv, w_up, up_cols, dtype, after):
    _, length, depth = near.shape
    cols = depth // 2
    width = 3 * cols + up_cols

    def kernel(b, near_ref, qkv_ref, up_ref, *refs):
        result, left, qkv, up, sems = refs[len(after) :]
        pairs = []
        for s in range(4):
            pairs.append((near_ref.at[s], left.at[s]))
            if s < 3:
                place = pl.multiple_of(b[0] * cols, LANES)
                pairs.append((qkv_ref.at[s, :, pl.ds(place, cols)], qkv.at[s]))
            else:
                place = pl.multiple_of(b[0] * up_cols, LANES)
                pairs.append((up_ref.at[:, pl.ds(place, up_cols)], up))
        copies = fetch(pairs, sems)
        for s in range(4):
            copies[2 * s].wait()
            copies[2 * s + 1].wait()
            if s < 3:
                result[:, s * cols : (s + 1) * cols] = plain_dot(left[s], qkv[s]).astype(dtype)
            else:
                result[:, 3 * cols :] = plain_dot(left[s], up[...]).astype(dtype)

    vmem = pl.BlockSpec(memory_space=pltpu.VMEM)
    return pl.pallas_call(
        kernel,
        out_shape=out((length, width), dtype),
        in_specs=[pl.BlockSpec(memory_space=pltpu.SMEM)] + [ANY] * 3 + waits(after),
        out_specs=vmem,
        scratch_shapes=[
            pltpu.VMEM((4, length, depth), bf16),
            pltpu.VMEM((3, depth, cols), bf16),
            pltpu.VMEM((depth, up_cols), bf16),
            pltpu.SemaphoreType.DMA((8,)),
        ],
        compiler_params=PARAMS if after else WIDE_PARAMS,
        cost_estimate=cost(2 * length * depth * width, 2 * depth * width + 4 * length * width),
    )(block, near, w_qkv, w_up, *after)


def spread_back(idx, block, own, other, w_down, w_out, up_cols, dtype, after):
    length, cols = own.shape

    def kernel(b, idx_ref, own_ref, other_ref, down_ref, out_ref, *refs):
        result, pair, down, outer, sems = refs[len(after) :]
        copies = fetch(
            [
                (down_ref.at[pl.ds(pl.multiple_of(b[0] * up_cols, up_cols), up_cols)], down),
                (out_ref.at[pl.ds(pl.multiple_of(b[0] * cols, cols), cols)], outer),
            ],
            sems,
        )
        pair[:, pl.ds(pl.multiple_of(idx_ref[0] * cols, LANES), cols)] = own_ref[...]
        pair[:, pl.ds(pl.multiple_of((1 - idx_ref[0]) * cols, LANES), cols)] = other_ref[...]
        copies[0].wait()
        result[:, :up_cols] = contract_cols(pair[...], down[...]).astype(dtype)
        copies[1].wait()
        result[:, up_cols:] = contract_cols(pair[...], outer[...]).astype(dtype)

    depth = up_cols + cols
    smem = pl.BlockSpec(memory_space=pltpu.SMEM)
    vmem = pl.BlockSpec(memory_space=pltpu.VMEM)
    return pl.pallas_call(
        kernel,
        out_shape=out((length, depth), dtype),
        in_specs=[smem, smem, vmem, vmem, ANY, ANY] + waits(after),
        out_specs=vmem,
        scratch_shapes=[
            pltpu.VMEM((length, 2 * cols), bf16),
            pltpu.VMEM((up_cols, 2 * cols), bf16),
            pltpu.VMEM((cols, 2 * cols), bf16),
            pltpu.SemaphoreType.DMA((2,)),
        ],
        compiler_params=PARAMS,
        cost_estimate=cost(4 * length * depth * cols, 4 * depth * cols + 4 * length * depth),
    )(block, idx, own, other, w_down, w_out, *after)


def take_body(up_cols, block, down_ref, out_ref, result, token, sems):
    mark(token)
    cols = result.shape[0] - up_cols
    copies = fetch(
        [
            (
                down_ref.at[pl.ds(pl.multiple_of(block[0] * up_cols, up_cols), up_cols)],
                result.at[pl.ds(0, up_cols)],
            ),
            (
                out_ref.at[pl.ds(pl.multiple_of(block[0] * cols, cols), cols)],
                result.at[pl.ds(up_cols, cols)],
            ),
        ],
        sems,
    )
    for item in copies:
        item.wait()


def take(block, w_down, w_out, up_cols, after):
    depth = up_cols + w_down.shape[1] // 2
    vmem = pl.BlockSpec(memory_space=pltpu.VMEM)

    def kernel(b, down_ref, out_ref, *refs):
        take_body(up_cols, b, down_ref, out_ref, *refs[len(after) :])

    return pl.pallas_call(
        kernel,
        out_shape=[out((depth, w_down.shape[1]), bf16), TOKEN],
        in_specs=[pl.BlockSpec(memory_space=pltpu.SMEM), ANY, ANY] + waits(after),
        out_specs=[vmem, vmem],
        scratch_shapes=[pltpu.SemaphoreType.DMA((2,))],
        compiler_params=PARAMS,
        cost_estimate=cost(0, 8 * depth * w_down.shape[1]),
    )(block, w_down, w_out, *after)


def first_back_body(idx, own, other, weights, result, pair):
    cols = own.shape[1]
    pair[:, pl.ds(pl.multiple_of(idx[0] * cols, LANES), cols)] = own[...]
    pair[:, pl.ds(pl.multiple_of((1 - idx[0]) * cols, LANES), cols)] = other[...]
    result[...] = contract_cols(pair[...], weights[...]).astype(bf16)


def add_body(arrived, term, result):
    result[...] = (arrived[...].astype(f32) + term[...]).astype(bf16)


def branch_step(block, item, so_far, w_down, w_out, up_cols, after):
    length, depth = item.shape
    cols = depth - up_cols
    wide_cols = w_down.shape[1]
    earlier = [] if so_far is None else [so_far]
    whole = pl.BlockSpec((length, wide_cols), lambda i, b: (0, 0))

    def kernel(b, item_ref, down_ref, out_ref, *refs):
        value = plain_dot(item_ref[:, :up_cols], down_ref[...]) + plain_dot(
            item_ref[:, up_cols:], out_ref[...]
        )
        refs[-2][...] = refs[0][...] + value if earlier else value
        mark(refs[-1])

    return prefetched(
        kernel,
        [block],
        (1,),
        [
            pl.BlockSpec((length, depth), lambda i, b: (0, 0)),
            pl.BlockSpec((up_cols, wide_cols), lambda i, b: (b[0], 0)),
            pl.BlockSpec((cols, wide_cols), lambda i, b: (b[0], 0)),
        ]
        + [whole] * len(earlier)
        + waits(after),
        [whole, pl.BlockSpec((8, LANES), lambda i, b: (0, 0))],
        [out((length, wide_cols), f32), TOKEN],
        [item, w_down, w_out, *earlier, *after],
        cost(2 * length * depth * wide_cols, 2 * depth * wide_cols),
    )


def halves_body(idx, value, theirs, mine):
    cols = mine.shape[1]
    mine[...] = value[:, pl.ds(pl.multiple_of(idx[0] * cols, LANES), cols)]
    theirs[...] = value[:, pl.ds(pl.multiple_of((1 - idx[0]) * cols, LANES), cols)].astype(bf16)


def near_step(block, item, so_far, w_qkv, w_up, cols, after):
    length = item.shape[0]
    depth = w_up.shape[0]
    up_cols = item.shape[1] - 3 * cols
    earlier = [] if so_far is None else [so_far]
    one = pl.BlockSpec((1, length, depth), lambda s, b: (s, 0, 0))

    def kernel(b, item_ref, qkv_ref, up_ref, *refs):
        step = pl.program_id(0)
        base = refs[0][0] if earlier else 0.0

        @pl.when(step < 3)
        def _():
            part = item_ref[:, pl.ds(pl.multiple_of(step * cols, LANES), cols)]
            refs[-2][0] = contract_cols(part, qkv_ref[0]) + base

        @pl.when(step == 3)
        def _():
            refs[-2][0] = contract_cols(item_ref[:, 3 * cols :], up_ref[...]) + base
            mark(refs[-1])

    return prefetched(
        kernel,
        [block],
        (4,),
        [
            pl.BlockSpec(item.shape, lambda s, b: (0, 0)),
            pl.BlockSpec((1, depth, cols), lambda s, b: (jnp.minimum(s, 2), 0, b[0])),
            pl.BlockSpec((depth, up_cols), lambda s, b: (0, b[0])),
        ]
        + [one] * len(earlier)
        + waits(after),
        [one, pl.BlockSpec((8, LANES), lambda s, b: (0, 0))],
        [out((4, length, depth), f32), TOKEN],
        [item, w_qkv, w_up, *earlier, *after],
        cost(2 * item.size * depth, 2 * item.size * depth // length + 32 * length * depth),
    )


def near_last(idx, block, item, so_far, w_qkv, w_up, own, other, stat, gain_own, gain_other):
    length = item.shape[0]
    depth = w_up.shape[0]
    cols = depth // 2
    up_cols = item.shape[1] - 3 * cols

    def kernel(b, x, item_ref, qkv_ref, up_ref, base, own_ref, other_ref, stat_ref, gain_o, gain_f,
               theirs, mine, stats, value, packed):
        step = pl.program_id(0)

        @pl.when(step < 3)
        def _():
            part = item_ref[:, pl.ds(pl.multiple_of(step * cols, LANES), cols)]
            value[...] = contract_cols(part, qkv_ref[0]) + base[0]

        @pl.when(step == 3)
        def _():
            value[...] = contract_cols(item_ref[:, 3 * cols :], up_ref[...]) + base[0]

        table = stat_ref[...]
        lanes = lane_ids(table.shape)
        mean = jnp.sum(jnp.where(lanes == step, table, 0.0), axis=1, keepdims=True)
        inv_std = jnp.sum(jnp.where(lanes == step + 4, table, 0.0), axis=1, keepdims=True)
        total = jnp.zeros((length, LANES), f32)
        cross = jnp.zeros((length, LANES), f32)
        for which, (src, gain) in enumerate(((own_ref, gain_o), (other_ref, gain_f))):
            place = pl.multiple_of((x[0] if which == 0 else 1 - x[0]) * cols, LANES)
            part = value[:, pl.ds(place, cols)]
            if which == 0:
                mine[0] = part
            else:
                theirs[0] = part.astype(bf16)
            scaled = part * gain[0].astype(f32)
            total = total + fold(scaled)
            cross = cross + fold(scaled * ((src[0].astype(f32) - mean) * inv_std))
        kept = jnp.where(step == 0, 0.0, packed[...])
        kept = jnp.where(lanes == step, jnp.sum(total, axis=1, keepdims=True), kept)
        kept = jnp.where(lanes == step + 4, jnp.sum(cross, axis=1, keepdims=True), kept)
        packed[...] = kept

        @pl.when(step == 3)
        def _():
            stats[...] = packed[...].T[:8]

    half = pl.BlockSpec((1, length, cols), lambda s, b, x: (s, 0, 0))
    row = pl.BlockSpec((1, 1, cols), lambda s, b, x: (s, 0, 0))
    return pl.pallas_call(
        kernel,
        grid_spec=pltpu.PrefetchScalarGridSpec(
            num_scalar_prefetch=2,
            grid=(4,),
            in_specs=[
                pl.BlockSpec(item.shape, lambda s, b, x: (0, 0)),
                pl.BlockSpec((1, depth, cols), lambda s, b, x: (jnp.minimum(s, 2), 0, b[0])),
                pl.BlockSpec((depth, up_cols), lambda s, b, x: (0, b[0])),
                pl.BlockSpec((1, length, depth), lambda s, b, x: (s, 0, 0)),
                half,
                half,
                pl.BlockSpec((length, LANES), lambda s, b, x: (0, 0)),
                row,
                row,
            ],
            out_specs=[half, half, pl.BlockSpec((8, length), lambda s, b, x: (0, 0))],
            scratch_shapes=[pltpu.VMEM((length, depth), f32), pltpu.VMEM((length, LANES), f32)],
        ),
        out_shape=[
            out((4, length, cols), bf16), out((4, length, cols), f32), out((8, length), f32),
        ],
        compiler_params=PARAMS,
        cost_estimate=cost(2 * item.size * depth, 2 * item.size * depth // length + 24 * length * depth),
    )(block, idx, item, w_qkv, w_up, so_far, own, other, stat, gain_own[:, None], gain_other[:, None])


def near_weights(order, block, near, parts, shapes, before, after=()):
    n_dp, _, length, depth = near.shape
    cols = depth // 2
    up_cols = parts[0].shape[1] - 3 * cols

    def kernel(order_ref, b, near_ref, *refs):
        qkv_grad, up_grad, done = refs[-3:]
        step = pl.program_id(0)
        left = jnp.concatenate([near_ref[order_ref[p], 0] for p in range(n_dp)], axis=0)

        @pl.when(step < 3)
        def _():
            place = pl.multiple_of(step * cols, LANES)
            right = jnp.concatenate([item[:, pl.ds(place, cols)] for item in refs[:n_dp]], axis=0)
            qkv_grad[0] = contract_rows(left, right)

        @pl.when(step == 3)
        def _():
            right = jnp.concatenate([item[:, 3 * cols :] for item in refs[:n_dp]], axis=0)
            up_grad[...] = contract_rows(left, right)
            done[...] = jnp.zeros(done.shape, f32)

    return prefetched(
        kernel,
        [order, block],
        (4,),
        [pl.BlockSpec((n_dp, 1, length, depth), lambda i, o, b: (0, i, 0, 0))]
        + [pl.BlockSpec(parts[0].shape, lambda i, o, b: (0, 0))] * n_dp
        + [ANY] * len(before)
        + waits(after),
        [
            pl.BlockSpec((1, depth, cols), lambda i, o, b: (jnp.minimum(i, 2), 0, b[0])),
            pl.BlockSpec((depth, up_cols), lambda i, o, b: (0, b[0])),
            pl.BlockSpec((8, LANES), lambda i, o, b: (0, 0)),
        ],
        [out(shape, f32) for shape in (*shapes, (8, LANES))],
        [near, *parts, *before, *after],
        cost(1000, 1000),
        {3 + n_dp + k: k for k in range(len(before))},
    )


def branch_weights(order, block, features, parts, up_cols, shapes, before):
    n_dp, length, depth = features.shape
    cols = depth - up_cols
    width = parts[0].shape[1]

    def kernel(order_ref, b, features_ref, *refs):
        left = jnp.concatenate([features_ref[order_ref[p]] for p in range(n_dp)], axis=0)
        right = jnp.concatenate([item[...] for item in refs[:n_dp]], axis=0)
        refs[-3][...] = contract_rows(left[:, :up_cols], right)
        refs[-2][...] = contract_rows(left[:, up_cols:], right)
        refs[-1][...] = jnp.zeros(refs[-1].shape, f32)

    return prefetched(
        kernel,
        [order, block],
        (1,),
        [pl.BlockSpec(features.shape, lambda i, o, b: (0, 0, 0))]
        + [pl.BlockSpec((length, width), lambda i, o, b: (0, 0))] * n_dp
        + [ANY] * len(before),
        [
            pl.BlockSpec((up_cols, width), lambda i, o, b: (b[0], 0)),
            pl.BlockSpec((cols, width), lambda i, o, b: (b[0], 0)),
            pl.BlockSpec((8, LANES), lambda i, o, b: (0, 0)),
        ],
        [out(shape, f32) for shape in (*shapes, (8, LANES))],
        [features, *parts, *before],
        cost(2 * features.size * width, 2 * features.size + 4 * depth * width),
        {3 + n_dp + k: k for k in range(len(before))},
    )


def gate(value, after):
    def kernel(*refs):
        pass

    return pl.pallas_call(
        kernel,
        out_shape=out(value.shape, value.dtype),
        in_specs=[ANY] + waits(after),
        out_specs=ANY,
        input_output_aliases={0: 0},
        compiler_params=pltpu.CompilerParams(
            has_side_effects=True, vmem_limit_bytes=VMEM_BYTES
        ),
    )(value, *after)


TOKEN = out((8, LANES), f32)


def mark(ref):
    ref[...] = jnp.zeros(ref.shape, f32)


def finish_body(rows, far, qkv_bias, up_bias, branch_bias, mix_gain, gain, shift_grad):
    total = rows[...] + far[...]
    qkv_bias[...] = total[0:3]
    mix_gain[...] = total[16:17]
    branch_bias[...] = total[17:18]
    up_bias[...] = total[8 : 8 + up_bias.shape[0]]
    gain[...] = total[24:28]
    shift_grad[...] = total[28:32]


def add_rows_body(*refs):
    total = refs[0][...]
    for item in refs[1:-1]:
        total = total + item[...]
    refs[-1][...] = total


def stats_body(streams, sums):
    length = streams.shape[1]
    lanes = lane_ids((length, LANES))
    packed = jnp.zeros((length, LANES), f32)
    for s in range(4):
        value = streams[s].astype(f32)
        packed = jnp.where(lanes == s, jnp.sum(fold(value), axis=1, keepdims=True), packed)
        packed = jnp.where(
            lanes == 4 + s, jnp.sum(fold(value * value), axis=1, keepdims=True), packed
        )
    sums[...] = packed.T[:8]


def build(n_dp, n_wide, n_narrow):
    def shift(value, axis, size, step):
        return lax.ppermute(value, axis, [(i, (i + step) % size) for i in range(size)])

    def swap(value, axis, size, bit):
        return lax.ppermute(value, axis, [(i, i ^ bit) for i in range(size)])

    def butterfly(value, axis, size):
        bit = 1
        while bit < size:
            value = value + swap(value, axis, size, bit)
            bit *= 2
        return value

    def narrow_swap(value):
        return swap(value, "narrow", n_narrow, 1)

    def model_parts(value):
        value = value + narrow_swap(value)
        return [value] + [shift(value, "wide", n_wide, k) for k in range(1, n_wide)]

    def model_butterfly(value):
        return butterfly(butterfly(value, "narrow", n_narrow), "wide", n_wide)

    def dp_sum(value):
        return butterfly(value, "dp", n_dp)

    def dp_gather(value):
        held = [value]
        far = value
        for _ in range(n_dp // CORES - 1):
            far = shift(far, "dp", n_dp, CORES)
            held.append(far)
        return held + [swap(item, "dp", n_dp, 1) for item in held]

    def across(value):
        held = [value]
        for _ in range(n_dp // CORES - 1):
            held.append(shift(held[-1], "dp", n_dp, CORES))
        return held

    def dp_order():
        me = lax.axis_index("dp")
        steps = [lax.rem(me + n_dp - CORES * k, n_dp) for k in range(n_dp // CORES)]
        return steps + [item ^ 1 for item in steps]

    def reduce_ring(product, hold):
        me = lax.axis_index("wide").astype(jnp.int32)
        block = lambda back: lax.rem(me + (n_wide - back), n_wide)[None]
        total = product(block(1), bf16, [])
        sent = [total]
        for at in range(n_wide - 1):
            arrived = shift(total, "wide", n_wide, 1)
            term = product(block(at + 2) if at + 2 < n_wide else me[None], f32, [total])
            if at < n_wide - 2:
                (total,) = call(
                    add_body, [out(total.shape, bf16)], [arrived, term], after=hold(at, total)
                )
                sent.append(total)
        return arrived, term, sent

    def per_device(
        streams, prior, streams_grad, w_qkv, qkv_bias, w_out, w_up, up_bias, w_down, branch_bias,
        norm_gain, norm_bias, mix_gain, mix_in, mix_out, mix_static,
    ):
        length = streams.shape[1]
        cols = streams.shape[2]
        scale = 1.0 / math.sqrt(HD)
        up_cols = w_up.shape[1] // n_wide
        tiles = up_cols // cols
        depth = up_cols + cols
        idx = lax.axis_index("narrow").astype(jnp.int32)[None]
        me = lax.axis_index("wide").astype(jnp.int32)
        order = jnp.stack(dp_order()).astype(jnp.int32)
        params = jnp.concatenate([norm_gain, norm_bias], axis=0)
        other_params = narrow_swap(params)
        gain_other = other_params[:4]
        other = narrow_swap(streams)
        (sums,) = call(stats_body, [out((8, length), f32)], [streams])
        (wide_sums,) = call(
            add_rows_body,
            [out((8, length), f32)],
            [sums] + [shift(sums, "wide", n_wide, k) for k in range(1, n_wide)],
            after=[other, other_params],
        )
        stat_parts = [wide_sums, narrow_swap(wide_sums)]
        (near,) = call(
            functools.partial(near_body, len(stat_parts)),
            [out((4, length, 2 * cols), bf16)],
            [*stat_parts, idx, streams, other, params, other_params],
            scalars={len(stat_parts)},
        )
        tables = rotary_tables(length)

        near_all = lax.all_gather(near, "dp", axis=0, tiled=False)
        near_token = near_all[0, 0, :8, :LANES]
        tables = rotary_tables(length)
        prior_rows = prior_products(streams_grad, prior)
        prior_sum = lax.psum(prior_rows, ("wide", "narrow"))
        arrived, own, sent = reduce_ring(
            lambda block, dtype, after: spread(
                block, near, w_qkv, w_up, up_cols, dtype, after
            ),
            lambda at, total: [],
        )
        qkv, up_pre, features = call(
            functools.partial(forward_body, scale),
            [
                out((3, length, cols), bf16),
                out((length, up_cols), f32),
                out((length, up_cols + cols), bf16),
            ],
            [arrived, own, qkv_bias, up_bias[None], *tables],
            flops=8 * length * length * cols,
        )
        (stat,) = call(table_body, [out((length, LANES), f32)], stat_parts, after=[features])
        blocks = [lax.rem(me + (n_wide - k), n_wide)[None] for k in range(n_wide)]
        item, branch_part, features_all = features, None, []
        for k in range(n_wide):
            branch_part, token = branch_step(
                blocks[k], item, branch_part, w_down, w_out, up_cols, []
            )
            features_all.append(lax.all_gather(item, "dp", axis=0, tiled=False))
            if k < n_wide - 1:
                item = gate(shift(item, "wide", n_wide, 1), [token])
        theirs, branch_own = call(
            halves_body,
            [out((length, cols), bf16), out((length, cols), f32)],
            [idx, branch_part],
            scalars={0},
        )
        branch_arrived = narrow_swap(theirs)
        mix_in_pad = jnp.pad(mix_in.astype(f32), ((0, 0), (0, LANES - MIXH)))
        mix_out_pad = jnp.pad(mix_out.astype(f32), ((0, LANES - MIXH), (0, LANES - MIXH)))
        static_pad = jnp.pad(mix_static.astype(f32)[None], ((0, 0), (0, LANES - MIXH)))
        gain_row = mix_gain[None]
        layer_out, packed = call(
            functools.partial(mix_first_body, 1),
            [out((length, cols), f32), out((64, length), f32)],
            [streams, branch_own, branch_arrived, branch_bias[None], gain_row, mix_in_pad, streams_grad],
            after=[near_token],
        )
        packed_parts = model_parts(packed)
        first_rows, rows_token = take(
            blocks[1 % n_wide], w_down, w_out, up_cols, [packed[:8, :LANES]]
        )
        branch_grad, packed_sum = call(
            functools.partial(mix_second_body, n_wide),
            [
                out((length, cols), bf16),
                out((64, length), f32),
            ],
            [me[None], *packed_parts, prior_sum, layer_out, streams_grad, gain_row, mix_in_pad,
             mix_out_pad, static_pad],
            scalars={0},
            scratch=[pltpu.VMEM((n_wide, 64, length), f32)],
            after=[rows_token],
        )
        branch_other = narrow_swap(branch_grad)
        mixer_outs, mixer_sums, branch_grads, tokens = [], [], [], []

        def branch_side(at, total):
            if at == 0:
                mixer_outs.extend(
                    mix_third(
                        packed_sum, prior_sum, mix_in_pad, mix_out_pad, static_pad, layer_out, prior,
                        streams_grad, gain_row, [total],
                    )
                )
                first = lax.axis_index("narrow") == 0
                pair = [gate(branch_grad, [total]), branch_other]
                near = jnp.concatenate(
                    [jnp.where(first, pair[0], pair[1]), jnp.where(first, pair[1], pair[0])], axis=1
                )
                branch_all = dp_gather(near)
                for k, block in enumerate(blocks):
                    *grads, token = branch_weights(
                        order, block, features_all[k], branch_all, up_cols,
                        (w_down.shape, w_out.shape), branch_grads[-1] if branch_grads else [],
                    )
                    branch_grads.append(grads)
                    tokens.append(token)
                mixer_sums.append(dp_sum(mixer_outs[2]))
                return [mixer_outs[3]]
            return tokens[:1]

        arrived, own, sent = reduce_ring(
            lambda block, dtype, after: (
                spread_back(
                    idx, block, branch_grad, branch_other, w_down, w_out, up_cols, dtype, after
                )
                if after
                else call(
                    first_back_body,
                    [out((length, up_cols + cols), bf16)],
                    [idx, branch_grad, branch_other, first_rows],
                    scalars={0},
                    scratch=[pltpu.VMEM((length, 2 * cols), bf16)],
                )[0]
            ),
            lambda at, total: branch_side(at, total),
        )
        (grads,) = call(
            functools.partial(backward_body, scale),
            [out((length, up_cols + 3 * cols), bf16)],
            [arrived, own, qkv, up_pre, *tables],
            flops=14 * length * length * cols,
            after=tokens[:1] + [mixer_sums[0][:8]],
        )
        (bias_rows,) = call(bias_rows_body, [out((16, cols), f32)], [grads])
        (mix_sums,) = mixer_sums
        item, near_grad, near_grads, held, mates = grads, None, [], [], []
        for k in range(n_wide):
            after = []
            if k < n_wide - 1:
                near_grad, token = near_step(blocks[k], item, near_grad, w_qkv, w_up, cols, [])
                after = [token, *([*tokens[1:], bias_rows] if k == 0 else [])]
            else:
                theirs, mine, stats = near_last(
                    idx, blocks[k], item, near_grad, w_qkv, w_up, streams, other, stat, norm_gain,
                    gain_other,
                )
            held.append(across(item))
            if k:
                far = [gate(part, [item]) for part in held[k - 1][1:]]
                crossed = [held[k - 1][0], *far, mates[k - 1]]
                crossed = crossed + [swap(part, "dp", n_dp, 1) for part in far]
                *near_grads, token = near_weights(
                    order, blocks[k - 1], near_all, crossed, (w_qkv.shape, w_up.shape), near_grads
                )
                after.append(token)
            if k < n_wide - 1:
                mates.append(swap(item, "dp", n_dp, 1))
                after += [held[k][-1], mates[k]]
            else:
                (wide_sum,) = call(
                    add_rows_body,
                    [out((8, length), f32)],
                    [stats] + [shift(stats, "wide", n_wide, j) for j in range(1, n_wide)],
                    after=[token],
                )
                mates.append(swap(gate(item, [wide_sum]), "dp", n_dp, 1))
            if k < n_wide - 1:
                item = gate(shift(item, "wide", n_wide, 1), after)
        down_weight_grad, out_weight_grad = branch_grads[-1]
        streams_out, prior_grad, _, _, layer_grad, mix_rows = mixer_outs
        stat_parts = [wide_sum, narrow_swap(wide_sum)]
        streams_in_grad, near_rows = call(
            functools.partial(norm_back_body, len(stat_parts)),
            [out((4, length, cols), bf16), out((8, cols), f32)],
            [mine, narrow_swap(theirs), streams, stat, norm_gain, *stat_parts, layer_grad],
        )
        far = [gate(part, [near_rows]) for part in held[-1][1:]]
        crossed = [held[-1][0], *far, mates[-1]] + [swap(part, "dp", n_dp, 1) for part in far]
        *near_grads, last_token = near_weights(
            order, blocks[-1], near_all, crossed, (w_qkv.shape, w_up.shape), near_grads
        )
        qkv_weight_grad, up_weight_grad = near_grads
        rows = jnp.concatenate([bias_rows, mix_rows, near_rows], axis=0)
        bit = 1
        while 2 * bit < n_dp:
            rows = rows + swap(rows, "dp", n_dp, bit)
            bit *= 2
        qkv_bias_grad, up_bias_grad, branch_bias_grad, mix_gain_grad, gain_grad, shift_grad = call(
            finish_body,
            [out((3, cols), f32), out((tiles, cols), f32), out((1, cols), f32), out((1, cols), f32),
             out((4, cols), f32), out((4, cols), f32)],
            [rows, swap(rows, "dp", n_dp, bit)],
            after=[last_token],
        )
        return (
            streams_out, streams_in_grad, prior_grad, qkv_weight_grad, qkv_bias_grad, out_weight_grad,
            up_weight_grad, up_bias_grad.reshape(-1), down_weight_grad, branch_bias_grad[0], gain_grad,
            shift_grad, mix_gain_grad[0], mix_sums[:cols, :MIXH],
            mix_sums[cols : cols + MIXH, :MIXH], mix_sums[cols + MIXH, :MIXH],
        )

    return per_device


def solution(mesh):
    tokens = P(None, "dp", ("wide", "narrow"))
    outer = P(("wide", "narrow"))
    inner = P(None, ("wide", "narrow"))
    column = P(("narrow", "wide"))
    return jax.shard_map(
        build(mesh.shape["dp"], mesh.shape["wide"], mesh.shape["narrow"]),
        mesh=mesh,
        in_specs=(
            tokens, tokens, tokens, P(None, "wide", "narrow"), P(None, ("narrow", "wide")),
            P("narrow", "wide"), P("wide", "narrow"), column, P("narrow", "wide"), outer, inner,
            inner, outer, P(("wide", "narrow"), None), P(), P(),
        ),
        out_specs=(
            tokens, tokens, tokens, P(None, "wide", "narrow"), P(None, ("narrow", "wide")),
            P("narrow", "wide"), P("wide", "narrow"), column, P("narrow", "wide"), outer, inner,
            inner, outer, P(("wide", "narrow"), None), P(), P(),
        ),
        check_vma=False,
    )
```

```python
import functools
import math

import jax
import jax.numpy as jnp
from jax import lax
from jax.experimental import pallas as pl
from jax.experimental.pallas import tpu as pltpu
from jax.sharding import PartitionSpec as P

D = 2048
HD = 128
ROT = 32
MIXH = 52
STACK = 13
CORES = 2
LANES = 128
ROWS = 16

norm_eps = 1e-05
rms_eps = 1e-06

f32 = jnp.float32
bf16 = jnp.bfloat16
high = lax.Precision.HIGHEST
VMEM_BYTES = 46 * 1024 * 1024


def gelu_exact(inputs):
    return 0.5 * inputs * (1.0 + lax.erf(inputs * (1.0 / math.sqrt(2.0))))


def gelu_slope(inputs):
    normal_cdf = 0.5 * (1.0 + lax.erf(inputs * (1.0 / math.sqrt(2.0))))
    return normal_cdf + inputs * jnp.exp(-0.5 * inputs * inputs) * (1.0 / math.sqrt(2.0 * math.pi))


def dot(left, right, dims, precision=None):
    return lax.dot_general(
        left, right, (dims, ((), ())), precision=precision, preferred_element_type=f32
    )


def contract_rows(left, right, precision=None):
    return dot(left, right, ((0,), (0,)), precision)


def contract_cols(left, right, precision=None):
    return dot(left, right, ((1,), (1,)), precision)


def plain_dot(left, right, precision=None):
    return dot(left, right, ((1,), (0,)), precision)


def to_columns(rows_in):
    pad = jnp.zeros((LANES - rows_in.shape[0], rows_in.shape[1]), f32)
    return jnp.concatenate([rows_in, pad], axis=0).T


def lane_ids(shape):
    return lax.broadcasted_iota(jnp.int32, shape, 1)


def waits(after):
    return [
        pl.BlockSpec(memory_space=pltpu.VMEM if item.size <= 4096 else pl.ANY) for item in after
    ]


def call(body, outs, args, scalars=(), flops=0, after=(), scratch=()):
    n_in = len(args)

    def kernel(*refs):
        body(*refs[:n_in], *refs[n_in + len(after) :])

    moved = sum(a.size * a.dtype.itemsize for a in args) + sum(
        math.prod(o.shape) * o.dtype.itemsize for o in outs
    )
    vmem = pl.BlockSpec(memory_space=pltpu.VMEM)
    smem = pl.BlockSpec(memory_space=pltpu.SMEM)
    in_specs = [smem if k in scalars else vmem for k in range(n_in)]
    in_specs += waits(after)
    return pl.pallas_call(
        kernel,
        out_shape=outs,
        in_specs=in_specs,
        out_specs=[vmem] * len(outs),
        scratch_shapes=list(scratch),
        compiler_params=pltpu.CompilerParams(vmem_limit_bytes=VMEM_BYTES),
        cost_estimate=pl.CostEstimate(flops=flops, bytes_accessed=moved, transcendentals=0),
    )(*args, *after)


def out(shape, dtype):
    return jax.ShapeDtypeStruct(shape, dtype)


def norm_table(parts):
    sums = parts[0][...]
    for item in parts[1:]:
        sums = sums + item[...]
    mean = sums[0:4] * (1.0 / D)
    inv_std = lax.rsqrt(sums[4:8] * (1.0 / D) - mean * mean + norm_eps)
    return to_columns(jnp.concatenate([mean, inv_std], axis=0))


def table_body(*refs):
    refs[-1][...] = norm_table(refs[:-1])


def near_body(parts, *refs):
    idx, own, other, own_params, other_params, near = refs[parts:]
    cols = own.shape[2]
    table = norm_table(refs[:parts])
    at = idx[0]
    for which, (src, affine) in enumerate(
        ((own, own_params), (other, other_params))
    ):
        place = pl.multiple_of((at if which == 0 else 1 - at) * cols, LANES)
        for s in range(4):
            centred = (src[s].astype(f32) - table[:, s : s + 1]) * table[:, 4 + s : 5 + s]
            value = centred * affine[s : s + 1].astype(f32) + affine[4 + s : 5 + s].astype(f32)
            near[s, :, pl.ds(place, cols)] = value.astype(bf16)


def norm_back_body(parts, grad, arrived, own, stat, gain, *refs):
    sums = refs[0][...]
    for k in range(1, parts):
        sums = sums + refs[k][...]
    layer_grad, result, reduced = refs[parts:]
    table = stat[...]
    totals = to_columns(sums * (1.0 / D))
    for k in range(4):
        s = k
        value = grad[k] + arrived[k].astype(f32)
        inv_std = table[:, 4 + s : 5 + s]
        centred = (own[s].astype(f32) - table[:, s : s + 1]) * inv_std
        reduced[k : k + 1] = jnp.sum(value * centred, axis=0, keepdims=True)
        reduced[4 + k : 5 + k] = jnp.sum(value, axis=0, keepdims=True)
        back = inv_std * (
            value * gain[s : s + 1].astype(f32)
            - totals[:, k : k + 1]
            - centred * totals[:, 4 + k : 5 + k]
        )
        if s == 3:
            back = back + layer_grad[...]
        result[k] = back.astype(bf16)


def turn(x, tables, direction):
    cosine, low_sine, high_sine = tables
    half = ROT // 2
    return (
        x * cosine
        + direction * (jnp.roll(x, -half, axis=1) * low_sine + jnp.roll(x, half, axis=1) * high_sine)
    )


def rotary_tables(length):
    positions = lax.iota(f32, length)
    freqs = jnp.exp(lax.iota(f32, ROT // 2) * (-2.0 * math.log(10000.0) / ROT))
    angles = positions[:, None] * freqs[None, :]
    cosine = jnp.cos(angles)
    sine = jnp.sin(angles)
    zero = jnp.zeros((length, ROT // 2), f32)
    rest = jnp.zeros((length, HD - ROT), f32)
    return (
        jnp.concatenate([cosine, cosine, rest + 1.0], axis=1),
        jnp.concatenate([-sine, zero, rest], axis=1),
        jnp.concatenate([zero, sine, rest], axis=1),
    )


def probabilities(query, key, scale):
    scores = contract_cols(query, key) * scale
    rows = lax.broadcasted_iota(jnp.int32, scores.shape, 0)
    scores = jnp.where(lane_ids(scores.shape) <= rows, scores, -1e30)
    top = jnp.max(scores, axis=1, keepdims=True)
    log_total = top + jnp.log(jnp.sum(jnp.exp(scores - top), axis=1, keepdims=True))
    return jnp.exp(scores - log_total)


def forward_body(scale, arrived, own, qkv_bias, up_bias, cosine, low_sine, high_sine, qkv, pre, features):
    tables = (cosine[...], low_sine[...], high_sine[...])
    cols, width = qkv.shape[2], pre.shape[1]
    for h in range(cols // HD):
        parts = []
        for i in range(3):
            at = slice(i * cols + h * HD, i * cols + (h + 1) * HD)
            bias = qkv_bias[i : i + 1, h * HD : (h + 1) * HD].astype(f32)
            value = arrived[:, at].astype(f32) + own[:, at] + bias
            if i < 2:
                value = turn(value, tables, 1.0)
            value = value.astype(bf16)
            qkv[i, :, h * HD : (h + 1) * HD] = value
            parts.append(value)
        probs = probabilities(parts[0], parts[1], scale).astype(bf16)
        features[:, width + h * HD : width + (h + 1) * HD] = plain_dot(probs, parts[2]).astype(bf16)
    value = arrived[:, 3 * cols :].astype(f32) + own[:, 3 * cols :] + up_bias[...].astype(f32)
    pre[...] = value
    features[:, :width] = gelu_exact(value).astype(bf16)


def backward_body(scale, arrived, own, qkv, pre, cosine, low_sine, high_sine, grads):
    tables = (cosine[...], low_sine[...], high_sine[...])
    cols, width = qkv.shape[2], pre.shape[1]
    for h in range(cols // HD):
        at = slice(h * HD, (h + 1) * HD)
        query, key, value = qkv[0, :, at], qkv[1, :, at], qkv[2, :, at]
        place = slice(width + h * HD, width + (h + 1) * HD)
        out_grad = (own[:, place] + arrived[:, place].astype(f32)).astype(bf16)
        probs = probabilities(query, key, scale)
        value_grad = contract_rows(probs.astype(bf16), out_grad)
        prob_grad = contract_cols(out_grad, value)
        row_dot = jnp.sum(probs * prob_grad, axis=1, keepdims=True)
        score_grad = (probs * (prob_grad - row_dot)).astype(bf16)
        query_grad = turn(plain_dot(score_grad, key) * scale, tables, -1.0)
        key_grad = turn(contract_rows(score_grad, query) * scale, tables, -1.0)
        for i, grad in enumerate((query_grad, key_grad, value_grad)):
            low = grad.astype(bf16)
            grads[:, i * cols + h * HD : i * cols + (h + 1) * HD] = low
    total = arrived[:, :width].astype(f32) + own[:, :width]
    low = (total * gelu_slope(pre[...])).astype(bf16)
    grads[:, 3 * cols :] = low


def bias_rows_body(grads, rows):
    cols = rows.shape[1]
    total = jnp.sum(grads[...].astype(f32), axis=0, keepdims=True)
    rows[...] = jnp.zeros(rows.shape, f32)
    for t in range(total.shape[1] // cols):
        at = t if t < 3 else 8 + t - 3
        rows[at : at + 1] = total[:, t * cols : (t + 1) * cols]


def fold(value):
    total = value[:, :LANES]
    for k in range(1, value.shape[1] // LANES):
        total = total + value[:, k * LANES : (k + 1) * LANES]
    return total


def prior_body(grad_out, prior, result, held):
    def group(r, carry):
        rows = pl.ds(pl.multiple_of(r * ROWS, ROWS), ROWS)
        grads = [grad_out[s, rows, :].astype(f32) for s in range(4)]
        lanes = lane_ids((ROWS, LANES))
        packed = jnp.zeros((ROWS, LANES), f32)
        for j in range(STACK - 1):
            value = prior[j, rows, :].astype(f32)
            for s in range(4):
                column = jnp.sum(fold(grads[s] * value), axis=1, keepdims=True)
                packed = jnp.where(lanes == s * STACK + j, column, packed)
        held[rows, :] = packed
        return carry

    lax.fori_loop(0, held.shape[0] // ROWS, group, 0)
    result[...] = held[...].T[:64]


def prior_products(streams_grad, prior, after=()):
    length, cols = prior.shape[1:]
    block = min(length, LANES)

    def kernel(grad_ref, prior_ref, *refs):
        prior_body(grad_ref, prior_ref, *refs[len(after) :])

    return pl.pallas_call(
        kernel,
        grid=(length // block,),
        out_shape=out((64, length), f32),
        in_specs=[
            pl.BlockSpec((4, block, cols), lambda t: (0, t, 0)),
            pl.BlockSpec((STACK - 1, block, cols), lambda t: (0, t, 0)),
        ]
        + waits(after),
        out_specs=pl.BlockSpec((64, block), lambda t: (0, t)),
        scratch_shapes=[pltpu.VMEM((block, LANES), f32)],
        compiler_params=pltpu.CompilerParams(vmem_limit_bytes=VMEM_BYTES),
        cost_estimate=pl.CostEstimate(
            flops=20_000_000, bytes_accessed=2 * length * cols * 16, transcendentals=0
        ),
    )(streams_grad, prior, *after)


def mix_first_body(
    parts, streams, own, *refs
):
    arrived = refs[:parts]
    branch_bias, gain, mix_in, grad_out, layer_out, packed_out = refs[parts:]
    value = own[...]
    for item in arrived:
        value = value + item[...].astype(f32)
    value = streams[3].astype(f32) + (value + branch_bias[...].astype(f32))
    layer_out[...] = value
    packed = plain_dot(value * gain[...].astype(f32), mix_in[...], high)
    lanes = lane_ids(packed.shape)
    energy = jnp.sum(fold(value * value), axis=1, keepdims=True)
    packed = jnp.where(lanes == MIXH, energy, packed)
    for s in range(4):
        column = jnp.sum(fold(grad_out[s].astype(f32) * value), axis=1, keepdims=True)
        packed = jnp.where(lanes == MIXH + 1 + s, column, packed)
    packed_out[...] = packed.T[:64]


def mix_tables(packed, prior_coef, mix_in, mix_out, mix_static, gain, value, grad_out):
    lanes = lane_ids(packed.shape)
    energy = packed[:, MIXH : MIXH + 1]
    rms = lax.rsqrt(energy * (1.0 / D) + rms_eps)
    logit_sum = jnp.where(lanes < MIXH, packed, 0.0)
    logits = logit_sum * rms
    mix_hidden = gelu_exact(logits)
    coef = plain_dot(mix_hidden, mix_out, high) + mix_static
    coef_grad = prior_coef
    for s in range(4):
        column = packed[:, MIXH + 1 + s : MIXH + 2 + s]
        coef_grad = jnp.where(lanes == s * STACK + STACK - 1, column, coef_grad)
    logit_grad = contract_cols(coef_grad, mix_out, high) * gelu_slope(logits)
    sum_grad = logit_grad * rms
    rms_grad = jnp.sum(logit_grad * logit_sum, axis=1, keepdims=True)
    energy_grad = rms_grad * rms * rms * rms * (-1.0 / D)
    scaled_grad = contract_cols(sum_grad, mix_in, high)
    total = scaled_grad * gain + energy_grad * value
    for s in range(4):
        at = s * STACK + STACK - 1
        total = total + coef[:, at : at + 1] * grad_out[s].astype(f32)
    return coef, coef_grad, mix_hidden, sum_grad, scaled_grad, total


def mix_second_body(parts, me, *refs):
    held = refs[-1]
    for k in range(parts):
        held[lax.rem(me[0] + (parts - k), parts)] = refs[k][...]
    sums = held[0]
    for k in range(1, parts):
        sums = sums + held[k]
    (prior_coef, layer_out, grad_out, gain, mix_in, mix_out, mix_static,
     branch_grad, packed) = refs[parts:-1]
    packed[...] = sums
    total = mix_tables(
        to_columns(sums), to_columns(prior_coef[...]), mix_in[...], mix_out[...], mix_static[...],
        gain[...].astype(f32), layer_out[...], grad_out,
    )[-1]
    branch_grad[...] = total.astype(bf16)


def mix_third_body(packed, prior_coef, mix_in, mix_out, mix_static, layer_out, prior, grad_out, gain,
                   streams_out, prior_grad, weight_grads, token, layer_grad, reduced, held):
    block, cols = layer_out.shape
    step = pl.program_id(0)
    coef, coef_grad, mix_hidden, sum_grad, scaled_grad, total = mix_tables(
        to_columns(packed[...]), to_columns(prior_coef[...]), mix_in[...], mix_out[...],
        mix_static[...], gain[...].astype(f32), layer_out[...], grad_out,
    )
    held[...] = coef
    layer_grad[...] = total

    @pl.when(step == 0)
    def _():
        weight_grads[...] = jnp.zeros(weight_grads.shape, f32)
        reduced[...] = jnp.zeros(reduced.shape, f32)
        mark(token)

    reduced[0:1] += jnp.sum(scaled_grad * layer_out[...], axis=0, keepdims=True)
    reduced[1:2] += jnp.sum(total.astype(bf16).astype(f32), axis=0, keepdims=True)
    scaled = layer_out[...] * gain[...].astype(f32)
    weight_grads[:cols] += contract_rows(scaled, sum_grad, high)
    chosen = jnp.where(lane_ids((block, LANES)) == MIXH, 1.0, mix_hidden)
    weight_grads[cols:] += contract_rows(chosen, coef_grad, high)[: weight_grads.shape[0] - cols]

    def group(r, carry):
        rows = pl.ds(pl.multiple_of(r * ROWS, ROWS), ROWS)
        coef = held[rows, :]
        grads = [grad_out[s, rows, :].astype(f32) for s in range(4)]
        value = layer_out[rows, :]
        totals = []
        for s in range(4):
            at = s * STACK + STACK - 1
            totals.append(coef[:, at : at + 1] * value)
        for j in range(STACK - 1):
            value = prior[j, rows, :].astype(f32)
            back = None
            for s in range(4):
                at = s * STACK + j
                column = jnp.broadcast_to(coef[:, at : at + 1], (ROWS, cols))
                totals[s] = totals[s] + column * value
                term = column * grads[s]
                back = term if back is None else back + term
            prior_grad[j, rows, :] = back.astype(bf16)
        for s in range(4):
            streams_out[s, rows, :] = totals[s].astype(bf16)
        return carry

    lax.fori_loop(0, block // ROWS, group, 0)


def mix_third(packed, prior_coef, mix_in, mix_out, mix_static, layer_out, prior, streams_grad, gain, after):
    length, cols = layer_out.shape
    block = min(length, LANES)
    tokens = lambda count: pl.BlockSpec((count, block, cols), lambda t: (0, t, 0))
    whole = lambda *shape: pl.BlockSpec(shape, lambda t: (0,) * len(shape))

    def kernel(*refs):
        mix_third_body(*refs[:9], *refs[9 + len(after) :])

    return pl.pallas_call(
        kernel,
        grid=(length // block,),
        out_shape=[
            out((4, length, cols), bf16),
            out((STACK - 1, length, cols), bf16),
            out((cols + 56, LANES), f32),
            TOKEN,
            out((length, cols), f32),
            out((8, cols), f32),
        ],
        in_specs=[
            pl.BlockSpec((64, block), lambda t: (0, t)),
            pl.BlockSpec((64, block), lambda t: (0, t)),
            whole(cols, LANES),
            whole(LANES, LANES),
            whole(1, LANES),
            pl.BlockSpec((block, cols), lambda t: (t, 0)),
            tokens(STACK - 1),
            tokens(4),
            whole(1, cols),
        ]
        + waits(after),
        out_specs=[
            tokens(4),
            tokens(STACK - 1),
            whole(cols + 56, LANES),
            whole(8, LANES),
            pl.BlockSpec((block, cols), lambda t: (t, 0)),
            whole(8, cols),
        ],
        scratch_shapes=[pltpu.VMEM((block, LANES), f32)],
        compiler_params=PARAMS,
        cost_estimate=pl.CostEstimate(
            flops=30_000_000, bytes_accessed=2 * length * cols * 34, transcendentals=0
        ),
    )(packed, prior_coef, mix_in, mix_out, mix_static, layer_out, prior, streams_grad, gain, *after)


def cost(flops, moved):
    return pl.CostEstimate(flops=flops, bytes_accessed=moved, transcendentals=0)


ANY = pl.BlockSpec(memory_space=pl.ANY)
PARAMS = pltpu.CompilerParams(vmem_limit_bytes=48 * 1024 * 1024)
WIDE_PARAMS = pltpu.CompilerParams(vmem_limit_bytes=60 * 1024 * 1024)


def prefetched(kernel, scalars, grid, in_specs, out_specs, out_shape, args, estimate, aliases=None):
    return pl.pallas_call(
        kernel,
        grid_spec=pltpu.PrefetchScalarGridSpec(
            num_scalar_prefetch=len(scalars), grid=grid, in_specs=in_specs, out_specs=out_specs
        ),
        out_shape=out_shape,
        input_output_aliases=aliases or {},
        compiler_params=PARAMS,
        cost_estimate=estimate,
    )(*scalars, *args)


def fetch(pairs, sems):
    copies = [pltpu.make_async_copy(src, dst, sems.at[k]) for k, (src, dst) in enumerate(pairs)]
    for item in copies:
        item.start()
    return copies


def spread(block, near, w_qkv, w_up, up_cols, dtype, after):
    _, length, depth = near.shape
    cols = depth // 2
    width = 3 * cols + up_cols

    def kernel(b, near_ref, qkv_ref, up_ref, *refs):
        result, left, qkv, up, sems = refs[len(after) :]
        pairs = []
        for s in range(4):
            pairs.append((near_ref.at[s], left.at[s]))
            if s < 3:
                place = pl.multiple_of(b[0] * cols, LANES)
                pairs.append((qkv_ref.at[s, :, pl.ds(place, cols)], qkv.at[s]))
            else:
                place = pl.multiple_of(b[0] * up_cols, LANES)
                pairs.append((up_ref.at[:, pl.ds(place, up_cols)], up))
        copies = fetch(pairs, sems)
        for s in range(4):
            copies[2 * s].wait()
            copies[2 * s + 1].wait()
            if s < 3:
                result[:, s * cols : (s + 1) * cols] = plain_dot(left[s], qkv[s]).astype(dtype)
            else:
                result[:, 3 * cols :] = plain_dot(left[s], up[...]).astype(dtype)

    vmem = pl.BlockSpec(memory_space=pltpu.VMEM)
    return pl.pallas_call(
        kernel,
        out_shape=out((length, width), dtype),
        in_specs=[pl.BlockSpec(memory_space=pltpu.SMEM)] + [ANY] * 3 + waits(after),
        out_specs=vmem,
        scratch_shapes=[
            pltpu.VMEM((4, length, depth), bf16),
            pltpu.VMEM((3, depth, cols), bf16),
            pltpu.VMEM((depth, up_cols), bf16),
            pltpu.SemaphoreType.DMA((8,)),
        ],
        compiler_params=PARAMS if after else WIDE_PARAMS,
        cost_estimate=cost(2 * length * depth * width, 2 * depth * width + 4 * length * width),
    )(block, near, w_qkv, w_up, *after)


def spread_back(idx, block, own, other, w_down, w_out, up_cols, dtype, after):
    length, cols = own.shape

    def kernel(b, idx_ref, own_ref, other_ref, down_ref, out_ref, *refs):
        result, pair, down, outer, sems = refs[len(after) :]
        copies = fetch(
            [
                (down_ref.at[pl.ds(pl.multiple_of(b[0] * up_cols, up_cols), up_cols)], down),
                (out_ref.at[pl.ds(pl.multiple_of(b[0] * cols, cols), cols)], outer),
            ],
            sems,
        )
        pair[:, pl.ds(pl.multiple_of(idx_ref[0] * cols, LANES), cols)] = own_ref[...]
        pair[:, pl.ds(pl.multiple_of((1 - idx_ref[0]) * cols, LANES), cols)] = other_ref[...]
        copies[0].wait()
        result[:, :up_cols] = contract_cols(pair[...], down[...]).astype(dtype)
        copies[1].wait()
        result[:, up_cols:] = contract_cols(pair[...], outer[...]).astype(dtype)

    depth = up_cols + cols
    smem = pl.BlockSpec(memory_space=pltpu.SMEM)
    vmem = pl.BlockSpec(memory_space=pltpu.VMEM)
    return pl.pallas_call(
        kernel,
        out_shape=out((length, depth), dtype),
        in_specs=[smem, smem, vmem, vmem, ANY, ANY] + waits(after),
        out_specs=vmem,
        scratch_shapes=[
            pltpu.VMEM((length, 2 * cols), bf16),
            pltpu.VMEM((up_cols, 2 * cols), bf16),
            pltpu.VMEM((cols, 2 * cols), bf16),
            pltpu.SemaphoreType.DMA((2,)),
        ],
        compiler_params=PARAMS,
        cost_estimate=cost(4 * length * depth * cols, 4 * depth * cols + 4 * length * depth),
    )(block, idx, own, other, w_down, w_out, *after)


def take_body(up_cols, block, down_ref, out_ref, result, token, sems):
    mark(token)
    cols = result.shape[0] - up_cols
    copies = fetch(
        [
            (
                down_ref.at[pl.ds(pl.multiple_of(block[0] * up_cols, up_cols), up_cols)],
                result.at[pl.ds(0, up_cols)],
            ),
            (
                out_ref.at[pl.ds(pl.multiple_of(block[0] * cols, cols), cols)],
                result.at[pl.ds(up_cols, cols)],
            ),
        ],
        sems,
    )
    for item in copies:
        item.wait()


def take(block, w_down, w_out, up_cols, after):
    depth = up_cols + w_down.shape[1] // 2
    vmem = pl.BlockSpec(memory_space=pltpu.VMEM)

    def kernel(b, down_ref, out_ref, *refs):
        take_body(up_cols, b, down_ref, out_ref, *refs[len(after) :])

    return pl.pallas_call(
        kernel,
        out_shape=[out((depth, w_down.shape[1]), bf16), TOKEN],
        in_specs=[pl.BlockSpec(memory_space=pltpu.SMEM), ANY, ANY] + waits(after),
        out_specs=[vmem, vmem],
        scratch_shapes=[pltpu.SemaphoreType.DMA((2,))],
        compiler_params=PARAMS,
        cost_estimate=cost(0, 8 * depth * w_down.shape[1]),
    )(block, w_down, w_out, *after)


def first_back_body(idx, own, other, weights, result, pair):
    cols = own.shape[1]
    pair[:, pl.ds(pl.multiple_of(idx[0] * cols, LANES), cols)] = own[...]
    pair[:, pl.ds(pl.multiple_of((1 - idx[0]) * cols, LANES), cols)] = other[...]
    result[...] = contract_cols(pair[...], weights[...]).astype(bf16)


def add_body(arrived, term, result):
    result[...] = (arrived[...].astype(f32) + term[...]).astype(bf16)


def branch_step(block, item, so_far, w_down, w_out, up_cols, after):
    length, depth = item.shape
    cols = depth - up_cols
    wide_cols = w_down.shape[1]
    earlier = [] if so_far is None else [so_far]
    whole = pl.BlockSpec((length, wide_cols), lambda i, b: (0, 0))

    def kernel(b, item_ref, down_ref, out_ref, *refs):
        value = plain_dot(item_ref[:, :up_cols], down_ref[...]) + plain_dot(
            item_ref[:, up_cols:], out_ref[...]
        )
        refs[-2][...] = refs[0][...] + value if earlier else value
        mark(refs[-1])

    return prefetched(
        kernel,
        [block],
        (1,),
        [
            pl.BlockSpec((length, depth), lambda i, b: (0, 0)),
            pl.BlockSpec((up_cols, wide_cols), lambda i, b: (b[0], 0)),
            pl.BlockSpec((cols, wide_cols), lambda i, b: (b[0], 0)),
        ]
        + [whole] * len(earlier)
        + waits(after),
        [whole, pl.BlockSpec((8, LANES), lambda i, b: (0, 0))],
        [out((length, wide_cols), f32), TOKEN],
        [item, w_down, w_out, *earlier, *after],
        cost(2 * length * depth * wide_cols, 2 * depth * wide_cols),
    )


def halves_body(idx, value, theirs, mine):
    cols = mine.shape[1]
    mine[...] = value[:, pl.ds(pl.multiple_of(idx[0] * cols, LANES), cols)]
    theirs[...] = value[:, pl.ds(pl.multiple_of((1 - idx[0]) * cols, LANES), cols)].astype(bf16)


def near_step(block, item, so_far, w_qkv, w_up, cols, after):
    length = item.shape[0]
    depth = w_up.shape[0]
    up_cols = item.shape[1] - 3 * cols
    earlier = [] if so_far is None else [so_far]
    one = pl.BlockSpec((1, length, depth), lambda s, b: (s, 0, 0))

    def kernel(b, item_ref, qkv_ref, up_ref, *refs):
        step = pl.program_id(0)
        base = refs[0][0] if earlier else 0.0

        @pl.when(step < 3)
        def _():
            part = item_ref[:, pl.ds(pl.multiple_of(step * cols, LANES), cols)]
            refs[-2][0] = contract_cols(part, qkv_ref[0]) + base

        @pl.when(step == 3)
        def _():
            refs[-2][0] = contract_cols(item_ref[:, 3 * cols :], up_ref[...]) + base
            mark(refs[-1])

    return prefetched(
        kernel,
        [block],
        (4,),
        [
            pl.BlockSpec(item.shape, lambda s, b: (0, 0)),
            pl.BlockSpec((1, depth, cols), lambda s, b: (jnp.minimum(s, 2), 0, b[0])),
            pl.BlockSpec((depth, up_cols), lambda s, b: (0, b[0])),
        ]
        + [one] * len(earlier)
        + waits(after),
        [one, pl.BlockSpec((8, LANES), lambda s, b: (0, 0))],
        [out((4, length, depth), f32), TOKEN],
        [item, w_qkv, w_up, *earlier, *after],
        cost(2 * item.size * depth, 2 * item.size * depth // length + 32 * length * depth),
    )


def near_last(idx, block, item, so_far, w_qkv, w_up, own, other, stat, gain_own, gain_other):
    length = item.shape[0]
    depth = w_up.shape[0]
    cols = depth // 2
    up_cols = item.shape[1] - 3 * cols

    def kernel(b, x, item_ref, qkv_ref, up_ref, base, own_ref, other_ref, stat_ref, gain_o, gain_f,
               theirs, mine, stats, value, packed):
        step = pl.program_id(0)

        @pl.when(step < 3)
        def _():
            part = item_ref[:, pl.ds(pl.multiple_of(step * cols, LANES), cols)]
            value[...] = contract_cols(part, qkv_ref[0]) + base[0]

        @pl.when(step == 3)
        def _():
            value[...] = contract_cols(item_ref[:, 3 * cols :], up_ref[...]) + base[0]

        table = stat_ref[...]
        lanes = lane_ids(table.shape)
        mean = jnp.sum(jnp.where(lanes == step, table, 0.0), axis=1, keepdims=True)
        inv_std = jnp.sum(jnp.where(lanes == step + 4, table, 0.0), axis=1, keepdims=True)
        total = jnp.zeros((length, LANES), f32)
        cross = jnp.zeros((length, LANES), f32)
        for which, (src, gain) in enumerate(((own_ref, gain_o), (other_ref, gain_f))):
            place = pl.multiple_of((x[0] if which == 0 else 1 - x[0]) * cols, LANES)
            part = value[:, pl.ds(place, cols)]
            if which == 0:
                mine[0] = part
            else:
                theirs[0] = part.astype(bf16)
            scaled = part * gain[0].astype(f32)
            total = total + fold(scaled)
            cross = cross + fold(scaled * ((src[0].astype(f32) - mean) * inv_std))
        kept = jnp.where(step == 0, 0.0, packed[...])
        kept = jnp.where(lanes == step, jnp.sum(total, axis=1, keepdims=True), kept)
        kept = jnp.where(lanes == step + 4, jnp.sum(cross, axis=1, keepdims=True), kept)
        packed[...] = kept

        @pl.when(step == 3)
        def _():
            stats[...] = packed[...].T[:8]

    half = pl.BlockSpec((1, length, cols), lambda s, b, x: (s, 0, 0))
    row = pl.BlockSpec((1, 1, cols), lambda s, b, x: (s, 0, 0))
    return pl.pallas_call(
        kernel,
        grid_spec=pltpu.PrefetchScalarGridSpec(
            num_scalar_prefetch=2,
            grid=(4,),
            in_specs=[
                pl.BlockSpec(item.shape, lambda s, b, x: (0, 0)),
                pl.BlockSpec((1, depth, cols), lambda s, b, x: (jnp.minimum(s, 2), 0, b[0])),
                pl.BlockSpec((depth, up_cols), lambda s, b, x: (0, b[0])),
                pl.BlockSpec((1, length, depth), lambda s, b, x: (s, 0, 0)),
                half,
                half,
                pl.BlockSpec((length, LANES), lambda s, b, x: (0, 0)),
                row,
                row,
            ],
            out_specs=[half, half, pl.BlockSpec((8, length), lambda s, b, x: (0, 0))],
            scratch_shapes=[pltpu.VMEM((length, depth), f32), pltpu.VMEM((length, LANES), f32)],
        ),
        out_shape=[
            out((4, length, cols), bf16), out((4, length, cols), f32), out((8, length), f32),
        ],
        compiler_params=PARAMS,
        cost_estimate=cost(2 * item.size * depth, 2 * item.size * depth // length + 24 * length * depth),
    )(block, idx, item, w_qkv, w_up, so_far, own, other, stat, gain_own[:, None], gain_other[:, None])


def near_weights(order, block, near, parts, shapes, before, after=()):
    n_dp, _, length, depth = near.shape
    cols = depth // 2
    up_cols = parts[0].shape[1] - 3 * cols

    def kernel(order_ref, b, near_ref, *refs):
        qkv_grad, up_grad, done = refs[-3:]
        step = pl.program_id(0)
        left = jnp.concatenate([near_ref[order_ref[p], 0] for p in range(n_dp)], axis=0)

        @pl.when(step < 3)
        def _():
            place = pl.multiple_of(step * cols, LANES)
            right = jnp.concatenate([item[:, pl.ds(place, cols)] for item in refs[:n_dp]], axis=0)
            qkv_grad[0] = contract_rows(left, right)

        @pl.when(step == 3)
        def _():
            right = jnp.concatenate([item[:, 3 * cols :] for item in refs[:n_dp]], axis=0)
            up_grad[...] = contract_rows(left, right)
            done[...] = jnp.zeros(done.shape, f32)

    return prefetched(
        kernel,
        [order, block],
        (4,),
        [pl.BlockSpec((n_dp, 1, length, depth), lambda i, o, b: (0, i, 0, 0))]
        + [pl.BlockSpec(parts[0].shape, lambda i, o, b: (0, 0))] * n_dp
        + [ANY] * len(before)
        + waits(after),
        [
            pl.BlockSpec((1, depth, cols), lambda i, o, b: (jnp.minimum(i, 2), 0, b[0])),
            pl.BlockSpec((depth, up_cols), lambda i, o, b: (0, b[0])),
            pl.BlockSpec((8, LANES), lambda i, o, b: (0, 0)),
        ],
        [out(shape, f32) for shape in (*shapes, (8, LANES))],
        [near, *parts, *before, *after],
        cost(1000, 1000),
        {3 + n_dp + k: k for k in range(len(before))},
    )


def branch_weights(order, block, features, parts, up_cols, shapes, before):
    n_dp, length, depth = features.shape
    cols = depth - up_cols
    width = parts[0].shape[1]

    def kernel(order_ref, b, features_ref, *refs):
        left = jnp.concatenate([features_ref[order_ref[p]] for p in range(n_dp)], axis=0)
        right = jnp.concatenate([item[...] for item in refs[:n_dp]], axis=0)
        refs[-3][...] = contract_rows(left[:, :up_cols], right)
        refs[-2][...] = contract_rows(left[:, up_cols:], right)
        refs[-1][...] = jnp.zeros(refs[-1].shape, f32)

    return prefetched(
        kernel,
        [order, block],
        (1,),
        [pl.BlockSpec(features.shape, lambda i, o, b: (0, 0, 0))]
        + [pl.BlockSpec((length, width), lambda i, o, b: (0, 0))] * n_dp
        + [ANY] * len(before),
        [
            pl.BlockSpec((up_cols, width), lambda i, o, b: (b[0], 0)),
            pl.BlockSpec((cols, width), lambda i, o, b: (b[0], 0)),
            pl.BlockSpec((8, LANES), lambda i, o, b: (0, 0)),
        ],
        [out(shape, f32) for shape in (*shapes, (8, LANES))],
        [features, *parts, *before],
        cost(2 * features.size * width, 2 * features.size + 4 * depth * width),
        {3 + n_dp + k: k for k in range(len(before))},
    )


def gate(value, after):
    def kernel(*refs):
        pass

    return pl.pallas_call(
        kernel,
        out_shape=out(value.shape, value.dtype),
        in_specs=[ANY] + waits(after),
        out_specs=ANY,
        input_output_aliases={0: 0},
        compiler_params=pltpu.CompilerParams(
            has_side_effects=True, vmem_limit_bytes=VMEM_BYTES
        ),
    )(value, *after)


TOKEN = out((8, LANES), f32)


def mark(ref):
    ref[...] = jnp.zeros(ref.shape, f32)


def finish_body(rows, far, qkv_bias, up_bias, branch_bias, mix_gain, gain, shift_grad):
    total = rows[...] + far[...]
    qkv_bias[...] = total[0:3]
    mix_gain[...] = total[16:17]
    branch_bias[...] = total[17:18]
    up_bias[...] = total[8 : 8 + up_bias.shape[0]]
    gain[...] = total[24:28]
    shift_grad[...] = total[28:32]


def add_rows_body(*refs):
    total = refs[0][...]
    for item in refs[1:-1]:
        total = total + item[...]
    refs[-1][...] = total


def stats_body(streams, sums):
    length = streams.shape[1]
    lanes = lane_ids((length, LANES))
    packed = jnp.zeros((length, LANES), f32)
    for s in range(4):
        value = streams[s].astype(f32)
        packed = jnp.where(lanes == s, jnp.sum(fold(value), axis=1, keepdims=True), packed)
        packed = jnp.where(
            lanes == 4 + s, jnp.sum(fold(value * value), axis=1, keepdims=True), packed
        )
    sums[...] = packed.T[:8]


def build(n_dp, n_wide, n_narrow):
    def shift(value, axis, size, step):
        return lax.ppermute(value, axis, [(i, (i + step) % size) for i in range(size)])

    def swap(value, axis, size, bit):
        return lax.ppermute(value, axis, [(i, i ^ bit) for i in range(size)])

    def butterfly(value, axis, size):
        bit = 1
        while bit < size:
            value = value + swap(value, axis, size, bit)
            bit *= 2
        return value

    def narrow_swap(value):
        return swap(value, "narrow", n_narrow, 1)

    def model_parts(value):
        value = value + narrow_swap(value)
        return [value] + [shift(value, "wide", n_wide, k) for k in range(1, n_wide)]

    def model_butterfly(value):
        return butterfly(butterfly(value, "narrow", n_narrow), "wide", n_wide)

    def dp_sum(value):
        return butterfly(value, "dp", n_dp)

    def dp_gather(value):
        held = [value]
        far = value
        for _ in range(n_dp // CORES - 1):
            far = shift(far, "dp", n_dp, CORES)
            held.append(far)
        return held + [swap(item, "dp", n_dp, 1) for item in held]

    def across(value):
        held = [value]
        for _ in range(n_dp // CORES - 1):
            held.append(shift(held[-1], "dp", n_dp, CORES))
        return held

    def dp_order():
        me = lax.axis_index("dp")
        steps = [lax.rem(me + n_dp - CORES * k, n_dp) for k in range(n_dp // CORES)]
        return steps + [item ^ 1 for item in steps]

    def reduce_ring(product, hold):
        me = lax.axis_index("wide").astype(jnp.int32)
        block = lambda back: lax.rem(me + (n_wide - back), n_wide)[None]
        total = product(block(1), bf16, [])
        sent = [total]
        for at in range(n_wide - 1):
            arrived = shift(total, "wide", n_wide, 1)
            term = product(block(at + 2) if at + 2 < n_wide else me[None], f32, [total])
            if at < n_wide - 2:
                (total,) = call(
                    add_body, [out(total.shape, bf16)], [arrived, term], after=hold(at, total)
                )
                sent.append(total)
        return arrived, term, sent

    def per_device(
        streams, prior, streams_grad, w_qkv, qkv_bias, w_out, w_up, up_bias, w_down, branch_bias,
        norm_gain, norm_bias, mix_gain, mix_in, mix_out, mix_static,
    ):
        length = streams.shape[1]
        cols = streams.shape[2]
        scale = 1.0 / math.sqrt(HD)
        up_cols = w_up.shape[1] // n_wide
        tiles = up_cols // cols
        depth = up_cols + cols
        idx = lax.axis_index("narrow").astype(jnp.int32)[None]
        me = lax.axis_index("wide").astype(jnp.int32)
        order = jnp.stack(dp_order()).astype(jnp.int32)
        params = jnp.concatenate([norm_gain, norm_bias], axis=0)
        other_params = narrow_swap(params)
        gain_other = other_params[:4]
        other = narrow_swap(streams)
        (sums,) = call(stats_body, [out((8, length), f32)], [streams])
        (wide_sums,) = call(
            add_rows_body,
            [out((8, length), f32)],
            [sums] + [shift(sums, "wide", n_wide, k) for k in range(1, n_wide)],
            after=[other, other_params],
        )
        stat_parts = [wide_sums, narrow_swap(wide_sums)]
        (near,) = call(
            functools.partial(near_body, len(stat_parts)),
            [out((4, length, 2 * cols), bf16)],
            [*stat_parts, idx, streams, other, params, other_params],
            scalars={len(stat_parts)},
        )
        tables = rotary_tables(length)

        near_all = lax.all_gather(near, "dp", axis=0, tiled=False)
        near_token = near_all[0, 0, :8, :LANES]
        tables = rotary_tables(length)
        prior_rows = prior_products(streams_grad, prior)
        prior_sum = lax.psum(prior_rows, ("wide", "narrow"))
        arrived, own, sent = reduce_ring(
            lambda block, dtype, after: spread(
                block, near, w_qkv, w_up, up_cols, dtype, after
            ),
            lambda at, total: [],
        )
        qkv, up_pre, features = call(
            functools.partial(forward_body, scale),
            [
                out((3, length, cols), bf16),
                out((length, up_cols), f32),
                out((length, up_cols + cols), bf16),
            ],
            [arrived, own, qkv_bias, up_bias[None], *tables],
            flops=8 * length * length * cols,
        )
        (stat,) = call(table_body, [out((length, LANES), f32)], stat_parts, after=[features])
        blocks = [lax.rem(me + (n_wide - k), n_wide)[None] for k in range(n_wide)]
        item, branch_part, features_all = features, None, []
        for k in range(n_wide):
            branch_part, token = branch_step(
                blocks[k], item, branch_part, w_down, w_out, up_cols, []
            )
            features_all.append(lax.all_gather(item, "dp", axis=0, tiled=False))
            if k < n_wide - 1:
                item = gate(shift(item, "wide", n_wide, 1), [token])
        theirs, branch_own = call(
            halves_body,
            [out((length, cols), bf16), out((length, cols), f32)],
            [idx, branch_part],
            scalars={0},
        )
        branch_arrived = narrow_swap(theirs)
        mix_in_pad = jnp.pad(mix_in.astype(f32), ((0, 0), (0, LANES - MIXH)))
        mix_out_pad = jnp.pad(mix_out.astype(f32), ((0, LANES - MIXH), (0, LANES - MIXH)))
        static_pad = jnp.pad(mix_static.astype(f32)[None], ((0, 0), (0, LANES - MIXH)))
        gain_row = mix_gain[None]
        layer_out, packed = call(
            functools.partial(mix_first_body, 1),
            [out((length, cols), f32), out((64, length), f32)],
            [streams, branch_own, branch_arrived, branch_bias[None], gain_row, mix_in_pad, streams_grad],
            after=[near_token],
        )
        packed_parts = model_parts(packed)
        first_rows, rows_token = take(
            blocks[1 % n_wide], w_down, w_out, up_cols, [packed[:8, :LANES]]
        )
        branch_grad, packed_sum = call(
            functools.partial(mix_second_body, n_wide),
            [
                out((length, cols), bf16),
                out((64, length), f32),
            ],
            [me[None], *packed_parts, prior_sum, layer_out, streams_grad, gain_row, mix_in_pad,
             mix_out_pad, static_pad],
            scalars={0},
            scratch=[pltpu.VMEM((n_wide, 64, length), f32)],
            after=[rows_token],
        )
        branch_other = narrow_swap(branch_grad)
        mixer_outs, mixer_sums, branch_grads, tokens = [], [], [], []

        def branch_side(at, total):
            if at == 0:
                mixer_outs.extend(
                    mix_third(
                        packed_sum, prior_sum, mix_in_pad, mix_out_pad, static_pad, layer_out, prior,
                        streams_grad, gain_row, [total],
                    )
                )
                first = lax.axis_index("narrow") == 0
                pair = [gate(branch_grad, [total]), branch_other]
                near = jnp.concatenate(
                    [jnp.where(first, pair[0], pair[1]), jnp.where(first, pair[1], pair[0])], axis=1
                )
                branch_all = dp_gather(near)
                for k, block in enumerate(blocks):
                    *grads, token = branch_weights(
                        order, block, features_all[k], branch_all, up_cols,
                        (w_down.shape, w_out.shape), branch_grads[-1] if branch_grads else [],
                    )
                    branch_grads.append(grads)
                    tokens.append(token)
                mixer_sums.append(dp_sum(mixer_outs[2]))
                return [mixer_outs[3]]
            return tokens[:1]

        arrived, own, sent = reduce_ring(
            lambda block, dtype, after: (
                spread_back(
                    idx, block, branch_grad, branch_other, w_down, w_out, up_cols, dtype, after
                )
                if after
                else call(
                    first_back_body,
                    [out((length, up_cols + cols), bf16)],
                    [idx, branch_grad, branch_other, first_rows],
                    scalars={0},
                    scratch=[pltpu.VMEM((length, 2 * cols), bf16)],
                )[0]
            ),
            lambda at, total: branch_side(at, total),
        )
        (grads,) = call(
            functools.partial(backward_body, scale),
            [out((length, up_cols + 3 * cols), bf16)],
            [arrived, own, qkv, up_pre, *tables],
            flops=14 * length * length * cols,
            after=tokens[:1] + [mixer_sums[0][:8]],
        )
        (bias_rows,) = call(bias_rows_body, [out((16, cols), f32)], [grads])
        (mix_sums,) = mixer_sums
        item, near_grad, near_grads, held, mates = grads, None, [], [], []
        for k in range(n_wide):
            after = []
            if k < n_wide - 1:
                near_grad, token = near_step(blocks[k], item, near_grad, w_qkv, w_up, cols, [])
                after = [token, *([*tokens[1:], bias_rows] if k == 0 else [])]
            else:
                theirs, mine, stats = near_last(
                    idx, blocks[k], item, near_grad, w_qkv, w_up, streams, other, stat, norm_gain,
                    gain_other,
                )
            held.append(across(item))
            if k:
                far = [gate(part, [item]) for part in held[k - 1][1:]]
                crossed = [held[k - 1][0], *far, mates[k - 1]]
                crossed = crossed + [swap(part, "dp", n_dp, 1) for part in far]
                *near_grads, token = near_weights(
                    order, blocks[k - 1], near_all, crossed, (w_qkv.shape, w_up.shape), near_grads
                )
                after.append(token)
            if k < n_wide - 1:
                mates.append(swap(item, "dp", n_dp, 1))
                after += [held[k][-1], mates[k]]
            else:
                (wide_sum,) = call(
                    add_rows_body,
                    [out((8, length), f32)],
                    [stats] + [shift(stats, "wide", n_wide, j) for j in range(1, n_wide)],
                    after=[token],
                )
                mates.append(swap(gate(item, [wide_sum]), "dp", n_dp, 1))
            if k < n_wide - 1:
                item = gate(shift(item, "wide", n_wide, 1), after)
        down_weight_grad, out_weight_grad = branch_grads[-1]
        streams_out, prior_grad, _, _, layer_grad, mix_rows = mixer_outs
        stat_parts = [wide_sum, narrow_swap(wide_sum)]
        streams_in_grad, near_rows = call(
            functools.partial(norm_back_body, len(stat_parts)),
            [out((4, length, cols), bf16), out((8, cols), f32)],
            [mine, narrow_swap(theirs), streams, stat, norm_gain, *stat_parts, layer_grad],
        )
        far = [gate(part, [near_rows]) for part in held[-1][1:]]
        crossed = [held[-1][0], *far, mates[-1]] + [swap(part, "dp", n_dp, 1) for part in far]
        *near_grads, last_token = near_weights(
            order, blocks[-1], near_all, crossed, (w_qkv.shape, w_up.shape), near_grads
        )
        qkv_weight_grad, up_weight_grad = near_grads
        rows = jnp.concatenate([bias_rows, mix_rows, near_rows], axis=0)
        bit = 1
        while 2 * bit < n_dp:
            rows = rows + swap(rows, "dp", n_dp, bit)
            bit *= 2
        qkv_bias_grad, up_bias_grad, branch_bias_grad, mix_gain_grad, gain_grad, shift_grad = call(
            finish_body,
            [out((3, cols), f32), out((tiles, cols), f32), out((1, cols), f32), out((1, cols), f32),
             out((4, cols), f32), out((4, cols), f32)],
            [rows, swap(rows, "dp", n_dp, bit)],
            after=[last_token],
        )
        return (
            streams_out, streams_in_grad, prior_grad, qkv_weight_grad, qkv_bias_grad, out_weight_grad,
            up_weight_grad, up_bias_grad.reshape(-1), down_weight_grad, branch_bias_grad[0], gain_grad,
            shift_grad, mix_gain_grad[0], mix_sums[:cols, :MIXH],
            mix_sums[cols : cols + MIXH, :MIXH], mix_sums[cols + MIXH, :MIXH],
        )

    return per_device


def solution(mesh):
    tokens = P(None, "dp", ("wide", "narrow"))
    outer = P(("wide", "narrow"))
    inner = P(None, ("wide", "narrow"))
    column = P(("narrow", "wide"))
    return jax.shard_map(
        build(mesh.shape["dp"], mesh.shape["wide"], mesh.shape["narrow"]),
        mesh=mesh,
        in_specs=(
            tokens, tokens, tokens, P(None, "wide", "narrow"), P(None, ("narrow", "wide")),
            P("narrow", "wide"), P("wide", "narrow"), column, P("narrow", "wide"), outer, inner,
            inner, outer, P(("wide", "narrow"), None), P(), P(),
        ),
        out_specs=(
            tokens, tokens, tokens, P(None, "wide", "narrow"), P(None, ("narrow", "wide")),
            P("narrow", "wide"), P("wide", "narrow"), column, P("narrow", "wide"), outer, inner,
            inner, outer, P(("wide", "narrow"), None), P(), P(),
        ),
        check_vma=False,
    )
```
